32 devices in a mesh: dev: 32 (over z, y, x, core).
Axes of the slice: x: 2, y: 2, z: 4, core: 2. Of those that a mesh axis runs over, the one named last changes fastest.
Arguments:
- cells_in: bfloat16 [12288, 1024], P('dev'), may hold values from -6 to 6
- lengths: int32 [64], replicated, may hold values from 1 to 383, as said below
- sets_weights: float32 [12582912], P('dev')
- rows_weights: float32 [49152], P('dev')
- norm_gains: float32 [2176], P('dev'), may hold values from 0.5 to 1.5
- sets_first: float32 [12582912], P('dev')
- rows_first: float32 [49152], P('dev')
- gains_first: float32 [2176], P('dev')
- sets_second: float32 [12582912], P('dev')
- rows_second: float32 [49152], P('dev')
- gains_second: float32 [2176], P('dev')
- out_grad: bfloat16 [11520, 1024], P('dev'), may hold values from -6 to 6
Outputs:
- rows_out: bfloat16 [11520, 1024], P('dev')
- cells_grad: float32 [12288, 1024], P('dev')
- sets_grad: float32 [12582912], P('dev')
- rows_grad: float32 [49152], P('dev')
- gains_grad: float32 [2176], P('dev')
- sets_new: float32 [12582912], P('dev')
- rows_new: float32 [49152], P('dev')
- gains_new: float32 [2176], P('dev')
- sets_first_new: float32 [12582912], P('dev')
- rows_first_new: float32 [49152], P('dev')
- gains_first_new: float32 [2176], P('dev')
- sets_second_new: float32 [12582912], P('dev')
- rows_second_new: float32 [49152], P('dev')
- gains_second_new: float32 [2176], P('dev')
- sets_low: bfloat16 [12582912], P('dev')
- rows_low: bfloat16 [49152], P('dev')
- gains_low: bfloat16 [2176], P('dev')
The draws below stay inside these ranges and needn't reach their ends.
Inputs may be any that keep to these rules, and one draw needn't show every extreme that they name: Each device's 2 lengths sum to a multiple of 32 that is at most 384, and some device's to exactly 384; all lengths together sum to 11520.
All inputs are finite; a program needn't handle non-finite values.
Results may differ from the reference program's by a relative error of at most 0.024.
Values may be sent and summed in bfloat16 or wider, within the bound.
No kernel may reach another device: no remote copies, remote signals or barrier semaphores. Data moves between devices by JAX's collectives and lax.ppermute only.
A program may use at most 320 MiB of HBM per device.

```python
import math
import jax
import jax.numpy as jnp
from jax import lax

E = 64
ATTRS = 16
HEADS = 8
SETS_DEV = 2
STEP = 5
CAP = 384
DEVS = 32
D = 1024
ROWS = 12288
ROWS_EVEN = 360
REAL_ROWS = 11520
P_ABD = 12582912
P_ABA = 49152
P_GAIN = 2176


def block_sizes(feature):
    return [3 * feature * feature, feature * feature, 4 * feature * feature, 4 * feature * feature]


def scaled_normal(key, scales, sizes):
    pieces = []
    for number in range(len(sizes)):
        noise = jax.random.normal(jax.random.fold_in(key, number), (sizes[number],), jnp.float32)
        pieces.append(noise * scales[number])
    return jnp.concatenate(pieces)


def scaled_square(key, scales, sizes):
    pieces = []
    for number in range(len(sizes)):
        factor = jnp.exp(jax.random.uniform(jax.random.fold_in(key, number), (sizes[number],), jnp.float32, 0.0, math.log(4.0)))
        pieces.append(factor * scales[number] * scales[number])
    return jnp.concatenate(pieces)


def set_scales():
    root_rows = (ROWS_EVEN * DEVS) ** 0.5
    return [root_rows, 2.0 * root_rows * CAP ** (-0.5), 0.3 * root_rows, 0.5 * root_rows]


def row_scales():
    root_cells = (ROWS_EVEN * DEVS * ATTRS) ** 0.5
    return [root_cells, 0.4 * root_cells, 0.3 * root_cells, 0.5 * root_cells]


def gain_scales():
    return [(ROWS_EVEN * DEVS) ** 0.5, (ROWS_EVEN * DEVS * ATTRS) ** 0.5]


def draw_lengths(key, part):
    key = jax.random.fold_in(key, 11)
    spare = CAP // DEVS - 1
    full = jax.random.randint(jax.random.fold_in(key, 1), (), 0, DEVS)
    units = jnp.arange(DEVS * spare, dtype=jnp.int32)
    owner = units // spare
    ranks = jax.random.permutation(jax.random.fold_in(key, 2), DEVS * spare).astype(jnp.int32)
    ranks = jnp.where(owner == full, -1, ranks)
    order = jnp.argsort(ranks, stable=True)
    chosen = jnp.zeros((DEVS * spare,), jnp.int32).at[order[:ROWS_EVEN - DEVS]].set(1)
    counts = 1 + jnp.sum(chosen.reshape(DEVS, spare), axis=1).astype(jnp.int32)
    totals = counts * DEVS
    leading = jax.random.randint(jax.random.fold_in(key, 3), (DEVS,), 1, totals).astype(jnp.int32)
    leading = jnp.where(jnp.arange(DEVS, dtype=jnp.int32) == full, totals * 8 // 9, leading)
    return jnp.stack([leading, totals - leading], axis=1).reshape(-1).astype(jnp.int32)


def draw_sets_weights(key, part):
    key = jax.random.fold_in(key, 31)
    fans = [D, max(1, 3 * D // CAP), D, 4 * D]
    return scaled_normal(key, [fan ** (-0.5) for fan in fans], block_sizes(D))


def draw_rows_weights(key, part):
    key = jax.random.fold_in(key, 32)
    fans = [E, max(1, E // 8), E, 4 * E]
    return scaled_normal(key, [fan ** (-0.5) for fan in fans], block_sizes(E))


def draw_sets_first(key, part):
    key = jax.random.fold_in(key, 41)
    return scaled_normal(key, set_scales(), block_sizes(D))


def draw_rows_first(key, part):
    key = jax.random.fold_in(key, 42)
    return scaled_normal(key, row_scales(), block_sizes(E))


def draw_gains_first(key, part):
    key = jax.random.fold_in(key, 43)
    return scaled_normal(key, gain_scales(), [2 * D, 2 * E])


def draw_sets_second(key, part):
    key = jax.random.fold_in(key, 51)
    return scaled_square(key, set_scales(), block_sizes(D))


def draw_rows_second(key, part):
    key = jax.random.fold_in(key, 52)
    return scaled_square(key, row_scales(), block_sizes(E))


def draw_gains_second(key, part):
    key = jax.random.fold_in(key, 53)
    return scaled_square(key, gain_scales(), [2 * D, 2 * E])


def level_of(rng, shape, cuts, least, top_value):
    level, own = 1.0, jax.random.fold_in(rng, 6)
    for dim, blocks in cuts:
        heights = jnp.exp(jax.random.uniform(jax.random.fold_in(own, dim), (blocks,), jnp.float32, least / len(cuts), top_value / len(cuts)))
        level = level * jnp.repeat(heights, shape[dim] // blocks).reshape([-1 if axis == dim else 1 for axis in range(len(shape))])
    return level


def bell_draw(rng, dims, width, bound, shards=(), held_as=jnp.bfloat16):
    array = jax.random.normal(rng, dims, jnp.float32) * width
    if len(shards) > 0:
        array = level_of(rng, dims, shards, -0.22, 0.18) * array
    return jnp.clip(array, min=-bound, max=bound).astype(held_as)


def setup_inputs(seed: int = 0) -> dict:
    splits = jax.random.split(jax.random.key(seed), 13)
    return {
        "cells_in": bell_draw(splits[0], (ROWS, D), 1.0, 6.0, ((0, 32),)),
        "lengths": draw_lengths(jax.random.fold_in(splits[12], 71), 0),
        "sets_weights": draw_sets_weights(jax.random.fold_in(splits[12], 71), 0),
        "rows_weights": draw_rows_weights(jax.random.fold_in(splits[12], 71), 0),
        "norm_gains": jnp.clip(1.0 + 0.1 * jax.random.normal(splits[4], (P_GAIN,), jnp.float32), 0.5, 1.5),
        "sets_first": draw_sets_first(jax.random.fold_in(splits[12], 71), 0),
        "rows_first": draw_rows_first(jax.random.fold_in(splits[12], 71), 0),
        "gains_first": draw_gains_first(jax.random.fold_in(splits[12], 71), 0),
        "sets_second": draw_sets_second(jax.random.fold_in(splits[12], 71), 0),
        "rows_second": draw_rows_second(jax.random.fold_in(splits[12], 71), 0),
        "gains_second": draw_gains_second(jax.random.fold_in(splits[12], 71), 0),
        "out_grad": bell_draw(splits[11], (REAL_ROWS, D), 1.0, 6.0, ((0, 32),)),
    }


@jax.custom_vjp
def low(v):
    return lax.optimization_barrier(v.astype(jnp.bfloat16)).astype(jnp.float32)

@jax.custom_vjp
def low_back(v):
    return v

def low_keep(v):
    return (low(v), None)

def low_pass(kept, grad):
    return (grad,)

def back_keep(v):
    return (v, None)

def back_low(kept, grad):
    return (low(grad),)
low.defvjp(low_keep, low_pass)
low_back.defvjp(back_keep, back_low)
highest = lax.Precision.HIGHEST
norm_eps = 1e-05
beta_one = 0.5
beta_two = 0.5
adam_eps = 1e-08
decay_rate = 0.1
gain_rate = 0.5

def matmul(left, right):
    return jnp.matmul(left, right, precision=highest)

def norm_gain(inputs, gain_vec):
    center = inputs - lax.optimization_barrier(jnp.mean(inputs, axis=-1, keepdims=True))
    spread = lax.optimization_barrier(jnp.mean(center * center, axis=-1, keepdims=True))
    return center * lax.rsqrt(spread + norm_eps) * gain_vec

def split_block(flat, feature):
    cut_one = 3 * feature * feature
    cut_two = cut_one + feature * feature
    cut_three = cut_two + 4 * feature * feature
    return (flat[:cut_one].reshape(feature, 3 * feature), flat[cut_one:cut_two].reshape(feature, feature), flat[cut_two:cut_three].reshape(feature, 4 * feature), flat[cut_three:].reshape(4 * feature, feature))

def split_gains(flat, model_width, feature):
    return (flat[:model_width], flat[model_width:2 * model_width], flat[2 * model_width:2 * model_width + feature], flat[2 * model_width + feature:])

def block_rates(position, feature, out_fan):
    cut_one = 3 * feature * feature
    cut_two = cut_one + feature * feature
    cut_three = cut_two + 4 * feature * feature
    fans = (feature, out_fan, feature, 4 * feature)
    rates = [0.5 * fan ** (-0.5) for fan in fans]
    return jnp.where(position < cut_one, rates[0], jnp.where(position < cut_two, rates[1], jnp.where(position < cut_three, rates[2], rates[3]))).astype(jnp.float32)

def adam_update(weight, gradient, first, second, rates, decay):
    first_new = beta_one * first + (1.0 - beta_one) * gradient
    second_new = beta_two * second + (1.0 - beta_two) * gradient * gradient
    corrected = first_new / (1.0 - beta_one ** STEP)
    scaled = second_new / (1.0 - beta_two ** STEP)
    weight_new = weight - rates * (corrected / (jnp.sqrt(scaled) + adam_eps) + decay * weight)
    return (weight_new, first_new, second_new)

def mlp_block(inputs, gain_vec, w_up, w_down):
    normed = low(norm_gain(inputs, gain_vec))
    before = low_back(matmul(normed, w_up))
    hidden = low(jax.nn.gelu(before, approximate=False))
    return inputs + low_back(matmul(hidden, w_down))

def set_block(inputs, lengths_here, params):
    w_qkv, w_out, w_up, w_down, gain_one, gain_two = params
    slots, feature = inputs.shape
    head_size = feature // HEADS
    normed = low(norm_gain(inputs, gain_one))
    joined = low_back(low(matmul(normed, w_qkv))).reshape(slots, 3, HEADS, head_size)
    queries, key_rows, values = (joined[:, 0], joined[:, 1], joined[:, 2])
    ends_at = jnp.cumsum(lengths_here).astype(jnp.int32)
    positions = jnp.arange(slots, dtype=jnp.int32)
    labels = lax.optimization_barrier(jnp.sum((positions[:, None] >= ends_at[None, :]).astype(jnp.int32), axis=1)).astype(jnp.int32)
    related = labels[:, None] == labels[None, :]
    scores = low_back(jnp.einsum('qhd,khd->hqk', queries, key_rows, precision=highest) * head_size ** (-0.5))
    scores = jnp.where(related[None], scores, -jnp.inf)
    chance = low(jax.nn.softmax(scores, axis=-1))
    blended = low_back(low(jnp.einsum('hqk,khd->qhd', chance, values, precision=highest).reshape(slots, feature)))
    after = inputs + low_back(matmul(blended, w_out))
    return mlp_block(after, gain_two, w_up, w_down)

def row_block(inputs, params):
    w_qkv, w_out, w_up, w_down, gain_three, gain_four = params
    row_count = inputs.shape[0]
    head_size = E // HEADS
    cells = inputs.reshape(row_count, ATTRS, E)
    normed = low(norm_gain(cells, gain_three))
    joined = low_back(low(matmul(normed, w_qkv))).reshape(row_count, ATTRS, 3, HEADS, head_size)
    queries, key_rows, values = (joined[:, :, 0], joined[:, :, 1], joined[:, :, 2])
    scores = low_back(jnp.einsum('rahd,rbhd->rhab', queries, key_rows, precision=highest) * head_size ** (-0.5))
    chance = low(jax.nn.softmax(scores, axis=-1))
    blended = low_back(low(jnp.einsum('rhab,rbhd->rahd', chance, values, precision=highest).reshape(row_count, ATTRS, E)))
    after = cells + low_back(matmul(blended, w_out))
    return mlp_block(after, gain_four, w_up, w_down).reshape(row_count, ATTRS * E)

def compact_index(lengths):
    length_table = lengths.reshape(DEVS, SETS_DEV)
    counts = (lax.optimization_barrier(jnp.sum(length_table, axis=1)) // DEVS).astype(jnp.int32)
    ends_at = jnp.cumsum(counts).astype(jnp.int32)
    starts = (ends_at - counts).astype(jnp.int32)
    position = jnp.arange(ROWS_EVEN, dtype=jnp.int32)
    source = lax.optimization_barrier(jnp.sum((ends_at[None, :] <= position[:, None]).astype(jnp.int32), axis=1)).astype(jnp.int32)
    within = (position - jnp.take(starts, source)).astype(jnp.int32)
    owner = jnp.arange(DEVS, dtype=jnp.int32)
    return (source[None, :] * CAP + within[None, :] * DEVS + owner[:, None]).reshape(-1).astype(jnp.int32)

def forward(cells, set_flat, row_flat, gain_flat, lengths):
    model_width = ATTRS * E
    wq1, wo1, wu1, wd1 = split_block(set_flat, model_width)
    wq2, wo2, wu2, wd2 = split_block(row_flat, E)
    gain_one, gain_two, gain_three, gain_four = split_gains(gain_flat, model_width, E)
    params_one = (wq1, wo1, wu1, wd1, gain_one, gain_two)
    params_two = (wq2, wo2, wu2, wd2, gain_three, gain_four)
    blocks = cells.reshape(DEVS, CAP, model_width)
    length_table = lengths.reshape(DEVS, SETS_DEV)
    mixed = lax.map(jax.checkpoint(lambda item: set_block(item[0], item[1], params_one)), (blocks, length_table))
    gathered = jnp.take(mixed.reshape(-1, model_width), compact_index(lengths), axis=0)
    rows_in = gathered.reshape(DEVS, ROWS_EVEN, model_width)
    final = lax.map(jax.checkpoint(lambda item: row_block(item, params_two)), rows_in)
    return final.reshape(-1, model_width)

def rounded(inputs):
    return lax.optimization_barrier(inputs.astype(jnp.bfloat16)).astype(jnp.float32)

def reference(cells_in, lengths, sets_weights, rows_weights, norm_gains, sets_first, rows_first, gains_first, sets_second, rows_second, gains_second, out_grad):
    model_width = ATTRS * E
    result, pull = jax.vjp(lambda cells, set_flat, row_flat, gain_flat: forward(cells, set_flat, row_flat, gain_flat, lengths), cells_in.astype(jnp.float32), rounded(sets_weights), rounded(rows_weights), rounded(norm_gains))
    cells_grad, sets_grad, rows_grad, gains_grad = pull(out_grad.astype(jnp.float32))
    set_rates = block_rates(jnp.arange(P_ABD, dtype=jnp.int32), model_width, max(1, 3 * model_width // CAP))
    row_rates = block_rates(jnp.arange(P_ABA, dtype=jnp.int32), E, max(1, E // 8))
    sets_new, sets_first_new, sets_second_new = adam_update(sets_weights, sets_grad, sets_first, sets_second, set_rates, decay_rate)
    rows_new, rows_first_new, rows_second_new = adam_update(rows_weights, rows_grad, rows_first, rows_second, row_rates, decay_rate)
    gains_new, gains_first_new, gains_second_new = adam_update(norm_gains, gains_grad, gains_first, gains_second, gain_rate, 0.0)
    return (result.astype(jnp.bfloat16), cells_grad, sets_grad, rows_grad, gains_grad, sets_new, rows_new, gains_new, sets_first_new, rows_first_new, gains_first_new, sets_second_new, rows_second_new, gains_second_new, sets_new.astype(jnp.bfloat16), rows_new.astype(jnp.bfloat16), gains_new.astype(jnp.bfloat16))
```

```python
import functools

import jax
import jax.numpy as jnp
from jax import lax
from jax.experimental import pallas as pl
from jax.experimental.pallas import tpu as pltpu
from jax.sharding import PartitionSpec as P

ATTRS = 16
HEADS = 8
SETS_DEV = 2
STEP = 5
LANES = 128

norm_eps = 1e-05
beta_one = 0.5
beta_two = 0.5
adam_eps = 1e-08
decay_rate = 0.1
gain_rate = 0.5

def mm(left, right, dims):
    return lax.dot_general(left, right, (dims, ((), ())), preferred_element_type=jnp.float32)


def gelu_pair(v):
    size = jnp.abs(v) * 0.7071067811865476
    t = 1.0 / (1.0 + 0.3275911 * size)
    bell = jnp.exp(-0.5 * v * v)
    poly = t * (0.254829592 + t * (-0.284496736 + t * (1.421413741 + t * (-1.453152027 + t * 1.061405429))))
    tail = 0.5 * poly * bell
    phi = jnp.where(v < 0.0, tail, 1.0 - tail)
    return v * phi, phi + v * (bell * 0.3989422804014327)


def rows_kernel(
    pick_ref, arrived_ref, og_ref, wq_ref, wqt_ref, wo_ref, wot_ref, wu_ref, wut_ref, wd_ref, wdt_ref, g3_ref, g4_ref,
    out_ref, back_ref, dwq_ref, dwo_ref, dwu_ref, dwd_ref, dg3_ref, dg4_ref,
    joined, prob, dscore, outs, douts, dj, back_acc,
):
    f32, bf = jnp.float32, jnp.bfloat16
    step = pl.program_id(0)
    last = pl.num_programs(0) - 1
    slots = arrived_ref.shape[0]
    scaling = HEADS ** (-0.5)
    feat = 64

    @pl.when(step == 0)
    def _():
        for ref in (dwq_ref, dwo_ref, dwu_ref, dwd_ref, dg3_ref, dg4_ref, back_acc):
            ref[...] = jnp.zeros_like(ref)

    source = lax.broadcasted_iota(jnp.int32, (slots, LANES), 0)
    hot = (source == pick_ref[0]).astype(f32).astype(bf)
    x_t = mm(arrived_ref[...], hot, ((0,), (0,)))

    def to_lanes(tall):
        return jnp.concatenate([tall[a * feat : (a + 1) * feat] for a in range(ATTRS)], axis=1)

    def to_tall(wide):
        return jnp.concatenate([wide[:, a * LANES : (a + 1) * LANES] for a in range(ATTRS)], axis=0)

    def norm(v):
        center = v - jnp.mean(v, axis=0, keepdims=True)
        root = lax.rsqrt(jnp.mean(center * center, axis=0, keepdims=True) + norm_eps)
        return center * root, root

    def norm_back(hat, root, gain, upstream):
        dhat = upstream * gain
        return root * (
            dhat - jnp.mean(dhat, axis=0, keepdims=True) - hat * jnp.mean(dhat * hat, axis=0, keepdims=True)
        )

    def fold(v):
        total = v[:, :LANES]
        for a in range(1, ATTRS):
            total = total + v[:, a * LANES : (a + 1) * LANES]
        return total

    x = to_lanes(x_t)
    g3, g4 = g3_ref[...], g4_ref[...]
    hat3, root3 = norm(x)
    a3 = (hat3 * g3).astype(bf)
    j_t = mm(wqt_ref[...], a3, ((1,), (0,))).astype(bf).astype(f32)
    for a in range(ATTRS):
        joined[a] = j_t[:, a * LANES : (a + 1) * LANES]

    def attend(a, carry):
        q = [joined[a, d * 8 : d * 8 + 8] * scaling for d in range(8)]
        scores = []
        for b in range(ATTRS):
            s = q[0] * joined[b, 64:72]
            for d in range(1, 8):
                s = s + q[d] * joined[b, 64 + d * 8 : 72 + d * 8]
            scores.append(s)
        peak = functools.reduce(jnp.maximum, scores)
        weights = [jnp.exp(s - peak) for s in scores]
        inverse = 1.0 / functools.reduce(jnp.add, weights)
        o = [None] * 8
        for b in range(ATTRS):
            p = weights[b] * inverse
            prob[a, b] = p
            p = p.astype(bf).astype(f32)
            for d in range(8):
                term = p * joined[b, 128 + d * 8 : 136 + d * 8]
                o[d] = term if b == 0 else o[d] + term
        for d in range(8):
            outs[a, d * 8 : d * 8 + 8] = o[d]
        return carry

    lax.fori_loop(0, ATTRS, attend, 0)
    o = jnp.concatenate([outs[a] for a in range(ATTRS)], axis=1).astype(bf)
    h3 = x + mm(wot_ref[...], o, ((1,), (0,)))
    hat4, root4 = norm(h3)
    a4 = (hat4 * g4).astype(bf)
    pre = mm(wut_ref[...], a4, ((1,), (0,)))
    active, slope = gelu_pair(pre)
    u = active.astype(bf)
    y = h3 + mm(wdt_ref[...], u, ((1,), (0,)))
    out_ref[...] = to_tall(y).T.astype(bf)

    grad = to_lanes(og_ref[...].astype(f32).T)
    gz = grad.astype(bf)
    dwd_ref[...] += mm(u, gz, ((1,), (1,)))
    dpre = (slope * mm(wd_ref[...], gz, ((1,), (0,)))).astype(bf)
    dwu_ref[...] += mm(a4, dpre, ((1,), (1,)))
    da4 = mm(wu_ref[...], dpre, ((1,), (0,)))
    dg4_ref[...] += fold(da4 * hat4)
    dh3 = grad + norm_back(hat4, root4, g4, da4)

    gz = dh3.astype(bf)
    dwo_ref[...] += mm(o, gz, ((1,), (1,)))
    do = mm(wo_ref[...], gz, ((1,), (0,))).astype(bf).astype(f32)
    for a in range(ATTRS):
        douts[a] = do[:, a * LANES : (a + 1) * LANES]

    def spread(a, carry):
        up = [douts[a, d * 8 : d * 8 + 8] for d in range(8)]
        dot = None
        slopes = []
        for b in range(ATTRS):
            s = up[0] * joined[b, 128:136]
            for d in range(1, 8):
                s = s + up[d] * joined[b, 128 + d * 8 : 136 + d * 8]
            slopes.append(s)
            term = prob[a, b] * s
            dot = term if b == 0 else dot + term
        dq = [None] * 8
        for b in range(ATTRS):
            ds = (prob[a, b] * (slopes[b] - dot)).astype(bf).astype(f32) * scaling
            dscore[a, b] = ds
            for d in range(8):
                term = ds * joined[b, 64 + d * 8 : 72 + d * 8]
                dq[d] = term if b == 0 else dq[d] + term
        for d in range(8):
            dj[a, d * 8 : d * 8 + 8] = dq[d]
        return carry

    lax.fori_loop(0, ATTRS, spread, 0)

    def collect(b, carry):
        dk, dv = [None] * 8, [None] * 8
        for a in range(ATTRS):
            ds = dscore[a, b]
            p = prob[a, b].astype(bf).astype(f32)
            for d in range(8):
                one = ds * joined[a, d * 8 : d * 8 + 8]
                two = p * douts[a, d * 8 : d * 8 + 8]
                dk[d] = one if a == 0 else dk[d] + one
                dv[d] = two if a == 0 else dv[d] + two
        for d in range(8):
            dj[b, 64 + d * 8 : 72 + d * 8] = dk[d]
            dj[b, 128 + d * 8 : 136 + d * 8] = dv[d]
        return carry

    lax.fori_loop(0, ATTRS, collect, 0)
    djl = jnp.concatenate([dj[a] for a in range(ATTRS)], axis=1).astype(bf)
    dwq_ref[...] += mm(a3, djl, ((1,), (1,)))
    da3 = mm(wq_ref[...], djl, ((1,), (0,)))
    dg3_ref[...] += fold(da3 * hat3)
    dhc = to_tall(dh3 + norm_back(hat3, root3, g3, da3)).astype(bf)
    back_acc[...] += mm(hot, dhc, ((1,), (1,)))

    @pl.when(step == last)
    def _():
        back_ref[...] = back_acc[...].astype(bf)


def rows_layer(pick, arrived, og, wq, wo, wu, wd, g3, g4):
    f32, bf = jnp.float32, jnp.bfloat16
    total, width = og.shape
    slots = arrived.shape[0]
    steps = total // LANES
    feat = 64
    wqp = wq.reshape(feat, 3, HEADS, 8).transpose(0, 1, 3, 2).reshape(feat, 3 * feat)
    wop = wo.reshape(HEADS, 8, feat).transpose(1, 0, 2).reshape(feat, feat)
    whole = lambda *shape: pl.BlockSpec(shape, lambda t: (0,) * len(shape))
    outs = pl.pallas_call(
        rows_kernel,
        grid=(steps,),
        in_specs=[
            pl.BlockSpec((1, 1, LANES), lambda t: (t, 0, 0)),
            whole(slots, width),
            pl.BlockSpec((LANES, width), lambda t: (t, 0)),
            whole(feat, 192), whole(192, feat), whole(feat, feat), whole(feat, feat),
            whole(feat, 256), whole(256, feat), whole(256, feat), whole(feat, 256),
            whole(feat, 1), whole(feat, 1),
        ],
        out_specs=[
            pl.BlockSpec((LANES, width), lambda t: (t, 0)),
            whole(slots, width),
            whole(feat, 192), whole(feat, feat), whole(feat, 256), whole(256, feat),
            whole(feat, LANES), whole(feat, LANES),
        ],
        out_shape=[
            jax.ShapeDtypeStruct((total, width), bf),
            jax.ShapeDtypeStruct((slots, width), bf),
            jax.ShapeDtypeStruct((feat, 192), f32),
            jax.ShapeDtypeStruct((feat, feat), f32),
            jax.ShapeDtypeStruct((feat, 256), f32),
            jax.ShapeDtypeStruct((256, feat), f32),
            jax.ShapeDtypeStruct((feat, LANES), f32),
            jax.ShapeDtypeStruct((feat, LANES), f32),
        ],
        scratch_shapes=[
            pltpu.VMEM((ATTRS, 192, LANES), f32),
            pltpu.VMEM((ATTRS, ATTRS, 8, LANES), f32),
            pltpu.VMEM((ATTRS, ATTRS, 8, LANES), f32),
            pltpu.VMEM((ATTRS, 64, LANES), f32),
            pltpu.VMEM((ATTRS, 64, LANES), f32),
            pltpu.VMEM((ATTRS, 192, LANES), f32),
            pltpu.VMEM((slots, width), f32),
        ],
        compiler_params=pltpu.CompilerParams(vmem_limit_bytes=56 * 2**20),
    )(
        pick.reshape(steps, 1, LANES), arrived, og,
        wqp, wqp.T, wop, wop.T, wu, wu.T, wd, wd.T, g3.reshape(feat, 1), g4.reshape(feat, 1),
    )
    rows_out, back, dwqp, dwop, dwu, dwd, dg3, dg4 = outs
    dwq = dwqp.reshape(feat, 3, 8, HEADS).transpose(0, 1, 3, 2).reshape(feat, 3 * feat)
    dwo = dwop.reshape(8, HEADS, feat).transpose(1, 0, 2).reshape(feat, feat)
    return rows_out, back, dwq, dwo, dwu, dwd, jnp.sum(dg3, axis=1), jnp.sum(dg4, axis=1)


def fwd_mul(left, right):
    return mm(left, right, ((1,), (0,)))


def outer(left, right):
    return mm(left, right, ((0,), (0,)))


def backmul(upstream, weight):
    return mm(upstream, weight, ((1,), (1,)))


def norm_parts(inputs):
    center = inputs - jnp.mean(inputs, axis=-1, keepdims=True)
    root = lax.rsqrt(jnp.mean(center * center, axis=-1, keepdims=True) + norm_eps)
    return center * root, root


def norm_pull(hat, root, gain, upstream):
    dhat = upstream * gain
    inner = jnp.mean(dhat * hat, axis=-1, keepdims=True)
    grad = root * (dhat - jnp.mean(dhat, axis=-1, keepdims=True) - hat * inner)
    return grad, jnp.sum(upstream * hat, axis=0)


def running(values):
    number = jnp.arange(values.shape[0], dtype=jnp.int32)
    return jnp.sum(jnp.where(number[None, :] <= number[:, None], values[None, :], 0), axis=1)


def block_rates(position, feature, out_fan):
    cut_one = 3 * feature * feature
    cut_two = cut_one + feature * feature
    cut_three = cut_two + 4 * feature * feature
    fans = (feature, out_fan, feature, 4 * feature)
    rates = [0.5 * fan ** (-0.5) for fan in fans]
    return jnp.where(
        position < cut_one,
        rates[0],
        jnp.where(position < cut_two, rates[1], jnp.where(position < cut_three, rates[2], rates[3])),
    ).astype(jnp.float32)


def adam_update(weight, gradient, first, second, rates, decay):
    first_new = beta_one * first + (1.0 - beta_one) * gradient
    second_new = beta_two * second + (1.0 - beta_two) * gradient * gradient
    corrected = first_new / (1.0 - beta_one**STEP)
    scaled = second_new / (1.0 - beta_two**STEP)
    weight_new = weight - rates * (corrected / (jnp.sqrt(scaled) + adam_eps) + decay * weight)
    return (weight_new, first_new, second_new)


def local(
    cells_in, lengths, sets_weights, rows_weights, norm_gains, sets_first, rows_first, gains_first,
    sets_second, rows_second, gains_second, out_grad,
):
    f32, bf = jnp.float32, jnp.bfloat16
    devices = lax.axis_size("dev")
    device = lax.axis_index("dev")
    slots, width = cells_in.shape
    feat = width // ATTRS
    per_peer = slots // devices
    rows_even = out_grad.shape[0]
    rows_pad = -(-rows_even // LANES) * LANES
    head = width // HEADS
    scaling = head ** (-0.5)

    n_rows, n_gains = rows_weights.shape[0], norm_gains.shape[0]
    small = jnp.concatenate([rows_weights, norm_gains]).astype(bf)
    small = jnp.pad(small, (0, -small.shape[0] % 1024)).reshape(-1, 1024)
    small = lax.all_gather(small, "dev", axis=0, tiled=False).reshape(devices, -1)
    full_rows = small[:, :n_rows].reshape(-1)
    full_gains = small[:, n_rows : n_rows + n_gains].reshape(-1).astype(f32)
    flat = lax.all_gather(sets_weights.astype(bf).reshape(-1, width), "dev", axis=0, tiled=True)
    wq1 = flat[: 3 * width].reshape(width, 3 * width)
    wo1 = flat[3 * width : 4 * width]
    wu1 = flat[4 * width : 8 * width].reshape(width, 4 * width)
    wd1 = flat[8 * width :]
    square = feat * feat
    wq2 = full_rows[: 3 * square].reshape(feat, 3 * feat)
    wo2 = full_rows[3 * square : 4 * square].reshape(feat, feat)
    wu2 = full_rows[4 * square : 8 * square].reshape(feat, 4 * feat)
    wd2 = full_rows[8 * square :].reshape(4 * feat, feat)
    g1, g2 = full_gains[:width], full_gains[width : 2 * width]
    g3, g4 = full_gains[2 * width : 2 * width + feat], full_gains[2 * width + feat :]

    table = lengths.reshape(devices, SETS_DEV)
    own = lax.dynamic_index_in_dim(table, device, 0, keepdims=False)
    positions = jnp.arange(slots, dtype=jnp.int32)
    labels = jnp.sum((positions[:, None] >= running(own)[None, :]).astype(jnp.int32), axis=1)
    counts = jnp.sum(table, axis=1) // devices
    ends = running(counts)
    spot = jnp.arange(rows_pad, dtype=jnp.int32)
    past = (ends[None, :] <= spot[:, None]).astype(jnp.int32)
    source = jnp.sum(past, axis=1)
    start = jnp.sum(past * counts[None, :], axis=1)
    pick = jnp.where(spot < rows_even, source * per_peer + spot - start, -1)

    h0 = cells_in.astype(f32)
    hat1, root1 = norm_parts(h0)
    a1 = (hat1 * g1).astype(bf)
    joined = fwd_mul(a1, wq1).astype(bf).reshape(slots, 3, HEADS, head)
    queries, key_rows, values = joined[:, 0], joined[:, 1], joined[:, 2]
    related = labels[:, None] == labels[None, :]
    scores = jnp.einsum("qhd,khd->hqk", queries, key_rows, preferred_element_type=f32) * scaling
    scores = jnp.where(related[None], scores, -jnp.inf)
    weights = jnp.exp(scores - jnp.max(scores, axis=-1, keepdims=True))
    chance = weights / jnp.sum(weights, axis=-1, keepdims=True)
    chance_low = chance.astype(bf)
    o1 = jnp.einsum("hqk,khd->qhd", chance_low, values, preferred_element_type=f32).astype(bf).reshape(slots, width)
    h1 = h0 + fwd_mul(o1, wo1)
    hat2, root2 = norm_parts(h1)
    a2 = (hat2 * g2).astype(bf)
    active, slope = gelu_pair(fwd_mul(a2, wu1))
    u1 = active.astype(bf)
    h2 = h1 + fwd_mul(u1, wd1)

    outgoing = h2.astype(bf).reshape(per_peer, devices, width).transpose(1, 0, 2)
    arrived = lax.all_to_all(outgoing, "dev", split_axis=0, concat_axis=0, tiled=True)
    og = jnp.pad(out_grad, ((0, rows_pad - rows_even), (0, 0)))
    rows_out, back, dq2, do2, du2, dd2, dg3, dg4 = rows_layer(
        pick, arrived.reshape(slots, width), og, wq2, wo2, wu2, wd2, g3, g4
    )
    rows_out = rows_out[:rows_even]
    rows_flat = jnp.concatenate([dq2.reshape(-1), do2.reshape(-1), du2.reshape(-1), dd2.reshape(-1)])
    extra = rows_flat.reshape(devices, n_rows).astype(bf)
    extra = jnp.pad(extra, ((0, 0), (0, -n_rows % width))).reshape(devices, -1, width)
    payload = jnp.concatenate([back.reshape(devices, per_peer, width), extra], axis=1)
    returned = lax.all_to_all(payload, "dev", split_axis=0, concat_axis=0, tiled=True)
    grad = returned[:, :per_peer].transpose(1, 0, 2).reshape(slots, width).astype(f32)
    rows_grad = jnp.sum(returned[:, per_peer:].reshape(devices, -1)[:, :n_rows].astype(f32), axis=0)

    gz = grad.astype(bf)
    dd1 = outer(u1, gz).astype(bf)
    dpre = (slope * backmul(gz, wd1)).astype(bf)
    du1 = outer(a2, dpre).astype(bf)
    dh, dg2 = norm_pull(hat2, root2, g2, backmul(dpre, wu1))
    grad = grad + dh
    gz = grad.astype(bf)
    do1 = outer(o1, gz).astype(bf)
    dblend = backmul(gz, wo1).astype(bf).reshape(slots, HEADS, head)
    dchance = jnp.einsum("qhd,khd->hqk", dblend, values, preferred_element_type=f32)
    dot = jnp.sum(chance * dchance, axis=-1, keepdims=True)
    dscores = (chance * (dchance - dot)).astype(bf)
    dq = jnp.einsum("hqk,khd->qhd", dscores, key_rows, preferred_element_type=f32) * scaling
    dk = jnp.einsum("hqk,qhd->khd", dscores, queries, preferred_element_type=f32) * scaling
    dv = jnp.einsum("hqk,qhd->khd", chance_low, dblend, preferred_element_type=f32)
    djoined = jnp.concatenate([part.reshape(slots, width).astype(bf) for part in (dq, dk, dv)], axis=1)
    dq1 = outer(a1, djoined).astype(bf)
    dh, dg1 = norm_pull(hat1, root1, g1, backmul(djoined, wq1))
    cells_grad = grad + dh

    full = jnp.concatenate([dq1.reshape(-1, width), do1, du1.reshape(-1, width), dd1])
    sets_grad = lax.psum_scatter(full, "dev", scatter_dimension=0, tiled=True).astype(f32).reshape(-1)
    gains = jnp.concatenate([dg1, dg2, dg3, dg4]).reshape(devices, 1, n_gains)
    gains_grad = jnp.sum(lax.all_to_all(gains, "dev", split_axis=0, concat_axis=0, tiled=True), axis=(0, 1))

    set_index = device * sets_grad.shape[0] + jnp.arange(sets_grad.shape[0], dtype=jnp.int32)
    row_index = device * n_rows + jnp.arange(n_rows, dtype=jnp.int32)
    set_rates = block_rates(set_index, width, max(1, 3 * width // slots))
    row_rates = block_rates(row_index, feat, max(1, feat // 8))
    sets_new, sets_first_new, sets_second_new = adam_update(
        sets_weights, sets_grad, sets_first, sets_second, set_rates, decay_rate
    )
    rows_new, rows_first_new, rows_second_new = adam_update(
        rows_weights, rows_grad, rows_first, rows_second, row_rates, decay_rate
    )
    gains_new, gains_first_new, gains_second_new = adam_update(
        norm_gains, gains_grad, gains_first, gains_second, gain_rate, 0.0
    )
    return (
        rows_out, cells_grad, sets_grad, rows_grad, gains_grad, sets_new, rows_new, gains_new,
        sets_first_new, rows_first_new, gains_first_new, sets_second_new, rows_second_new, gains_second_new,
        sets_new.astype(bf), rows_new.astype(bf), gains_new.astype(bf),
    )


def solution(mesh):
    flat = P("dev")
    tall = P("dev", None)
    return jax.shard_map(
        local,
        mesh=mesh,
        in_specs=(tall, P()) + (flat,) * 9 + (tall,),
        out_specs=(tall, tall) + (flat,) * 15,
        check_vma=False,
    )
```

```python
import functools

import jax
import jax.numpy as jnp
import numpy as np
from jax import lax
from jax.experimental import pallas as pl
from jax.experimental.pallas import tpu as pltpu
from jax.sharding import PartitionSpec as P

ATTRS = 16
HEADS = 8
SETS_DEV = 2
STEP = 5
LANES = 128

norm_eps = 1e-05
beta_one = 0.5
beta_two = 0.5
adam_eps = 1e-08
decay_rate = 0.1
gain_rate = 0.5

def mm(left, right, dims):
    return lax.dot_general(left, right, (dims, ((), ())), preferred_element_type=jnp.float32)


def gelu_pair(v):
    size = jnp.abs(v) * 0.7071067811865476
    t = 1.0 / (1.0 + 0.3275911 * size)
    bell = jnp.exp(-0.5 * v * v)
    poly = t * (0.254829592 + t * (-0.284496736 + t * (1.421413741 + t * (-1.453152027 + t * 1.061405429))))
    tail = 0.5 * poly * bell
    phi = jnp.where(v < 0.0, tail, 1.0 - tail)
    return v * phi, phi + v * (bell * 0.3989422804014327)


def rows_kernel(
    pick_ref, arrived_ref, og_ref, wq_ref, wqt_ref, wo_ref, wot_ref, wu_ref, wut_ref, wd_ref, wdt_ref, g3_ref, g4_ref,
    out_ref, back_ref, dwq_ref, dwo_ref, dwu_ref, dwd_ref, dg3_ref, dg4_ref,
    joined, prob, dscore, outs, douts, dj, back_acc,
):
    f32, bf = jnp.float32, jnp.bfloat16
    step = pl.program_id(0)
    last = pl.num_programs(0) - 1
    slots = arrived_ref.shape[0]
    scaling = HEADS ** (-0.5)
    feat = 64

    @pl.when(step == 0)
    def _():
        for ref in (dwq_ref, dwo_ref, dwu_ref, dwd_ref, dg3_ref, dg4_ref, back_acc):
            ref[...] = jnp.zeros_like(ref)

    source = lax.broadcasted_iota(jnp.int32, (slots, LANES), 0)
    hot = (source == pick_ref[0]).astype(f32).astype(bf)
    x_t = mm(arrived_ref[...], hot, ((0,), (0,)))

    def to_lanes(tall):
        return jnp.concatenate([tall[a * feat : (a + 1) * feat] for a in range(ATTRS)], axis=1)

    def to_tall(wide):
        return jnp.concatenate([wide[:, a * LANES : (a + 1) * LANES] for a in range(ATTRS)], axis=0)

    def norm(v):
        center = v - jnp.mean(v, axis=0, keepdims=True)
        root = lax.rsqrt(jnp.mean(center * center, axis=0, keepdims=True) + norm_eps)
        return center * root, root

    def norm_back(hat, root, gain, upstream):
        dhat = upstream * gain
        return root * (
            dhat - jnp.mean(dhat, axis=0, keepdims=True) - hat * jnp.mean(dhat * hat, axis=0, keepdims=True)
        )

    def fold(v):
        total = v[:, :LANES]
        for a in range(1, ATTRS):
            total = total + v[:, a * LANES : (a + 1) * LANES]
        return total

    x = to_lanes(x_t)
    g3, g4 = g3_ref[...], g4_ref[...]
    hat3, root3 = norm(x)
    a3 = (hat3 * g3).astype(bf)
    j_t = mm(wqt_ref[...], a3, ((1,), (0,))).astype(bf).astype(f32)
    for a in range(ATTRS):
        joined[a] = j_t[:, a * LANES : (a + 1) * LANES]

    def attend(a, carry):
        q = [joined[a, d * 8 : d * 8 + 8] * scaling for d in range(8)]
        scores = []
        for b in range(ATTRS):
            s = q[0] * joined[b, 64:72]
            for d in range(1, 8):
                s = s + q[d] * joined[b, 64 + d * 8 : 72 + d * 8]
            scores.append(s)
        peak = functools.reduce(jnp.maximum, scores)
        weights = [jnp.exp(s - peak) for s in scores]
        inverse = 1.0 / functools.reduce(jnp.add, weights)
        o = [None] * 8
        for b in range(ATTRS):
            p = weights[b] * inverse
            prob[a, b] = p
            p = p.astype(bf).astype(f32)
            for d in range(8):
                term = p * joined[b, 128 + d * 8 : 136 + d * 8]
                o[d] = term if b == 0 else o[d] + term
        for d in range(8):
            outs[a, d * 8 : d * 8 + 8] = o[d]
        return carry

    lax.fori_loop(0, ATTRS, attend, 0)
    o = jnp.concatenate([outs[a] for a in range(ATTRS)], axis=1).astype(bf)
    h3 = x + mm(wot_ref[...], o, ((1,), (0,)))
    hat4, root4 = norm(h3)
    a4 = (hat4 * g4).astype(bf)
    pre = mm(wut_ref[...], a4, ((1,), (0,)))
    active, slope = gelu_pair(pre)
    u = active.astype(bf)
    y = h3 + mm(wdt_ref[...], u, ((1,), (0,)))
    out_ref[...] = to_tall(y).T.astype(bf)

    grad = to_lanes(og_ref[...].astype(f32).T)
    gz = grad.astype(bf)
    dwd_ref[...] += mm(u, gz, ((1,), (1,)))
    dpre = (slope * mm(wd_ref[...], gz, ((1,), (0,)))).astype(bf)
    dwu_ref[...] += mm(a4, dpre, ((1,), (1,)))
    da4 = mm(wu_ref[...], dpre, ((1,), (0,)))
    dg4_ref[...] += fold(da4 * hat4)
    dh3 = grad + norm_back(hat4, root4, g4, da4)

    gz = dh3.astype(bf)
    dwo_ref[...] += mm(o, gz, ((1,), (1,)))
    do = mm(wo_ref[...], gz, ((1,), (0,))).astype(bf).astype(f32)
    for a in range(ATTRS):
        douts[a] = do[:, a * LANES : (a + 1) * LANES]

    def spread(a, carry):
        up = [douts[a, d * 8 : d * 8 + 8] for d in range(8)]
        dot = None
        slopes = []
        for b in range(ATTRS):
            s = up[0] * joined[b, 128:136]
            for d in range(1, 8):
                s = s + up[d] * joined[b, 128 + d * 8 : 136 + d * 8]
            slopes.append(s)
            term = prob[a, b] * s
            dot = term if b == 0 else dot + term
        dq = [None] * 8
        for b in range(ATTRS):
            ds = (prob[a, b] * (slopes[b] - dot)).astype(bf).astype(f32) * scaling
            dscore[a, b] = ds
            for d in range(8):
                term = ds * joined[b, 64 + d * 8 : 72 + d * 8]
                dq[d] = term if b == 0 else dq[d] + term
        for d in range(8):
            dj[a, d * 8 : d * 8 + 8] = dq[d]
        return carry

    lax.fori_loop(0, ATTRS, spread, 0)

    def collect(b, carry):
        dk, dv = [None] * 8, [None] * 8
        for a in range(ATTRS):
            ds = dscore[a, b]
            p = prob[a, b].astype(bf).astype(f32)
            for d in range(8):
                one = ds * joined[a, d * 8 : d * 8 + 8]
                two = p * douts[a, d * 8 : d * 8 + 8]
                dk[d] = one if a == 0 else dk[d] + one
                dv[d] = two if a == 0 else dv[d] + two
        for d in range(8):
            dj[b, 64 + d * 8 : 72 + d * 8] = dk[d]
            dj[b, 128 + d * 8 : 136 + d * 8] = dv[d]
        return carry

    lax.fori_loop(0, ATTRS, collect, 0)
    djl = jnp.concatenate([dj[a] for a in range(ATTRS)], axis=1).astype(bf)
    dwq_ref[...] += mm(a3, djl, ((1,), (1,)))
    da3 = mm(wq_ref[...], djl, ((1,), (0,)))
    dg3_ref[...] += fold(da3 * hat3)
    dhc = to_tall(dh3 + norm_back(hat3, root3, g3, da3)).astype(bf)
    back_acc[...] += mm(hot, dhc, ((1,), (1,)))

    @pl.when(step == last)
    def _():
        back_ref[...] = back_acc[...].astype(bf)


def rows_layer(pick, arrived, og, wq, wo, wu, wd, g3, g4):
    f32, bf = jnp.float32, jnp.bfloat16
    total, width = og.shape
    slots = arrived.shape[0]
    steps = total // LANES
    feat = 64
    wqp = wq.reshape(feat, 3, HEADS, 8).transpose(0, 1, 3, 2).reshape(feat, 3 * feat)
    wop = wo.reshape(HEADS, 8, feat).transpose(1, 0, 2).reshape(feat, feat)
    whole = lambda *shape: pl.BlockSpec(shape, lambda t: (0,) * len(shape))
    outs = pl.pallas_call(
        rows_kernel,
        grid=(steps,),
        in_specs=[
            pl.BlockSpec((1, 1, LANES), lambda t: (t, 0, 0)),
            whole(slots, width),
            pl.BlockSpec((LANES, width), lambda t: (t, 0)),
            whole(feat, 192), whole(192, feat), whole(feat, feat), whole(feat, feat),
            whole(feat, 256), whole(256, feat), whole(256, feat), whole(feat, 256),
            whole(feat, 1), whole(feat, 1),
        ],
        out_specs=[
            pl.BlockSpec((LANES, width), lambda t: (t, 0)),
            whole(slots, width),
            whole(feat, 192), whole(feat, feat), whole(feat, 256), whole(256, feat),
            whole(feat, LANES), whole(feat, LANES),
        ],
        out_shape=[
            jax.ShapeDtypeStruct((total, width), bf),
            jax.ShapeDtypeStruct((slots, width), bf),
            jax.ShapeDtypeStruct((feat, 192), f32),
            jax.ShapeDtypeStruct((feat, feat), f32),
            jax.ShapeDtypeStruct((feat, 256), f32),
            jax.ShapeDtypeStruct((256, feat), f32),
            jax.ShapeDtypeStruct((feat, LANES), f32),
            jax.ShapeDtypeStruct((feat, LANES), f32),
        ],
        scratch_shapes=[
            pltpu.VMEM((ATTRS, 192, LANES), f32),
            pltpu.VMEM((ATTRS, ATTRS, 8, LANES), f32),
            pltpu.VMEM((ATTRS, ATTRS, 8, LANES), f32),
            pltpu.VMEM((ATTRS, 64, LANES), f32),
            pltpu.VMEM((ATTRS, 64, LANES), f32),
            pltpu.VMEM((ATTRS, 192, LANES), f32),
            pltpu.VMEM((slots, width), f32),
        ],
        compiler_params=pltpu.CompilerParams(vmem_limit_bytes=56 * 2**20),
    )(
        pick.reshape(steps, 1, LANES), arrived, og,
        wqp, wqp.T, wop, wop.T, wu, wu.T, wd, wd.T, g3.reshape(feat, 1), g4.reshape(feat, 1),
    )
    rows_out, back, dwqp, dwop, dwu, dwd, dg3, dg4 = outs
    dwq = dwqp.reshape(feat, 3, 8, HEADS).transpose(0, 1, 3, 2).reshape(feat, 3 * feat)
    dwo = dwop.reshape(8, HEADS, feat).transpose(1, 0, 2).reshape(feat, feat)
    return rows_out, back, dwq, dwo, dwu, dwd, jnp.sum(dg3, axis=1), jnp.sum(dg4, axis=1)


def flipped(bit):
    return [(d, d ^ bit) for d in range(32)]


def along_z(*moves):
    return [(src * 8 + i, dst * 8 + i) for src, dst in moves for i in range(8)]


CORE, SIDE_X, SIDE_Y = flipped(1), flipped(2), flipped(4)
CHAINS = (
    (((3, 2),), ((2, 1),), ((1, 0),)),
    (((3, 2), (0, 1)), ((2, 1),)),
    (((0, 1), (3, 2)), ((1, 2),)),
    (((0, 1),), ((1, 2),), ((2, 3),)),
)


def send(v, pairs):
    return lax.ppermute(v, "dev", pairs)


def plane_sum(group, spot):
    f32, bf = jnp.float32, jnp.bfloat16
    half = group.shape[1] // 2
    block = lambda i: lax.dynamic_index_in_dim(group, i, 0, keepdims=False)
    far, side, other = block(spot ^ 3), block(spot ^ 1), block(spot ^ 2)
    from_x = send(far[:half], SIDE_X)
    from_y = send(far[half:], SIDE_Y)
    side = jnp.concatenate([side[:half], (side[half:].astype(f32) + from_y.astype(f32)).astype(bf)])
    other = jnp.concatenate([(other[:half].astype(f32) + from_x.astype(f32)).astype(bf), other[half:]])
    return block(spot).astype(f32) + send(side, SIDE_X).astype(f32) + send(other, SIDE_Y).astype(f32)


def chain_sum(share, plane):
    for moves in CHAINS[plane]:
        share = share + send(share.astype(jnp.bfloat16), along_z(*moves)).astype(jnp.float32)
    return share


def chip_rows():
    table = []
    for chip in range(16):
        keys = []
        for flat in range(chip * 768, chip * 768 + 768):
            if flat < 3072:
                keys.append((flat % 3, flat // 3))
            elif flat < 4096 or flat >= 8192:
                keys.append((0 if flat < 4096 else 9, flat))
            else:
                keys.append((1 + flat % 4, flat // 4))
        order = sorted(range(768), key=lambda i: keys[i])
        place = [0] * 768
        for at, i in enumerate(order):
            place[i] = at
        table.append(place)
    return np.array(table, np.int32)


def sum_to_owners(groups, device):
    core, spot, plane = device % 2, device // 2 % 4, device // 8
    total = None
    for z in (3, 2, 1, 0):
        share = chain_sum(plane_sum(groups[z], spot), z)
        total = share if total is None else jnp.where(plane == z, share, total)
    order = lax.dynamic_index_in_dim(jnp.asarray(chip_rows()), device // 2, 0, keepdims=False)
    total = jnp.take(total, order, axis=0)
    rows, lanes = total.shape[0] // 2, total.shape[1]
    mine = lax.dynamic_slice_in_dim(total, core * rows, rows, 0)
    peer = send(lax.dynamic_slice_in_dim(total, (1 - core) * rows, rows, 0), CORE)
    return jnp.where(core == 0, jnp.concatenate([mine, peer], axis=1), jnp.concatenate([peer, mine], axis=1))


def both(v):
    return jnp.concatenate([v, send(v, CORE)])


def both_half(v, core, parts):
    width = v.shape[1] // parts
    half = width // 2
    pick = lambda c: jnp.concatenate(
        [lax.dynamic_slice_in_dim(v, j * width + c * half, half, 1) for j in range(parts)], axis=1
    )
    return jnp.concatenate([pick(core), send(pick(1 - core), CORE)])


def fwd_mul(left, right):
    return mm(left, right, ((1,), (0,)))


def outer(left, right):
    return mm(left, right, ((0,), (0,)))


def backmul(upstream, weight):
    return mm(upstream, weight, ((1,), (1,)))


def norm_parts(inputs):
    center = inputs - jnp.mean(inputs, axis=-1, keepdims=True)
    root = lax.rsqrt(jnp.mean(center * center, axis=-1, keepdims=True) + norm_eps)
    return center * root, root


def norm_pull(hat, root, gain, upstream):
    dhat = upstream * gain
    inner = jnp.mean(dhat * hat, axis=-1, keepdims=True)
    grad = root * (dhat - jnp.mean(dhat, axis=-1, keepdims=True) - hat * inner)
    return grad, jnp.sum(upstream * hat, axis=0)


def running(values):
    number = jnp.arange(values.shape[0], dtype=jnp.int32)
    return jnp.sum(jnp.where(number[None, :] <= number[:, None], values[None, :], 0), axis=1)


def block_rates(position, feature, out_fan):
    cut_one = 3 * feature * feature
    cut_two = cut_one + feature * feature
    cut_three = cut_two + 4 * feature * feature
    fans = (feature, out_fan, feature, 4 * feature)
    rates = [0.5 * fan ** (-0.5) for fan in fans]
    return jnp.where(
        position < cut_one,
        rates[0],
        jnp.where(position < cut_two, rates[1], jnp.where(position < cut_three, rates[2], rates[3])),
    ).astype(jnp.float32)


def adam_update(weight, gradient, first, second, rates, decay):
    first_new = beta_one * first + (1.0 - beta_one) * gradient
    second_new = beta_two * second + (1.0 - beta_two) * gradient * gradient
    corrected = first_new / (1.0 - beta_one**STEP)
    scaled = second_new / (1.0 - beta_two**STEP)
    weight_new = weight - rates * (corrected / (jnp.sqrt(scaled) + adam_eps) + decay * weight)
    return (weight_new, first_new, second_new)


def local(
    cells_in, lengths, sets_weights, rows_weights, norm_gains, sets_first, rows_first, gains_first,
    sets_second, rows_second, gains_second, out_grad,
):
    f32, bf = jnp.float32, jnp.bfloat16
    devices = lax.axis_size("dev")
    device = lax.axis_index("dev")
    slots, width = cells_in.shape
    feat = width // ATTRS
    per_peer = slots // devices
    rows_even = out_grad.shape[0]
    rows_pad = -(-rows_even // LANES) * LANES
    head = width // HEADS
    scaling = head ** (-0.5)
    grid = devices == 32 and width == 1024 and slots == 384

    n_rows, n_gains = rows_weights.shape[0], norm_gains.shape[0]
    small = jnp.concatenate([rows_weights, norm_gains]).astype(bf)
    small = jnp.pad(small, (0, -small.shape[0] % 1024)).reshape(-1, 1024)
    small = lax.all_gather(small, "dev", axis=0, tiled=False).reshape(devices, -1)
    full_rows = small[:, :n_rows].reshape(-1)
    full_gains = small[:, n_rows : n_rows + n_gains].reshape(-1).astype(f32)
    flat = lax.all_gather(sets_weights.astype(bf).reshape(-1, width), "dev", axis=0, tiled=True)
    wq1 = flat[: 3 * width].reshape(width, 3 * width)
    wo1 = flat[3 * width : 4 * width]
    wu1 = flat[4 * width : 8 * width].reshape(width, 4 * width)
    wd1 = flat[8 * width :]
    square = feat * feat
    wq2 = full_rows[: 3 * square].reshape(feat, 3 * feat)
    wo2 = full_rows[3 * square : 4 * square].reshape(feat, feat)
    wu2 = full_rows[4 * square : 8 * square].reshape(feat, 4 * feat)
    wd2 = full_rows[8 * square :].reshape(4 * feat, feat)
    g1, g2 = full_gains[:width], full_gains[width : 2 * width]
    g3, g4 = full_gains[2 * width : 2 * width + feat], full_gains[2 * width + feat :]

    table = lengths.reshape(devices, SETS_DEV)
    own = lax.dynamic_index_in_dim(table, device, 0, keepdims=False)
    positions = jnp.arange(slots, dtype=jnp.int32)
    labels = jnp.sum((positions[:, None] >= running(own)[None, :]).astype(jnp.int32), axis=1)
    counts = jnp.sum(table, axis=1) // devices
    ends = running(counts)
    spot = jnp.arange(rows_pad, dtype=jnp.int32)
    past = (ends[None, :] <= spot[:, None]).astype(jnp.int32)
    source = jnp.sum(past, axis=1)
    start = jnp.sum(past * counts[None, :], axis=1)
    pick = jnp.where(spot < rows_even, source * per_peer + spot - start, -1)

    h0 = cells_in.astype(f32)
    hat1, root1 = norm_parts(h0)
    a1 = (hat1 * g1).astype(bf)
    joined = fwd_mul(a1, wq1).astype(bf).reshape(slots, 3, HEADS, head)
    queries, key_rows, values = joined[:, 0], joined[:, 1], joined[:, 2]
    related = labels[:, None] == labels[None, :]
    scores = jnp.einsum("qhd,khd->hqk", queries, key_rows, preferred_element_type=f32) * scaling
    scores = jnp.where(related[None], scores, -jnp.inf)
    weights = jnp.exp(scores - jnp.max(scores, axis=-1, keepdims=True))
    chance = weights / jnp.sum(weights, axis=-1, keepdims=True)
    chance_low = chance.astype(bf)
    o1 = jnp.einsum("hqk,khd->qhd", chance_low, values, preferred_element_type=f32).astype(bf).reshape(slots, width)
    h1 = h0 + fwd_mul(o1, wo1)
    hat2, root2 = norm_parts(h1)
    a2 = (hat2 * g2).astype(bf)
    active, slope = gelu_pair(fwd_mul(a2, wu1))
    u1 = active.astype(bf)
    h2 = h1 + fwd_mul(u1, wd1)

    outgoing = h2.astype(bf).reshape(per_peer, devices, width).transpose(1, 0, 2)
    arrived = lax.all_to_all(outgoing, "dev", split_axis=0, concat_axis=0, tiled=True)
    og = jnp.pad(out_grad, ((0, rows_pad - rows_even), (0, 0)))
    rows_out, back, dq2, do2, du2, dd2, dg3, dg4 = rows_layer(
        pick, arrived.reshape(slots, width), og, wq2, wo2, wu2, wd2, g3, g4
    )
    rows_out = rows_out[:rows_even]
    rows_flat = jnp.concatenate([dq2.reshape(-1), do2.reshape(-1), du2.reshape(-1), dd2.reshape(-1)])
    extra = rows_flat.reshape(devices, n_rows).astype(bf)
    extra = jnp.pad(extra, ((0, 0), (0, -n_rows % width))).reshape(devices, -1, width)
    payload = jnp.concatenate([back.reshape(devices, per_peer, width), extra], axis=1)
    returned = lax.all_to_all(payload, "dev", split_axis=0, concat_axis=0, tiled=True)
    grad = returned[:, :per_peer].transpose(1, 0, 2).reshape(slots, width).astype(f32)
    rows_grad = jnp.sum(returned[:, per_peer:].reshape(devices, -1)[:, :n_rows].astype(f32), axis=0)

    gz = grad.astype(bf)
    if grid:
        core = device % 2
        a1_both, a2_both, o1_both, u1_both = both(a1), both(a2), both(o1), both(u1)
        dd1 = outer(u1_both, both_half(gz, core, 1)).astype(bf)
    else:
        dd1 = outer(u1, gz).astype(bf)
    dpre = (slope * backmul(gz, wd1)).astype(bf)
    if grid:
        dpre_half = both_half(dpre, core, 4)
        half = width // 2
        du1 = jnp.stack([outer(a2_both, dpre_half[:, j * half : (j + 1) * half]).astype(bf) for j in range(4)])
    else:
        du1 = outer(a2, dpre).astype(bf)
    dh, dg2 = norm_pull(hat2, root2, g2, backmul(dpre, wu1))
    grad = grad + dh
    gz = grad.astype(bf)
    if grid:
        do1 = outer(o1_both, both_half(gz, core, 1)).astype(bf)
    else:
        do1 = outer(o1, gz).astype(bf)
    dblend = backmul(gz, wo1).astype(bf).reshape(slots, HEADS, head)
    dchance = jnp.einsum("qhd,khd->hqk", dblend, values, preferred_element_type=f32)
    dot = jnp.sum(chance * dchance, axis=-1, keepdims=True)
    dscores = (chance * (dchance - dot)).astype(bf)
    dq = jnp.einsum("hqk,khd->qhd", dscores, key_rows, preferred_element_type=f32) * scaling
    dk = jnp.einsum("hqk,qhd->khd", dscores, queries, preferred_element_type=f32) * scaling
    dv = jnp.einsum("hqk,qhd->khd", chance_low, dblend, preferred_element_type=f32)
    djoined = jnp.concatenate([part.reshape(slots, width).astype(bf) for part in (dq, dk, dv)], axis=1)
    if grid:
        dj_half = both_half(djoined, core, 3)
        dq1 = [outer(a1_both, dj_half[:, j * half : (j + 1) * half]).astype(bf).reshape(4, width // 4, half) for j in range(3)]
    else:
        dq1 = outer(a1, djoined).astype(bf)
    dh, dg1 = norm_pull(hat1, root1, g1, backmul(djoined, wq1))
    cells_grad = grad + dh

    if grid:
        tall = lambda lo, hi: du1[:, lo:hi].reshape(4 * (hi - lo), half)
        groups = (
            jnp.concatenate(dq1, axis=1),
            jnp.concatenate([do1, tall(0, 128), tall(128, 320), tall(320, 512)]).reshape(4, -1, half),
            jnp.concatenate([tall(512, 704), tall(704, 896), tall(896, 1024), dd1[:1024]]).reshape(4, -1, half),
            dd1[1024:].reshape(4, -1, half),
        )
        sets_grad = sum_to_owners(groups, device).reshape(-1)
    else:
        full = jnp.concatenate([dq1.reshape(-1, width), do1, du1.reshape(-1, width), dd1])
        sets_grad = lax.psum_scatter(full, "dev", scatter_dimension=0, tiled=True).astype(f32).reshape(-1)
    gains = jnp.concatenate([dg1, dg2, dg3, dg4]).reshape(devices, 1, n_gains)
    gains_grad = jnp.sum(lax.all_to_all(gains, "dev", split_axis=0, concat_axis=0, tiled=True), axis=(0, 1))

    set_index = device * sets_grad.shape[0] + jnp.arange(sets_grad.shape[0], dtype=jnp.int32)
    row_index = device * n_rows + jnp.arange(n_rows, dtype=jnp.int32)
    set_rates = block_rates(set_index, width, max(1, 3 * width // slots))
    row_rates = block_rates(row_index, feat, max(1, feat // 8))
    sets_new, sets_first_new, sets_second_new = adam_update(
        sets_weights, sets_grad, sets_first, sets_second, set_rates, decay_rate
    )
    rows_new, rows_first_new, rows_second_new = adam_update(
        rows_weights, rows_grad, rows_first, rows_second, row_rates, decay_rate
    )
    gains_new, gains_first_new, gains_second_new = adam_update(
        norm_gains, gains_grad, gains_first, gains_second, gain_rate, 0.0
    )
    return (
        rows_out, cells_grad, sets_grad, rows_grad, gains_grad, sets_new, rows_new, gains_new,
        sets_first_new, rows_first_new, gains_first_new, sets_second_new, rows_second_new, gains_second_new,
        sets_new.astype(bf), rows_new.astype(bf), gains_new.astype(bf),
    )


def solution(mesh):
    flat = P("dev")
    tall = P("dev", None)
    return jax.shard_map(
        local,
        mesh=mesh,
        in_specs=(tall, P()) + (flat,) * 9 + (tall,),
        out_specs=(tall, tall) + (flat,) * 15,
        check_vma=False,
    )
```

```python
import functools

import jax
import jax.numpy as jnp
import numpy as np
from jax import lax
from jax.experimental import pallas as pl
from jax.experimental.pallas import tpu as pltpu
from jax.sharding import PartitionSpec as P

ATTRS = 16
HEADS = 8
SETS_DEV = 2
STEP = 5
LANES = 128

norm_eps = 1e-05
beta_one = 0.5
beta_two = 0.5
adam_eps = 1e-08
decay_rate = 0.1
gain_rate = 0.5


def mm(left, right, dims):
    return lax.dot_general(left, right, (dims, ((), ())), preferred_element_type=jnp.float32)


def gelu_pair(v):
    size = jnp.abs(v) * 0.7071067811865476
    t = 1.0 / (1.0 + 0.3275911 * size)
    bell = jnp.exp(-0.5 * v * v)
    poly = t * (0.254829592 + t * (-0.284496736 + t * (1.421413741 + t * (-1.453152027 + t * 1.061405429))))
    tail = 0.5 * poly * bell
    phi = jnp.where(v < 0.0, tail, 1.0 - tail)
    return v * phi, phi + v * (bell * 0.3989422804014327)


def rows_kernel(
    pick_ref, arrived_ref, og_ref, wq_ref, wqt_ref, wo_ref, wot_ref, wu_ref, wut_ref, wd_ref, wdt_ref, g3_ref, g4_ref,
    out_ref, back_ref, dwq_ref, dwo_ref, dwu_ref, dwd_ref, dg3_ref, dg4_ref,
    joined, prob, dscore, outs, douts, dj, back_acc,
):
    f32, bf = jnp.float32, jnp.bfloat16
    step = pl.program_id(0)
    last = pl.num_programs(0) - 1
    slots = arrived_ref.shape[0]
    scaling = HEADS ** (-0.5)
    feat = 64

    @pl.when(step == 0)
    def _():
        for ref in (dwq_ref, dwo_ref, dwu_ref, dwd_ref, dg3_ref, dg4_ref, back_acc):
            ref[...] = jnp.zeros_like(ref)

    source = lax.broadcasted_iota(jnp.int32, (slots, LANES), 0)
    hot = (source == pick_ref[0]).astype(f32).astype(bf)
    x_t = mm(arrived_ref[...], hot, ((0,), (0,)))

    def to_lanes(tall):
        return jnp.concatenate([tall[a * feat : (a + 1) * feat] for a in range(ATTRS)], axis=1)

    def to_tall(wide):
        return jnp.concatenate([wide[:, a * LANES : (a + 1) * LANES] for a in range(ATTRS)], axis=0)

    def norm(v):
        center = v - jnp.mean(v, axis=0, keepdims=True)
        root = lax.rsqrt(jnp.mean(center * center, axis=0, keepdims=True) + norm_eps)
        return center * root, root

    def norm_back(hat, root, gain, upstream):
        dhat = upstream * gain
        return root * (
            dhat - jnp.mean(dhat, axis=0, keepdims=True) - hat * jnp.mean(dhat * hat, axis=0, keepdims=True)
        )

    def fold(v):
        total = v[:, :LANES]
        for a in range(1, ATTRS):
            total = total + v[:, a * LANES : (a + 1) * LANES]
        return total

    x = to_lanes(x_t)
    g3, g4 = g3_ref[...], g4_ref[...]
    hat3, root3 = norm(x)
    a3 = (hat3 * g3).astype(bf)
    j_t = mm(wqt_ref[...], a3, ((1,), (0,))).astype(bf).astype(f32)
    for a in range(ATTRS):
        joined[a] = j_t[:, a * LANES : (a + 1) * LANES]

    def attend(a, carry):
        q = [joined[a, d * 8 : d * 8 + 8] * scaling for d in range(8)]
        scores = []
        for b in range(ATTRS):
            s = q[0] * joined[b, 64:72]
            for d in range(1, 8):
                s = s + q[d] * joined[b, 64 + d * 8 : 72 + d * 8]
            scores.append(s)
        peak = functools.reduce(jnp.maximum, scores)
        weights = [jnp.exp(s - peak) for s in scores]
        inverse = 1.0 / functools.reduce(jnp.add, weights)
        o = [None] * 8
        for b in range(ATTRS):
            p = weights[b] * inverse
            prob[a, b] = p
            p = p.astype(bf).astype(f32)
            for d in range(8):
                term = p * joined[b, 128 + d * 8 : 136 + d * 8]
                o[d] = term if b == 0 else o[d] + term
        for d in range(8):
            outs[a, d * 8 : d * 8 + 8] = o[d]
        return carry

    lax.fori_loop(0, ATTRS, attend, 0)
    o = jnp.concatenate([outs[a] for a in range(ATTRS)], axis=1).astype(bf)
    h3 = x + mm(wot_ref[...], o, ((1,), (0,)))
    hat4, root4 = norm(h3)
    a4 = (hat4 * g4).astype(bf)
    pre = mm(wut_ref[...], a4, ((1,), (0,)))
    active, slope = gelu_pair(pre)
    u = active.astype(bf)
    y = h3 + mm(wdt_ref[...], u, ((1,), (0,)))
    out_ref[...] = to_tall(y).T.astype(bf)

    grad = to_lanes(og_ref[...].astype(f32).T)
    gz = grad.astype(bf)
    dwd_ref[...] += mm(u, gz, ((1,), (1,)))
    dpre = (slope * mm(wd_ref[...], gz, ((1,), (0,)))).astype(bf)
    dwu_ref[...] += mm(a4, dpre, ((1,), (1,)))
    da4 = mm(wu_ref[...], dpre, ((1,), (0,)))
    dg4_ref[...] += fold(da4 * hat4)
    dh3 = grad + norm_back(hat4, root4, g4, da4)

    gz = dh3.astype(bf)
    dwo_ref[...] += mm(o, gz, ((1,), (1,)))
    do = mm(wo_ref[...], gz, ((1,), (0,))).astype(bf).astype(f32)
    for a in range(ATTRS):
        douts[a] = do[:, a * LANES : (a + 1) * LANES]

    def spread(a, carry):
        up = [douts[a, d * 8 : d * 8 + 8] for d in range(8)]
        dot = None
        slopes = []
        for b in range(ATTRS):
            s = up[0] * joined[b, 128:136]
            for d in range(1, 8):
                s = s + up[d] * joined[b, 128 + d * 8 : 136 + d * 8]
            slopes.append(s)
            term = prob[a, b] * s
            dot = term if b == 0 else dot + term
        dq = [None] * 8
        for b in range(ATTRS):
            ds = (prob[a, b] * (slopes[b] - dot)).astype(bf).astype(f32) * scaling
            dscore[a, b] = ds
            for d in range(8):
                term = ds * joined[b, 64 + d * 8 : 72 + d * 8]
                dq[d] = term if b == 0 else dq[d] + term
        for d in range(8):
            dj[a, d * 8 : d * 8 + 8] = dq[d]
        return carry

    lax.fori_loop(0, ATTRS, spread, 0)

    def collect(b, carry):
        dk, dv = [None] * 8, [None] * 8
        for a in range(ATTRS):
            ds = dscore[a, b]
            p = prob[a, b].astype(bf).astype(f32)
            for d in range(8):
                one = ds * joined[a, d * 8 : d * 8 + 8]
                two = p * douts[a, d * 8 : d * 8 + 8]
                dk[d] = one if a == 0 else dk[d] + one
                dv[d] = two if a == 0 else dv[d] + two
        for d in range(8):
            dj[b, 64 + d * 8 : 72 + d * 8] = dk[d]
            dj[b, 128 + d * 8 : 136 + d * 8] = dv[d]
        return carry

    lax.fori_loop(0, ATTRS, collect, 0)
    djl = jnp.concatenate([dj[a] for a in range(ATTRS)], axis=1).astype(bf)
    dwq_ref[...] += mm(a3, djl, ((1,), (1,)))
    da3 = mm(wq_ref[...], djl, ((1,), (0,)))
    dg3_ref[...] += fold(da3 * hat3)
    dhc = to_tall(dh3 + norm_back(hat3, root3, g3, da3)).astype(bf)
    back_acc[...] += mm(hot, dhc, ((1,), (1,)))

    @pl.when(step == last)
    def _():
        back_ref[...] = back_acc[...].astype(bf)


def rows_layer(pick, arrived, og, wq, wo, wu, wd, g3, g4):
    f32, bf = jnp.float32, jnp.bfloat16
    total, width = og.shape
    slots = arrived.shape[0]
    steps = total // LANES
    feat = 64
    wqp = wq.reshape(feat, 3, HEADS, 8).transpose(0, 1, 3, 2).reshape(feat, 3 * feat)
    wop = wo.reshape(HEADS, 8, feat).transpose(1, 0, 2).reshape(feat, feat)
    whole = lambda *shape: pl.BlockSpec(shape, lambda t: (0,) * len(shape))
    outs = pl.pallas_call(
        rows_kernel,
        grid=(steps,),
        in_specs=[
            pl.BlockSpec((1, 1, LANES), lambda t: (t, 0, 0)),
            whole(slots, width),
            pl.BlockSpec((LANES, width), lambda t: (t, 0)),
            whole(feat, 192), whole(192, feat), whole(feat, feat), whole(feat, feat),
            whole(feat, 256), whole(256, feat), whole(256, feat), whole(feat, 256),
            whole(feat, 1), whole(feat, 1),
        ],
        out_specs=[
            pl.BlockSpec((LANES, width), lambda t: (t, 0)),
            whole(slots, width),
            whole(feat, 192), whole(feat, feat), whole(feat, 256), whole(256, feat),
            whole(feat, LANES), whole(feat, LANES),
        ],
        out_shape=[
            jax.ShapeDtypeStruct((total, width), bf),
            jax.ShapeDtypeStruct((slots, width), bf),
            jax.ShapeDtypeStruct((feat, 192), f32),
            jax.ShapeDtypeStruct((feat, feat), f32),
            jax.ShapeDtypeStruct((feat, 256), f32),
            jax.ShapeDtypeStruct((256, feat), f32),
            jax.ShapeDtypeStruct((feat, LANES), f32),
            jax.ShapeDtypeStruct((feat, LANES), f32),
        ],
        scratch_shapes=[
            pltpu.VMEM((ATTRS, 192, LANES), f32),
            pltpu.VMEM((ATTRS, ATTRS, 8, LANES), f32),
            pltpu.VMEM((ATTRS, ATTRS, 8, LANES), f32),
            pltpu.VMEM((ATTRS, 64, LANES), f32),
            pltpu.VMEM((ATTRS, 64, LANES), f32),
            pltpu.VMEM((ATTRS, 192, LANES), f32),
            pltpu.VMEM((slots, width), f32),
        ],
        compiler_params=pltpu.CompilerParams(vmem_limit_bytes=56 * 2**20),
    )(
        pick.reshape(steps, 1, LANES), arrived, og,
        wqp, wqp.T, wop, wop.T, wu, wu.T, wd, wd.T, g3.reshape(feat, 1), g4.reshape(feat, 1),
    )
    rows_out, back, dwqp, dwop, dwu, dwd, dg3, dg4 = outs
    dwq = dwqp.reshape(feat, 3, 8, HEADS).transpose(0, 1, 3, 2).reshape(feat, 3 * feat)
    dwo = dwop.reshape(8, HEADS, feat).transpose(1, 0, 2).reshape(feat, feat)
    return rows_out, back, dwq, dwo, dwu, dwd, jnp.sum(dg3, axis=1), jnp.sum(dg4, axis=1)


def placed(flat):
    if flat < 3072:
        return flat % 3 * 1024 + flat // 3
    if flat < 4096 or flat >= 8192:
        return flat
    return 4096 + flat % 4 * 1024 + (flat - 4096) // 4


def shard_orders():
    orders, runs = [], []
    for d in range(32):
        places = [placed(384 * d + i) for i in range(384)]
        order = sorted(range(384), key=lambda i: places[i])
        orders.append(order)
        for at, i in enumerate(order):
            if at and places[i] == runs[-1][1] + runs[-1][2] and places[i] % 1024:
                runs[-1][2] += 1
            else:
                runs.append([384 * d + at, places[i], 1])
    return np.array(orders, np.int32), sorted((tuple(run) for run in runs), key=lambda run: run[1])


def forward_kernel(runs, turn, h0_ref, g1_ref, g2_ref, tall_ref, wide_ref, flat_ref,
                   big_ref, joined_ref, a1_ref, o1_ref, a2_ref, u1_ref, slope_ref, h1_ref, out_ref,
                   mats, bias, loaded, stored):
    f32, bf = jnp.float32, jnp.bfloat16
    slots, width = h0_ref.shape
    head = width // HEADS
    tile = 512
    groups = {}
    for n, (src, dst, rows) in enumerate(runs):
        copy = pltpu.make_async_copy(flat_ref.at[pl.ds(src, rows)], mats.at[pl.ds(dst, rows)], loaded.at[n])
        copy.start()
        groups.setdefault(dst // width, []).append(copy)
    saves = []

    def arrive(i):
        for copy in groups[i]:
            copy.wait()
        saves.append(pltpu.make_async_copy(mats.at[pl.ds(i * width, width)], big_ref.at[pl.ds(i * width, width)], stored.at[i]))
        saves[-1].start()

    def norm(v, gain):
        center = v - jnp.mean(v, axis=1, keepdims=True)
        root = lax.rsqrt(jnp.mean(center * center, axis=1, keepdims=True) + norm_eps)
        return (center * root * gain).astype(bf)

    bias[...] = jnp.where(tall_ref[...] == wide_ref[...], 0.0, -jnp.inf)
    a1_ref[...] = norm(h0_ref[...].astype(f32), g1_ref[...])
    for i in range(3):
        arrive(i)

        def project(t, carry):
            cols = pl.ds(pl.multiple_of(t * tile, tile), tile)
            joined_ref[:, pl.ds(pl.multiple_of(i * width + t * tile, tile), tile)] = mm(
                a1_ref[...], mats[i * width : (i + 1) * width, cols], ((1,), (0,))
            ).astype(bf)
            return carry

        lax.fori_loop(0, width // tile, project, 0)

    def attend(h, carry):
        part = lambda i: joined_ref[:, pl.ds(pl.multiple_of(i * width + h * head, head), head)]
        scores = mm(part(0), part(1), ((1,), (1,))) * head ** (-0.5) + bias[...]
        weights = jnp.exp(scores - jnp.max(scores, axis=1, keepdims=True))
        chance = weights * (1.0 / jnp.sum(weights, axis=1, keepdims=True))
        o1_ref[:, pl.ds(pl.multiple_of(h * head, head), head)] = mm(chance.astype(bf), part(2), ((1,), (0,))).astype(bf)
        return carry

    lax.fori_loop(0, HEADS, attend, 0)
    arrive(3)
    for t in range(width // tile):
        cols = slice(t * tile, (t + 1) * tile)
        h1_ref[:, cols] = h0_ref[:, cols].astype(f32) + mm(o1_ref[...], mats[3 * width : 4 * width, cols], ((1,), (0,)))
    a2_ref[...] = norm(h1_ref[...], g2_ref[...])
    for i in range(4):
        arrive(4 + i)

        def widen(t, carry):
            cols = pl.ds(pl.multiple_of(t * tile, tile), tile)
            active, slope = gelu_pair(mm(a2_ref[...], mats[(4 + i) * width : (5 + i) * width, cols], ((1,), (0,))))
            cols = pl.ds(pl.multiple_of(i * width + t * tile, tile), tile)
            u1_ref[:, cols] = active.astype(bf)
            slope_ref[:, cols] = slope.astype(bf)
            return carry

        lax.fori_loop(0, width // tile, widen, 0)
    for i in range(4):
        arrive(8 + i)
    to, source = (lax.broadcasted_iota(jnp.int32, (slots, slots), axis) for axis in (0, 1))
    hot = (source == to % turn * (slots // turn) + to // turn).astype(f32).astype(bf)
    for t in range(width // tile):
        cols = slice(t * tile, (t + 1) * tile)
        h2 = (h1_ref[:, cols] + mm(u1_ref[...], mats[8 * width :, cols], ((1,), (0,)))).astype(bf)
        out_ref[:, cols] = mm(hot, h2, ((1,), (0,))).astype(bf)
    for save in saves:
        save.wait()


def forward_layer(runs, turn, h0, g1, g2, labels, flat):
    f32, bf = jnp.float32, jnp.bfloat16
    slots, width = h0.shape
    vmem = pl.BlockSpec(memory_space=pltpu.VMEM)
    anywhere = pl.BlockSpec(memory_space=pl.ANY)
    shape = jax.ShapeDtypeStruct
    return pl.pallas_call(
        functools.partial(forward_kernel, runs, turn),
        in_specs=[vmem] * 5 + [anywhere],
        out_specs=[anywhere] + [vmem] * 8,
        out_shape=[
            shape(flat.shape, bf),
            shape((slots, 3 * width), bf),
            shape((slots, width), bf),
            shape((slots, width), bf),
            shape((slots, width), bf),
            shape((slots, 4 * width), bf),
            shape((slots, 4 * width), bf),
            shape((slots, width), f32),
            shape((slots, width), bf),
        ],
        scratch_shapes=[
            pltpu.VMEM(flat.shape, bf),
            pltpu.VMEM((slots, slots), f32),
            pltpu.SemaphoreType.DMA((len(runs),)),
            pltpu.SemaphoreType.DMA((12,)),
        ],
        compiler_params=pltpu.CompilerParams(vmem_limit_bytes=56 * 2**20),
        cost_estimate=pl.CostEstimate(flops=10**10, bytes_accessed=64 * 2**20, transcendentals=3 * 10**6),
    )(h0, g1.reshape(1, -1), g2.reshape(1, -1), labels.reshape(-1, 1), labels.reshape(1, -1), flat)


def pull_norm(v, gain, upstream):
    center = v - jnp.mean(v, axis=1, keepdims=True)
    root = lax.rsqrt(jnp.mean(center * center, axis=1, keepdims=True) + norm_eps)
    hat = center * root
    dhat = upstream * gain
    inner = jnp.mean(dhat * hat, axis=1, keepdims=True)
    grad = root * (dhat - jnp.mean(dhat, axis=1, keepdims=True) - hat * inner)
    return grad, jnp.sum(upstream * hat, axis=0, keepdims=True)


def widen_back_kernel(core_ref, gz_ref, slope_ref, h1_ref, g2_ref, big_ref, dpre_ref, dh_ref, gz_out_ref, dg_ref, ups, downs, da, sems):
    f32, bf = jnp.float32, jnp.bfloat16
    width = gz_ref.shape[1]
    half = width // 2
    core = core_ref[0]
    copies = []
    for i in range(4):
        for n, (first, held) in enumerate(((8, downs), (4, ups))):
            rows = pl.ds((first + i) * width, width)
            copies.append(pltpu.make_async_copy(big_ref.at[rows], held.at[pl.ds(i * width, width)], sems.at[2 * i + n]))
            copies[-1].start()
    da[...] = jnp.zeros_like(da)
    for i in range(4):
        copies[2 * i].wait()
        copies[2 * i + 1].wait()

        def side(s, carry):
            hidden = pl.ds(pl.multiple_of(i * width + s * half, half), half)
            lanes = pl.ds(pl.multiple_of(s * half, half), half)
            du = mm(gz_ref[...], downs[hidden], ((1,), (1,)))
            dpre = (slope_ref[:, hidden].astype(f32) * du).astype(bf)
            dpre_ref[s ^ core, :, i * half : (i + 1) * half] = dpre
            da[...] += mm(dpre, ups[i * width : (i + 1) * width, lanes], ((1,), (1,)))
            return carry

        lax.fori_loop(0, 2, side, 0)
    grad, dg_ref[...] = pull_norm(h1_ref[...], g2_ref[...], da[...])
    dh_ref[...] = gz_ref[...].astype(f32) + grad
    for s in range(2):
        gz_out_ref[s ^ core] = dh_ref[:, s * half : (s + 1) * half].astype(bf)


def widen_back(core, gz, slope, h1, g2, big):
    f32, bf = jnp.float32, jnp.bfloat16
    slots, width = gz.shape
    vmem = pl.BlockSpec(memory_space=pltpu.VMEM)
    shape = jax.ShapeDtypeStruct
    return pl.pallas_call(
        widen_back_kernel,
        in_specs=[pl.BlockSpec(memory_space=pltpu.SMEM)] + [vmem] * 4 + [pl.BlockSpec(memory_space=pl.ANY)],
        out_specs=[vmem] * 4,
        out_shape=[
            shape((2, slots, 2 * width), bf),
            shape((slots, width), f32),
            shape((2, slots, width // 2), bf),
            shape((1, width), f32),
        ],
        scratch_shapes=[
            pltpu.VMEM((4 * width, width), bf),
            pltpu.VMEM((4 * width, width), bf),
            pltpu.VMEM((slots, width), f32),
            pltpu.SemaphoreType.DMA((8,)),
        ],
        compiler_params=pltpu.CompilerParams(vmem_limit_bytes=48 * 2**20),
        cost_estimate=pl.CostEstimate(flops=64 * 10**8, bytes_accessed=32 * 2**20, transcendentals=0),
    )(core, gz, slope, h1, g2.reshape(1, -1), big)


def attend_back_kernel(
    core_ref, dh_ref, h0_ref, g1_ref, joined_ref, tall_ref, wide_ref, big_ref, dj_ref, out_ref, dg_ref, mats, bias, dblend, dj, sems
):
    f32, bf = jnp.float32, jnp.bfloat16
    slots, width = dh_ref.shape
    head = width // HEADS
    half = width // 2
    tile = 512
    scaling = head ** (-0.5)
    core = core_ref[0]
    copies = []
    for n, i in enumerate((3, 0, 1, 2)):
        rows = pl.ds(i * width, width)
        copies.append(pltpu.make_async_copy(big_ref.at[rows], mats.at[rows], sems.at[n]))
        copies[-1].start()
    bias[...] = jnp.where(tall_ref[...] == wide_ref[...], 0.0, -jnp.inf)
    copies[0].wait()
    gz = dh_ref[...].astype(bf)
    for t in range(width // tile):
        rows = slice(3 * width + t * tile, 3 * width + (t + 1) * tile)
        dblend[:, t * tile : (t + 1) * tile] = mm(gz, mats[rows], ((1,), (1,))).astype(bf)

    def attend(h, carry):
        lanes = lambda i: pl.ds(pl.multiple_of(i * width + h * head, head), head)
        q, k, v = (joined_ref[:, lanes(i)] for i in range(3))
        do = dblend[:, pl.ds(pl.multiple_of(h * head, head), head)]
        scores = mm(q, k, ((1,), (1,))) * scaling + bias[...]
        weights = jnp.exp(scores - jnp.max(scores, axis=1, keepdims=True))
        chance = weights * (1.0 / jnp.sum(weights, axis=1, keepdims=True))
        dchance = mm(do, v, ((1,), (1,)))
        dot = jnp.sum(chance * dchance, axis=1, keepdims=True)
        ds = (chance * (dchance - dot)).astype(bf)
        parts = (
            mm(ds, k, ((1,), (0,))) * scaling,
            mm(ds, q, ((0,), (0,))) * scaling,
            mm(chance.astype(bf), do, ((0,), (0,))),
        )
        per_side = HEADS // 2
        for i in range(3):
            part = parts[i].astype(bf)
            dj[:, lanes(i)] = part
            dj_ref[(h // per_side) ^ core, :, pl.ds(pl.multiple_of(i * half + h % per_side * head, head), head)] = part
        return carry

    lax.fori_loop(0, HEADS, attend, 0)
    da = None
    for i in range(3):
        copies[1 + i].wait()
        term = mm(dj[:, i * width : (i + 1) * width], mats[i * width : (i + 1) * width], ((1,), (1,)))
        da = term if da is None else da + term
    grad, dg_ref[...] = pull_norm(h0_ref[...].astype(f32), g1_ref[...], da)
    out_ref[...] = dh_ref[...] + grad


def attend_back(core, dh, h0, g1, joined, labels, big):
    f32, bf = jnp.float32, jnp.bfloat16
    slots, width = dh.shape
    vmem = pl.BlockSpec(memory_space=pltpu.VMEM)
    shape = jax.ShapeDtypeStruct
    return pl.pallas_call(
        attend_back_kernel,
        in_specs=[pl.BlockSpec(memory_space=pltpu.SMEM)] + [vmem] * 6 + [pl.BlockSpec(memory_space=pl.ANY)],
        out_specs=[vmem] * 3,
        out_shape=[shape((2, slots, 3 * width // 2), bf), shape((slots, width), f32), shape((1, width), f32)],
        scratch_shapes=[
            pltpu.VMEM((4 * width, width), bf),
            pltpu.VMEM((slots, slots), f32),
            pltpu.VMEM((slots, width), bf),
            pltpu.VMEM((slots, 3 * width), bf),
            pltpu.SemaphoreType.DMA((4,)),
        ],
        compiler_params=pltpu.CompilerParams(vmem_limit_bytes=48 * 2**20),
        cost_estimate=pl.CostEstimate(flops=64 * 10**8, bytes_accessed=16 * 2**20, transcendentals=10**6),
    )(core, dh, h0, g1.reshape(1, -1), joined, labels.reshape(-1, 1), labels.reshape(1, -1), big)


CORE = 1


def send(v, bit):
    return lax.ppermute(v, "dev", [(d, d ^ bit) for d in range(32)])


def after(*values):
    return lax.optimization_barrier(values)


def chip_rows():
    table = []
    for chip in range(16):
        places = [placed(flat) for flat in range(chip * 768, chip * 768 + 768)]
        order = sorted(range(768), key=lambda i: places[i])
        place = [0] * 768
        for at, i in enumerate(order):
            place[i] = at
        table.append(place)
    return np.array(table, np.int32)


def sum_to_owners(blocks, device):
    f32, bf = jnp.float32, jnp.bfloat16
    core, chip = device % 2, device // 2
    half = blocks.shape[1] // 2
    block = lambda m: lax.dynamic_index_in_dim(blocks, chip ^ (m >> 1), 0, keepdims=False)
    total = lambda *parts: sum(part.astype(f32) for part in parts)
    both = lambda one, two: jnp.concatenate([one, two]).astype(bf)

    far = block(30)
    a, b = after(send(far[:half], 4), send(far[half:], 2))
    side, other, next_far = block(26), block(28), block(22)
    side = both(total(side[:half], a), side[half:])
    other = both(other[:half], total(other[half:], b))
    a, b, c = after(send(side, 8), send(other, 4), send(next_far, 2))

    far = block(14)
    over_x, over_y, across = total(block(18), a).astype(bf), total(block(20), c).astype(bf), total(block(24), b).astype(bf)
    a, b, c, d, e = after(send(far[:half], 4), send(far[half:], 2), send(over_x, 2), send(over_y, 4), send(across, 8))
    far = block(6)
    side, other = block(10), block(12)
    up_x = both(total(side[:half], a), side[half:])
    up_y = both(other[:half], total(other[half:], b))
    over = total(block(16), c, d, e).astype(bf)
    a, b, c, d, e = after(send(far[:half], 4), send(far[half:], 2), send(up_x, 2), send(up_y, 4), send(over, 16))
    side, other = block(2), block(4)
    own_x = both(total(side[:half], a), side[half:])
    own_y = both(other[:half], total(other[half:], b))
    up = total(block(8), c, d).astype(bf)
    own = total(block(0), e, send(own_x, 2), send(own_y, 4), send(up, 8))

    order = lax.dynamic_index_in_dim(jnp.asarray(chip_rows()), chip, 0, keepdims=False)
    own = jnp.take(own, order, axis=0)
    mine = lax.dynamic_slice_in_dim(own, core * half, half, 0)
    peer = send(lax.dynamic_slice_in_dim(own, (1 - core) * half, half, 0), CORE)
    return jnp.where(core == 0, jnp.concatenate([mine, peer], axis=1), jnp.concatenate([peer, mine], axis=1))


def fwd_mul(left, right):
    return mm(left, right, ((1,), (0,)))


def outer(left, right):
    return mm(left, right, ((0,), (0,)))


def backmul(upstream, weight):
    return mm(upstream, weight, ((1,), (1,)))


def norm_parts(inputs):
    center = inputs - jnp.mean(inputs, axis=-1, keepdims=True)
    root = lax.rsqrt(jnp.mean(center * center, axis=-1, keepdims=True) + norm_eps)
    return center * root, root


def norm_pull(hat, root, gain, upstream):
    dhat = upstream * gain
    inner = jnp.mean(dhat * hat, axis=-1, keepdims=True)
    grad = root * (dhat - jnp.mean(dhat, axis=-1, keepdims=True) - hat * inner)
    return grad, jnp.sum(upstream * hat, axis=0)


def running(values):
    number = jnp.arange(values.shape[0], dtype=jnp.int32)
    return jnp.sum(jnp.where(number[None, :] <= number[:, None], values[None, :], 0), axis=1)


def block_rates(position, feature, out_fan):
    cut_one = 3 * feature * feature
    cut_two = cut_one + feature * feature
    cut_three = cut_two + 4 * feature * feature
    fans = (feature, out_fan, feature, 4 * feature)
    rates = [0.5 * fan ** (-0.5) for fan in fans]
    return jnp.where(
        position < cut_one,
        rates[0],
        jnp.where(position < cut_two, rates[1], jnp.where(position < cut_three, rates[2], rates[3])),
    ).astype(jnp.float32)


def adam_update(weight, gradient, first, second, rates, decay):
    first_new = beta_one * first + (1.0 - beta_one) * gradient
    second_new = beta_two * second + (1.0 - beta_two) * gradient * gradient
    corrected = first_new / (1.0 - beta_one**STEP)
    scaled = second_new / (1.0 - beta_two**STEP)
    weight_new = weight - rates * (corrected / (jnp.sqrt(scaled) + adam_eps) + decay * weight)
    return (weight_new, first_new, second_new)


def local(
    cells_in, lengths, sets_weights, rows_weights, norm_gains, sets_first, rows_first, gains_first,
    sets_second, rows_second, gains_second, out_grad,
):
    f32, bf = jnp.float32, jnp.bfloat16
    devices = lax.axis_size("dev")
    device = lax.axis_index("dev")
    slots, width = cells_in.shape
    feat = width // ATTRS
    per_peer = slots // devices
    rows_even = out_grad.shape[0]
    rows_pad = -(-rows_even // LANES) * LANES
    grid = devices == 32 and width == 1024 and slots == 384

    n_rows, n_gains = rows_weights.shape[0], norm_gains.shape[0]
    small = jnp.concatenate([rows_weights, norm_gains]).astype(bf)
    small = jnp.pad(small, (0, -small.shape[0] % 1024)).reshape(-1, 1024)
    small = lax.all_gather(small, "dev", axis=0, tiled=False)
    shard = sets_weights.astype(bf).reshape(-1, width)
    if grid:
        orders, runs = shard_orders()
        order = lax.dynamic_index_in_dim(jnp.asarray(orders), device, 0, keepdims=False)
        hot = (order[:, None] == jnp.arange(shard.shape[0], dtype=jnp.int32)[None, :]).astype(bf)
        flat = lax.all_gather(fwd_mul(hot, shard).astype(bf), "dev", axis=0, tiled=True)
    else:
        flat = lax.all_gather(shard, "dev", axis=0, tiled=True)
        parts = lambda v, n: v.reshape(width, n, width).transpose(1, 0, 2).reshape(n * width, width)
        flat = jnp.concatenate(
            [parts(flat[: 3 * width], 3), flat[3 * width : 4 * width], parts(flat[4 * width : 8 * width], 4), flat[8 * width :]]
        )
        runs = [(i * width, i * width, width) for i in range(12)]
    small = small.reshape(devices, -1)
    full_rows = small[:, :n_rows].reshape(-1)
    full_gains = small[:, n_rows : n_rows + n_gains].reshape(-1).astype(f32)
    square = feat * feat
    wq2 = full_rows[: 3 * square].reshape(feat, 3 * feat)
    wo2 = full_rows[3 * square : 4 * square].reshape(feat, feat)
    wu2 = full_rows[4 * square : 8 * square].reshape(feat, 4 * feat)
    wd2 = full_rows[8 * square :].reshape(4 * feat, feat)
    g1, g2 = full_gains[:width], full_gains[width : 2 * width]
    g3, g4 = full_gains[2 * width : 2 * width + feat], full_gains[2 * width + feat :]

    table = lengths.reshape(devices, SETS_DEV)
    own = lax.dynamic_index_in_dim(table, device, 0, keepdims=False)
    positions = jnp.arange(slots, dtype=jnp.int32)
    labels = jnp.sum((positions[:, None] >= running(own)[None, :]).astype(jnp.int32), axis=1)
    counts = jnp.sum(table, axis=1) // devices
    ends = running(counts)
    spot = jnp.arange(rows_pad, dtype=jnp.int32)
    past = (ends[None, :] <= spot[:, None]).astype(jnp.int32)
    start = jnp.sum(past * counts[None, :], axis=1)
    pick = jnp.where(spot < rows_even, jnp.sum(past, axis=1) * per_peer + spot - start, -1)

    big, joined, a1, o1, a2, u1, slope, h1, leaving = forward_layer(runs, per_peer, cells_in, g1, g2, labels, flat)

    swap = lambda v: lax.all_to_all(v.reshape(devices, -1, width), "dev", split_axis=0, concat_axis=0, tiled=True)
    og = jnp.pad(out_grad, ((0, rows_pad - rows_even), (0, 0)))
    rows_out, back, dq2, do2, du2, dd2, dg3, dg4 = rows_layer(
        pick, swap(leaving).reshape(slots, width), og, wq2, wo2, wu2, wd2, g3, g4
    )
    rows_out = rows_out[:rows_even]
    gz = swap(back).transpose(1, 0, 2).reshape(slots, width)

    core = device % 2
    which = core.reshape(1)
    half = width // 2
    dpre, dh1, gz_out, dg2 = widen_back(which, gz, slope, h1, g2, big)
    dj, cells_grad, dg1 = attend_back(which, dh1, cells_in, g1, joined, labels, big)
    rows_flat = jnp.concatenate([v.reshape(-1) for v in (dq2, do2, du2, dd2)])
    if grid:
        gz_sides = [lax.dynamic_slice_in_dim(gz, side * half, half, 1) for side in (core, 1 - core)]

        def chip_outer(left, sides, part):
            lanes = slice(part * half, (part + 1) * half)
            return (outer(left[0], sides[0][:, lanes]) + outer(left[1], sides[1][:, lanes])).astype(bf)

        pair = lambda v: (v, send(v, CORE))
        dd1 = chip_outer(pair(u1), (gz_sides[0], send(gz_sides[1], CORE)), 0)
        sides, left = (dpre[0], send(dpre[1], CORE)), pair(a2)
        du1 = jnp.stack([chip_outer(left, sides, j) for j in range(4)])
        do1 = chip_outer(pair(o1), (gz_out[0], send(gz_out[1], CORE)), 0)
        sides, left = (dj[0], send(dj[1], CORE)), pair(a1)
        dq1 = jnp.stack([chip_outer(left, sides, j) for j in range(3)])
        tall = lambda lo, hi: du1[:, lo:hi].reshape(4 * (hi - lo), half)
        cuts = (0, 128, 320, 512, 704, 896, 1024)
        blocks = jnp.concatenate(
            [dq1.reshape(3, 4, -1, half).transpose(1, 0, 2, 3).reshape(3 * width, half), do1]
            + [tall(lo, hi) for lo, hi in zip(cuts[:-1], cuts[1:], strict=True)]
            + [dd1]
        )
        sets_grad = sum_to_owners(blocks.reshape(16, -1, half), device).reshape(-1)
    else:
        sides = lambda v, n: jnp.where(core == 0, v, v[::-1]).reshape(2, slots, n, half).transpose(1, 2, 0, 3).reshape(slots, -1)
        dq1, du1 = outer(a1, sides(dj, 3)), outer(a2, sides(dpre, 4))
        full = jnp.concatenate([dq1.reshape(-1, width), outer(o1, dh1.astype(bf)), du1.reshape(-1, width), outer(u1, gz)])
        sets_grad = lax.psum_scatter(full.astype(bf), "dev", scatter_dimension=0, tiled=True).astype(f32).reshape(-1)

    gains = jnp.concatenate([dg1[0], dg2[0], dg3, dg4]).reshape(devices, n_gains)
    extra = jnp.concatenate([rows_flat.reshape(devices, n_rows), gains], axis=1).reshape(devices, 1, -1)
    extra = jnp.sum(lax.all_to_all(extra, "dev", split_axis=0, concat_axis=0, tiled=True), axis=(0, 1))
    rows_grad, gains_grad = extra[:n_rows], extra[n_rows:]

    set_index = device * sets_grad.shape[0] + jnp.arange(sets_grad.shape[0], dtype=jnp.int32)
    row_index = device * n_rows + jnp.arange(n_rows, dtype=jnp.int32)
    set_rates = block_rates(set_index, width, max(1, 3 * width // slots))
    row_rates = block_rates(row_index, feat, max(1, feat // 8))
    sets_new, sets_first_new, sets_second_new = adam_update(
        sets_weights, sets_grad, sets_first, sets_second, set_rates, decay_rate
    )
    rows_new, rows_first_new, rows_second_new = adam_update(
        rows_weights, rows_grad, rows_first, rows_second, row_rates, decay_rate
    )
    gains_new, gains_first_new, gains_second_new = adam_update(
        norm_gains, gains_grad, gains_first, gains_second, gain_rate, 0.0
    )
    return (
        rows_out, cells_grad, sets_grad, rows_grad, gains_grad, sets_new, rows_new, gains_new,
        sets_first_new, rows_first_new, gains_first_new, sets_second_new, rows_second_new, gains_second_new,
        sets_new.astype(bf), rows_new.astype(bf), gains_new.astype(bf),
    )


def solution(mesh):
    flat = P("dev")
    tall = P("dev", None)
    return jax.shard_map(
        local,
        mesh=mesh,
        in_specs=(tall, P()) + (flat,) * 9 + (tall,),
        out_specs=(tall, tall) + (flat,) * 15,
        check_vma=False,
    )
```

```python
import functools

import jax
import jax.numpy as jnp
import numpy as np
from jax import lax
from jax.experimental import pallas as pl
from jax.experimental.pallas import tpu as pltpu
from jax.sharding import PartitionSpec as P

ATTRS = 16
HEADS = 8
SETS_DEV = 2
STEP = 5
LANES = 128

norm_eps = 1e-05
beta_one = 0.5
beta_two = 0.5
adam_eps = 1e-08
decay_rate = 0.1
gain_rate = 0.5


def mm(left, right, dims):
    return lax.dot_general(left, right, (dims, ((), ())), preferred_element_type=jnp.float32)


def gelu_pair(v):
    size = jnp.abs(v) * 0.7071067811865476
    t = 1.0 / (1.0 + 0.3275911 * size)
    bell = jnp.exp(-0.5 * v * v)
    poly = t * (0.254829592 + t * (-0.284496736 + t * (1.421413741 + t * (-1.453152027 + t * 1.061405429))))
    tail = 0.5 * poly * bell
    phi = jnp.where(v < 0.0, tail, 1.0 - tail)
    return v * phi, phi + v * (bell * 0.3989422804014327)


def rows_kernel(
    pick_ref, arrived_ref, og_ref, wq_ref, wqt_ref, wo_ref, wot_ref, wu_ref, wut_ref, wd_ref, wdt_ref, g3_ref, g4_ref,
    out_ref, back_ref, dwq_ref, dwo_ref, dwu_ref, dwd_ref, dg3_ref, dg4_ref,
    joined, prob, dscore, outs, douts, dj, back_acc,
):
    f32, bf = jnp.float32, jnp.bfloat16
    step = pl.program_id(0)
    last = pl.num_programs(0) - 1
    slots = arrived_ref.shape[0]
    scaling = HEADS ** (-0.5)
    feat = 64

    @pl.when(step == 0)
    def _():
        for ref in (dwq_ref, dwo_ref, dwu_ref, dwd_ref, dg3_ref, dg4_ref, back_acc):
            ref[...] = jnp.zeros_like(ref)

    source = lax.broadcasted_iota(jnp.int32, (slots, LANES), 0)
    hot = (source == pick_ref[0]).astype(f32).astype(bf)
    x_t = mm(arrived_ref[...], hot, ((0,), (0,)))

    def to_lanes(tall):
        return jnp.concatenate([tall[a * feat : (a + 1) * feat] for a in range(ATTRS)], axis=1)

    def to_tall(wide):
        return jnp.concatenate([wide[:, a * LANES : (a + 1) * LANES] for a in range(ATTRS)], axis=0)

    def norm(v):
        center = v - jnp.mean(v, axis=0, keepdims=True)
        root = lax.rsqrt(jnp.mean(center * center, axis=0, keepdims=True) + norm_eps)
        return center * root, root

    def norm_back(hat, root, gain, upstream):
        dhat = upstream * gain
        return root * (
            dhat - jnp.mean(dhat, axis=0, keepdims=True) - hat * jnp.mean(dhat * hat, axis=0, keepdims=True)
        )

    def fold(v):
        total = v[:, :LANES]
        for a in range(1, ATTRS):
            total = total + v[:, a * LANES : (a + 1) * LANES]
        return total

    x = to_lanes(x_t)
    g3, g4 = g3_ref[...], g4_ref[...]
    hat3, root3 = norm(x)
    a3 = (hat3 * g3).astype(bf)
    j_t = mm(wqt_ref[...], a3, ((1,), (0,))).astype(bf).astype(f32)
    for a in range(ATTRS):
        joined[a] = j_t[:, a * LANES : (a + 1) * LANES]

    def attend(a, carry):
        q = [joined[a, d * 8 : d * 8 + 8] * scaling for d in range(8)]
        scores = []
        for b in range(ATTRS):
            s = q[0] * joined[b, 64:72]
            for d in range(1, 8):
                s = s + q[d] * joined[b, 64 + d * 8 : 72 + d * 8]
            scores.append(s)
        peak = functools.reduce(jnp.maximum, scores)
        weights = [jnp.exp(s - peak) for s in scores]
        inverse = 1.0 / functools.reduce(jnp.add, weights)
        o = [None] * 8
        for b in range(ATTRS):
            p = weights[b] * inverse
            prob[a, b] = p
            p = p.astype(bf).astype(f32)
            for d in range(8):
                term = p * joined[b, 128 + d * 8 : 136 + d * 8]
                o[d] = term if b == 0 else o[d] + term
        for d in range(8):
            outs[a, d * 8 : d * 8 + 8] = o[d]
        return carry

    lax.fori_loop(0, ATTRS, attend, 0)
    o = jnp.concatenate([outs[a] for a in range(ATTRS)], axis=1).astype(bf)
    h3 = x + mm(wot_ref[...], o, ((1,), (0,)))
    hat4, root4 = norm(h3)
    a4 = (hat4 * g4).astype(bf)
    pre = mm(wut_ref[...], a4, ((1,), (0,)))
    active, slope = gelu_pair(pre)
    u = active.astype(bf)
    y = h3 + mm(wdt_ref[...], u, ((1,), (0,)))
    out_ref[...] = to_tall(y).T.astype(bf)

    grad = to_lanes(og_ref[...].astype(f32).T)
    gz = grad.astype(bf)
    dwd_ref[...] += mm(u, gz, ((1,), (1,)))
    dpre = (slope * mm(wd_ref[...], gz, ((1,), (0,)))).astype(bf)
    dwu_ref[...] += mm(a4, dpre, ((1,), (1,)))
    da4 = mm(wu_ref[...], dpre, ((1,), (0,)))
    dg4_ref[...] += fold(da4 * hat4)
    dh3 = grad + norm_back(hat4, root4, g4, da4)

    gz = dh3.astype(bf)
    dwo_ref[...] += mm(o, gz, ((1,), (1,)))
    do = mm(wo_ref[...], gz, ((1,), (0,))).astype(bf).astype(f32)
    for a in range(ATTRS):
        douts[a] = do[:, a * LANES : (a + 1) * LANES]

    def spread(a, carry):
        up = [douts[a, d * 8 : d * 8 + 8] for d in range(8)]
        dot = None
        slopes = []
        for b in range(ATTRS):
            s = up[0] * joined[b, 128:136]
            for d in range(1, 8):
                s = s + up[d] * joined[b, 128 + d * 8 : 136 + d * 8]
            slopes.append(s)
            term = prob[a, b] * s
            dot = term if b == 0 else dot + term
        dq = [None] * 8
        for b in range(ATTRS):
            ds = (prob[a, b] * (slopes[b] - dot)).astype(bf).astype(f32) * scaling
            dscore[a, b] = ds
            for d in range(8):
                term = ds * joined[b, 64 + d * 8 : 72 + d * 8]
                dq[d] = term if b == 0 else dq[d] + term
        for d in range(8):
            dj[a, d * 8 : d * 8 + 8] = dq[d]
        return carry

    lax.fori_loop(0, ATTRS, spread, 0)

    def collect(b, carry):
        dk, dv = [None] * 8, [None] * 8
        for a in range(ATTRS):
            ds = dscore[a, b]
            p = prob[a, b].astype(bf).astype(f32)
            for d in range(8):
                one = ds * joined[a, d * 8 : d * 8 + 8]
                two = p * douts[a, d * 8 : d * 8 + 8]
                dk[d] = one if a == 0 else dk[d] + one
                dv[d] = two if a == 0 else dv[d] + two
        for d in range(8):
            dj[b, 64 + d * 8 : 72 + d * 8] = dk[d]
            dj[b, 128 + d * 8 : 136 + d * 8] = dv[d]
        return carry

    lax.fori_loop(0, ATTRS, collect, 0)
    djl = jnp.concatenate([dj[a] for a in range(ATTRS)], axis=1).astype(bf)
    dwq_ref[...] += mm(a3, djl, ((1,), (1,)))
    da3 = mm(wq_ref[...], djl, ((1,), (0,)))
    dg3_ref[...] += fold(da3 * hat3)
    dhc = to_tall(dh3 + norm_back(hat3, root3, g3, da3)).astype(bf)
    back_acc[...] += mm(hot, dhc, ((1,), (1,)))

    @pl.when(step == last)
    def _():
        back_ref[...] = back_acc[...].astype(bf)


def rows_layer(pick, arrived, og, wq, wo, wu, wd, g3, g4):
    f32, bf = jnp.float32, jnp.bfloat16
    total, width = og.shape
    slots = arrived.shape[0]
    steps = total // LANES
    feat = 64
    wqp = wq.reshape(feat, 3, HEADS, 8).transpose(0, 1, 3, 2).reshape(feat, 3 * feat)
    wop = wo.reshape(HEADS, 8, feat).transpose(1, 0, 2).reshape(feat, feat)
    whole = lambda *shape: pl.BlockSpec(shape, lambda t: (0,) * len(shape))
    outs = pl.pallas_call(
        rows_kernel,
        grid=(steps,),
        in_specs=[
            pl.BlockSpec((1, 1, LANES), lambda t: (t, 0, 0)),
            whole(slots, width),
            pl.BlockSpec((LANES, width), lambda t: (t, 0)),
            whole(feat, 192), whole(192, feat), whole(feat, feat), whole(feat, feat),
            whole(feat, 256), whole(256, feat), whole(256, feat), whole(feat, 256),
            whole(feat, 1), whole(feat, 1),
        ],
        out_specs=[
            pl.BlockSpec((LANES, width), lambda t: (t, 0)),
            whole(slots, width),
            whole(feat, 192), whole(feat, feat), whole(feat, 256), whole(256, feat),
            whole(feat, LANES), whole(feat, LANES),
        ],
        out_shape=[
            jax.ShapeDtypeStruct((total, width), bf),
            jax.ShapeDtypeStruct((slots, width), bf),
            jax.ShapeDtypeStruct((feat, 192), f32),
            jax.ShapeDtypeStruct((feat, feat), f32),
            jax.ShapeDtypeStruct((feat, 256), f32),
            jax.ShapeDtypeStruct((256, feat), f32),
            jax.ShapeDtypeStruct((feat, LANES), f32),
            jax.ShapeDtypeStruct((feat, LANES), f32),
        ],
        scratch_shapes=[
            pltpu.VMEM((ATTRS, 192, LANES), f32),
            pltpu.VMEM((ATTRS, ATTRS, 8, LANES), f32),
            pltpu.VMEM((ATTRS, ATTRS, 8, LANES), f32),
            pltpu.VMEM((ATTRS, 64, LANES), f32),
            pltpu.VMEM((ATTRS, 64, LANES), f32),
            pltpu.VMEM((ATTRS, 192, LANES), f32),
            pltpu.VMEM((slots, width), f32),
        ],
        compiler_params=pltpu.CompilerParams(vmem_limit_bytes=56 * 2**20),
    )(
        pick.reshape(steps, 1, LANES), arrived, og,
        wqp, wqp.T, wop, wop.T, wu, wu.T, wd, wd.T, g3.reshape(feat, 1), g4.reshape(feat, 1),
    )
    return outs


def rows_order(dwqp, dwop):
    feat = dwop.shape[0]
    dwq = dwqp.reshape(feat, 3, 8, HEADS).transpose(0, 1, 3, 2).reshape(feat, 3 * feat)
    return dwq, dwop.reshape(8, HEADS, feat).transpose(1, 0, 2).reshape(feat, feat)


def placed(flat):
    if flat < 3072:
        return flat % 3 * 1024 + flat // 3
    if flat < 4096 or flat >= 8192:
        return flat
    return 4096 + flat % 4 * 1024 + (flat - 4096) // 4


def sorted_runs(per):
    orders, runs = [], []
    for first in range(0, 12288, per):
        places = [placed(first + i) for i in range(per)]
        order = sorted(range(per), key=lambda i: places[i])
        orders.append(order)
        for at, i in enumerate(order):
            if at and places[i] == runs[-1][1] + runs[-1][2] and places[i] % 1024:
                runs[-1][2] += 1
            else:
                runs.append([first + at, places[i], 1])
    return np.array(orders, np.int32), sorted((tuple(run) for run in runs), key=lambda run: run[1])


class Copies:
    def __init__(self, sems):
        self.sems, self.used = sems, 0

    def start(self, src, dst):
        copy = pltpu.make_async_copy(src, dst, self.sems.at[self.used])
        copy.start()
        self.used += 1
        return copy

    def rows(self, src, dst, parts=4):
        count = src.shape[0] // parts
        cuts = [pl.ds(i * count, count) for i in range(parts)]
        return [self.start(src.at[cut], dst.at[cut]) for cut in cuts]


def wait(copies):
    for copy in copies:
        copy.wait()


def load_mats(copies, runs, flat_ref, held, first, width):
    groups = [[] for _ in range(held.shape[0] // width)]
    for src, dst, rows in runs:
        i = dst // width - first
        if 0 <= i < len(groups):
            groups[i].append(copies.start(flat_ref.at[pl.ds(src, rows)], held.at[pl.ds(dst - first * width, rows)]))
    return groups


def low_norm(v, gain):
    center = v - jnp.mean(v, axis=1, keepdims=True)
    root = lax.rsqrt(jnp.mean(center * center, axis=1, keepdims=True) + norm_eps)
    return (center * root * gain).astype(jnp.bfloat16)


def pull_norm(v, gain, upstream):
    center = v - jnp.mean(v, axis=1, keepdims=True)
    root = lax.rsqrt(jnp.mean(center * center, axis=1, keepdims=True) + norm_eps)
    hat = center * root
    dhat = upstream * gain
    inner = jnp.mean(dhat * hat, axis=1, keepdims=True)
    grad = root * (dhat - jnp.mean(dhat, axis=1, keepdims=True) - hat * inner)
    return grad, jnp.sum(upstream * hat, axis=0, keepdims=True)


def forward_kernel(runs, turn, h0_ref, g1_ref, g2_ref, tall_ref, wide_ref, flat_ref,
                   joined_out, a1_out, o1_out, a2_out, u1_out, slope_out, h1_out, leave_out,
                   mats, bias, h0, joined, a1, o1, a2, u1, slope, h1, leave, load_sems, store_sems):
    f32, bf = jnp.float32, jnp.bfloat16
    slots, width = h0.shape
    head = width // HEADS
    tile = 512
    loads, stores = Copies(load_sems), Copies(store_sems)
    first = loads.rows(h0_ref, h0)
    groups = load_mats(loads, runs, flat_ref, mats, 0, width)
    saves = []
    bias[...] = jnp.where(tall_ref[...] == wide_ref[...], 0.0, -jnp.inf)
    wait(first)
    a1[...] = low_norm(h0[...].astype(f32), g1_ref[...])
    saves += stores.rows(a1, a1_out)
    for i in range(3):
        wait(groups[i])
        for t in range(width // tile):
            cols = slice(i * width + t * tile, i * width + (t + 1) * tile)
            joined[:, cols] = mm(a1[...], mats[i * width : (i + 1) * width, t * tile : (t + 1) * tile], ((1,), (0,))).astype(bf)
    saves += stores.rows(joined, joined_out)

    def attend(h, carry):
        part = lambda i: joined[:, pl.ds(pl.multiple_of(i * width + h * head, head), head)]
        scores = mm(part(0), part(1), ((1,), (1,))) * head ** (-0.5) + bias[...]
        weights = jnp.exp(scores - jnp.max(scores, axis=1, keepdims=True))
        chance = weights * (1.0 / jnp.sum(weights, axis=1, keepdims=True))
        o1[:, pl.ds(pl.multiple_of(h * head, head), head)] = mm(chance.astype(bf), part(2), ((1,), (0,))).astype(bf)
        return carry

    lax.fori_loop(0, HEADS, attend, 0, unroll=2)
    saves += stores.rows(o1, o1_out)
    wait(groups[3])
    for t in range(width // tile):
        cols = slice(t * tile, (t + 1) * tile)
        h1[:, cols] = h0[:, cols].astype(f32) + mm(o1[...], mats[3 * width : 4 * width, cols], ((1,), (0,)))
    saves += stores.rows(h1, h1_out)
    a2[...] = low_norm(h1[...], g2_ref[...])
    saves += stores.rows(a2, a2_out)
    for i in range(4):
        wait(groups[4 + i])
        for t in range(width // tile):
            cols = slice(t * tile, (t + 1) * tile)
            active, rise = gelu_pair(mm(a2[...], mats[(4 + i) * width : (5 + i) * width, cols], ((1,), (0,))))
            cols = slice(i * width + t * tile, i * width + (t + 1) * tile)
            u1[:, cols] = active.astype(bf)
            slope[:, cols] = rise.astype(bf)
            saves.append(stores.start(u1.at[:, cols], u1_out.at[:, cols]))
            saves.append(stores.start(slope.at[:, cols], slope_out.at[:, cols]))
    for i in range(4):
        wait(groups[8 + i])
    to, source = (lax.broadcasted_iota(jnp.int32, (slots, slots), axis) for axis in (0, 1))
    hot = (source == to % turn * (slots // turn) + to // turn).astype(f32).astype(bf)
    for t in range(width // tile):
        cols = slice(t * tile, (t + 1) * tile)
        h2 = (h1[:, cols] + mm(u1[...], mats[8 * width :, cols], ((1,), (0,)))).astype(bf)
        leave[:, cols] = mm(hot, h2, ((1,), (0,))).astype(bf)
        saves.append(stores.start(leave.at[:, cols], leave_out.at[:, cols]))
    wait(saves)


def own_kernel(kernel, operands, small, outs, scratch, limit, flops):
    def spec(v):
        space = pltpu.SMEM if v.ndim == 1 else pltpu.VMEM
        return pl.BlockSpec(memory_space=space)

    anywhere = pl.BlockSpec(memory_space=pl.ANY)
    tiny = pl.BlockSpec(memory_space=pltpu.VMEM)
    return pl.pallas_call(
        kernel,
        in_specs=[spec(v) if n in small else anywhere for n, v in enumerate(operands)],
        out_specs=[tiny if out.shape[0] == 1 else anywhere for out in outs],
        out_shape=outs,
        scratch_shapes=scratch,
        compiler_params=pltpu.CompilerParams(vmem_limit_bytes=limit * 2**20),
        cost_estimate=pl.CostEstimate(flops=flops, bytes_accessed=40 * 2**20, transcendentals=10**6),
    )(*operands)


def forward_layer(runs, turn, h0, g1, g2, labels, flat):
    f32, bf = jnp.float32, jnp.bfloat16
    slots, width = h0.shape
    shape, vmem = jax.ShapeDtypeStruct, pltpu.VMEM
    sizes = [(3, bf), (1, bf), (1, bf), (1, bf), (4, bf), (4, bf), (1, f32), (1, bf)]
    return own_kernel(
        functools.partial(forward_kernel, runs, turn),
        (h0, g1.reshape(1, -1), g2.reshape(1, -1), labels.reshape(-1, 1), labels.reshape(1, -1), flat),
        (1, 2, 3, 4),
        [shape((slots, n * width), kind) for n, kind in sizes],
        [vmem(flat.shape, bf), vmem((slots, slots), f32), vmem((slots, width), bf)]
        + [vmem((slots, n * width), kind) for n, kind in sizes]
        + [pltpu.SemaphoreType.DMA((len(runs) + 4,)), pltpu.SemaphoreType.DMA((38,))],
        60,
        10**10,
    )


def widen_back_kernel(runs, turn, core_ref, g2_ref, raw_ref, slope_ref, h1_ref, flat_ref,
                      dpre_own, dpre_peer, dh_out, low_own, low_peer, gz_own, gz_peer, dg_ref,
                      ups, downs, raw, gz, slope, h1, dpre, dh, low, gz_sides, da, load_sems, store_sems):
    f32, bf = jnp.float32, jnp.bfloat16
    width = gz.shape[1]
    half = width // 2
    core = core_ref[0]
    loads, stores = Copies(load_sems), Copies(store_sems)
    raw_copies = loads.rows(raw_ref, raw)
    down_copies = load_mats(loads, runs, flat_ref, downs, 8, width)
    slope_copies = [
        loads.start(slope_ref.at[:, pl.ds(i * width, width)], slope.at[:, pl.ds(i * width, width)]) for i in range(4)
    ]
    up_copies = load_mats(loads, runs, flat_ref, ups, 4, width)
    h1_copies = loads.rows(h1_ref, h1)
    wait(raw_copies)
    slots = gz.shape[0]
    slot, source = (lax.broadcasted_iota(jnp.int32, (slots, slots), axis) for axis in (0, 1))
    devices = slots // turn
    hot = (source == slot % devices * turn + slot // devices).astype(f32).astype(bf)
    gz[...] = mm(hot, raw[...], ((1,), (0,))).astype(bf)
    saves = []
    for s in range(2):
        gz_sides[s ^ core] = gz[:, s * half : (s + 1) * half]
    saves += [stores.start(gz_sides.at[0], gz_own), stores.start(gz_sides.at[1], gz_peer)]
    for i in range(4):
        wait(down_copies[i] + [slope_copies[i]] + up_copies[i])
        for s in range(2):
            hidden = slice(i * width + s * half, i * width + (s + 1) * half)
            du = mm(gz[...], downs[hidden], ((1,), (1,)))
            piece = (slope[:, hidden].astype(f32) * du).astype(bf)
            dpre[s ^ core, :, i * half : (i + 1) * half] = piece
            term = mm(piece, ups[i * width : (i + 1) * width, s * half : (s + 1) * half], ((1,), (1,)))
            da[...] = term if i == s == 0 else da[...] + term
        lanes = pl.ds(i * half, half)
        saves += [stores.start(dpre.at[0, :, lanes], dpre_own.at[:, lanes]), stores.start(dpre.at[1, :, lanes], dpre_peer.at[:, lanes])]
    wait(h1_copies)
    grad, dg_ref[...] = pull_norm(h1[...], g2_ref[...], da[...])
    dh[...] = gz[...].astype(f32) + grad
    saves += stores.rows(dh, dh_out)
    for s in range(2):
        low[s ^ core] = dh[:, s * half : (s + 1) * half].astype(bf)
    saves += [stores.start(low.at[0], low_own), stores.start(low.at[1], low_peer)]
    wait(saves)


def widen_back(runs, turn, core, raw, slope, h1, g2, flat):
    f32, bf = jnp.float32, jnp.bfloat16
    slots, width = raw.shape
    half = width // 2
    shape, vmem = jax.ShapeDtypeStruct, pltpu.VMEM
    side = shape((slots, half), bf)
    ups = sum(4 <= dst // width < 12 for _, dst, _ in runs)
    return own_kernel(
        functools.partial(widen_back_kernel, runs, turn),
        (core, g2.reshape(1, -1), raw, slope, h1, flat),
        (0, 1),
        [shape((slots, 2 * width), bf)] * 2 + [shape((slots, width), f32)] + [side] * 4 + [shape((1, width), f32)],
        [
            vmem((4 * width, width), bf), vmem((4 * width, width), bf), vmem((slots, width), bf), vmem((slots, width), bf),
            vmem((slots, 4 * width), bf),
            vmem((slots, width), f32), vmem((2, slots, 2 * width), bf), vmem((slots, width), f32), vmem((2, slots, half), bf),
            vmem((2, slots, half), bf), vmem((slots, width), f32),
            pltpu.SemaphoreType.DMA((ups + 12,)), pltpu.SemaphoreType.DMA((16,)),
        ],
        60,
        64 * 10**8,
    )


def attend_back_kernel(runs, core_ref, g1_ref, tall_ref, wide_ref, dh_ref, h0_ref, joined_ref, flat_ref,
                       own_out, peer_out, grad_out, dg_ref,
                       mats, bias, dh, h0, joined, dblend, dj, sides, load_sems, store_sems):
    f32, bf = jnp.float32, jnp.bfloat16
    slots, width = dh.shape
    head = width // HEADS
    half = width // 2
    tile = 512
    scaling = head ** (-0.5)
    core = core_ref[0]
    loads, stores = Copies(load_sems), Copies(store_sems)
    dh_copies = loads.rows(dh_ref, dh)
    out_copies = load_mats(loads, runs, flat_ref, mats.at[pl.ds(3 * width, width)], 3, width)
    joined_copies = loads.rows(joined_ref, joined)
    mat_copies = load_mats(loads, runs, flat_ref, mats.at[pl.ds(0, 3 * width)], 0, width)
    h0_copies = loads.rows(h0_ref, h0)
    bias[...] = jnp.where(tall_ref[...] == wide_ref[...], 0.0, -jnp.inf)
    wait(dh_copies)
    gz = dh[...].astype(bf)
    wait(out_copies[0])
    for t in range(width // tile):
        rows = slice(3 * width + t * tile, 3 * width + (t + 1) * tile)
        dblend[:, t * tile : (t + 1) * tile] = mm(gz, mats[rows], ((1,), (1,))).astype(bf)
    wait(joined_copies)

    def attend(h, carry):
        lanes = lambda i: pl.ds(pl.multiple_of(i * width + h * head, head), head)
        q, k, v = (joined[:, lanes(i)] for i in range(3))
        do = dblend[:, pl.ds(pl.multiple_of(h * head, head), head)]
        scores = mm(q, k, ((1,), (1,))) * scaling + bias[...]
        weights = jnp.exp(scores - jnp.max(scores, axis=1, keepdims=True))
        chance = weights * (1.0 / jnp.sum(weights, axis=1, keepdims=True))
        dchance = mm(do, v, ((1,), (1,)))
        dot = jnp.sum(chance * dchance, axis=1, keepdims=True)
        ds = (chance * (dchance - dot)).astype(bf)
        parts = (
            mm(ds, k, ((1,), (0,))) * scaling,
            mm(ds, q, ((0,), (0,))) * scaling,
            mm(chance.astype(bf), do, ((0,), (0,))),
        )
        per_side = HEADS // 2
        for i in range(3):
            part = parts[i].astype(bf)
            dj[:, lanes(i)] = part
            sides[(h // per_side) ^ core, :, pl.ds(pl.multiple_of(i * half + h % per_side * head, head), head)] = part
        return carry

    lax.fori_loop(0, HEADS, attend, 0, unroll=2)
    saves = [stores.start(sides.at[1], peer_out), stores.start(sides.at[0], own_out)]
    da = None
    for i in range(3):
        wait(mat_copies[i])
        term = mm(dj[:, i * width : (i + 1) * width], mats[i * width : (i + 1) * width], ((1,), (1,)))
        da = term if da is None else da + term
    wait(h0_copies)
    grad, dg_ref[...] = pull_norm(h0[...].astype(f32), g1_ref[...], da)
    dh[...] = dh[...] + grad
    wait(saves + stores.rows(dh, grad_out))


def attend_back(runs, core, dh, h0, g1, joined, labels, flat):
    f32, bf = jnp.float32, jnp.bfloat16
    slots, width = dh.shape
    shape, vmem = jax.ShapeDtypeStruct, pltpu.VMEM
    mats = sum(dst // width < 4 for _, dst, _ in runs)
    return own_kernel(
        functools.partial(attend_back_kernel, runs),
        (core, g1.reshape(1, -1), labels.reshape(-1, 1), labels.reshape(1, -1), dh, h0, joined, flat),
        (0, 1, 2, 3),
        [shape((slots, 3 * width // 2), bf)] * 2 + [shape((slots, width), f32), shape((1, width), f32)],
        [
            vmem((4 * width, width), bf), vmem((slots, slots), f32), vmem((slots, width), f32), vmem((slots, width), bf),
            vmem((slots, 3 * width), bf), vmem((slots, width), bf), vmem((slots, 3 * width), bf),
            vmem((2, slots, 3 * width // 2), bf),
            pltpu.SemaphoreType.DMA((mats + 12,)), pltpu.SemaphoreType.DMA((6,)),
        ],
        60,
        64 * 10**8,
    )


def chip_outer_kernel(runs, jobs, shift, *refs):
    bf = jnp.bfloat16
    count = 4 * len(jobs)
    operands, out, held = refs[:count], refs[count], refs[count + 1 : 2 * count + 1]
    result, load_sems, store_sems = refs[2 * count + 1 :]
    loads, stores = Copies(load_sems), Copies(store_sems)
    arrivals = [loads.rows(ref, v, 2) for ref, v in zip(operands, held, strict=True)]
    width, lanes_out = 1024, result.shape[1]
    half, tile = width // 2, 512
    saves, done = [], 0
    for n, (first, matrices, tall) in enumerate(jobs):
        left, left_peer, right, right_peer = held[4 * n : 4 * n + 4]
        for copies in arrivals[4 * n : 4 * n + 4]:
            wait(copies)
        for i in range(matrices):
            from_lane = (0 if tall else i * half) + shift
            lanes = slice(from_lane, from_lane + lanes_out)
            for t in range(width // tile):
                cols = (i if tall else 0) * width + t * tile
                cols = slice(cols, cols + tile)
                term = mm(left[:, cols], right[:, lanes], ((0,), (0,))) + mm(left_peer[:, cols], right_peer[:, lanes], ((0,), (0,)))
                result[done * width + t * tile : done * width + (t + 1) * tile, :] = term.astype(bf)
            for to, place, rows in runs:
                if place // width == first + i:
                    part = result.at[pl.ds(done * width + place % width, rows)]
                    saves.append(stores.start(part, out.at[pl.ds(to, rows)]))
            done += 1
    wait(saves)


def chip_outer(runs, jobs, operands, shift, lanes):
    bf = jnp.bfloat16
    anywhere = pl.BlockSpec(memory_space=pl.ANY)
    return pl.pallas_call(
        functools.partial(chip_outer_kernel, runs, jobs, shift),
        in_specs=[anywhere] * len(operands),
        out_specs=anywhere,
        out_shape=jax.ShapeDtypeStruct((12288, lanes), bf),
        scratch_shapes=[pltpu.VMEM(v.shape, bf) for v in operands]
        + [
            pltpu.VMEM((12288, lanes), bf),
            pltpu.SemaphoreType.DMA((2 * len(operands),)),
            pltpu.SemaphoreType.DMA((len(runs),)),
        ],
        compiler_params=pltpu.CompilerParams(vmem_limit_bytes=60 * 2**20),
        cost_estimate=pl.CostEstimate(flops=6 * 10**9, bytes_accessed=24 * 2**20, transcendentals=0),
    )(*operands)


CORE = 1


def send(v, bit):
    return lax.ppermute(v, "dev", [(d, d ^ bit) for d in range(32)])


def after(*values):
    return lax.optimization_barrier(values)


def sum_blocks(blocks, chip):
    f32, bf = jnp.float32, jnp.bfloat16
    half = blocks.shape[1] // 2
    block = lambda m: lax.dynamic_index_in_dim(blocks, chip ^ (m >> 1), 0, keepdims=False)
    total = lambda *parts: sum(part.astype(f32) for part in parts)
    both = lambda one, two: jnp.concatenate([one.astype(bf), two.astype(bf)])

    across_far, up_far, across = block(30), block(14), block(24)
    a, b, c, d, e = after(
        send(across_far[:half], 4), send(across_far[half:], 2), send(across, 8), send(up_far[:half], 4), send(up_far[half:], 2)
    )
    side, other = block(26), block(28)
    across_x, across_y = both(total(side[:half], a), side[half:]), both(other[:half], total(other[half:], b))
    side, other = block(10), block(12)
    up_x, up_y = both(total(side[:half], d), side[half:]), both(other[:half], total(other[half:], e))
    over = total(block(16), c)

    a, b, c = after(send(across_x, 8), send(up_x, 2), send(up_y, 4))
    over_x, up = total(block(18), a), total(block(8), b, c).astype(bf)
    over_far, own_far = block(22), block(6)
    a, b, c, d, e = after(
        send(across_y, 8), send(over_far[:half], 4), send(over_far[half:], 2), send(own_far[:half], 4), send(own_far[half:], 2)
    )
    other = total(block(20), a)
    over_x, over_y = both(total(over_x[:half], b), over_x[half:]), both(other[:half], total(other[half:], c))
    side, other = block(2), block(4)
    own_x, own_y = both(total(side[:half], d), side[half:]), both(other[:half], total(other[half:], e))

    a, b, c = after(send(over_x, 2), send(over_y, 4), send(up, 8))
    own = total(block(0), c)
    over = total(over, a, b).astype(bf)
    return total(own, send(over, 16), send(own_x, 2), send(own_y, 4))


def owned_rows(own, device):
    core, chip = device % 2, device // 2
    half = own.shape[0] // 2
    orders, _ = sorted_runs(2 * half)
    order = lax.dynamic_index_in_dim(jnp.asarray(np.argsort(orders, axis=1).astype(np.int32)), chip, 0, keepdims=False)
    own = jnp.take(own, order, axis=0)
    mine = lax.dynamic_slice_in_dim(own, core * half, half, 0)
    peer = send(lax.dynamic_slice_in_dim(own, (1 - core) * half, half, 0), CORE)
    return jnp.where(core == 0, jnp.concatenate([mine, peer], axis=1), jnp.concatenate([peer, mine], axis=1))


def fwd_mul(left, right):
    return mm(left, right, ((1,), (0,)))


def outer(left, right):
    return mm(left, right, ((0,), (0,)))


def running(values):
    number = jnp.arange(values.shape[0], dtype=jnp.int32)
    return jnp.sum(jnp.where(number[None, :] <= number[:, None], values[None, :], 0), axis=1)


def block_rates(position, feature, out_fan):
    cut_one = 3 * feature * feature
    cut_two = cut_one + feature * feature
    cut_three = cut_two + 4 * feature * feature
    fans = (feature, out_fan, feature, 4 * feature)
    rates = [0.5 * fan ** (-0.5) for fan in fans]
    return jnp.where(
        position < cut_one,
        rates[0],
        jnp.where(position < cut_two, rates[1], jnp.where(position < cut_three, rates[2], rates[3])),
    ).astype(jnp.float32)


def adam_update(weight, gradient, first, second, rates, decay):
    first_new = beta_one * first + (1.0 - beta_one) * gradient
    second_new = beta_two * second + (1.0 - beta_two) * gradient * gradient
    corrected = first_new / (1.0 - beta_one**STEP)
    scaled = second_new / (1.0 - beta_two**STEP)
    weight_new = weight - rates * (corrected / (jnp.sqrt(scaled) + adam_eps) + decay * weight)
    return (weight_new, first_new, second_new)


def local(
    cells_in, lengths, sets_weights, rows_weights, norm_gains, sets_first, rows_first, gains_first,
    sets_second, rows_second, gains_second, out_grad,
):
    f32, bf = jnp.float32, jnp.bfloat16
    devices = lax.axis_size("dev")
    device = lax.axis_index("dev")
    slots, width = cells_in.shape
    feat = width // ATTRS
    per_peer = slots // devices
    rows_even = out_grad.shape[0]
    rows_pad = -(-rows_even // LANES) * LANES
    grid = devices == 32 and width == 1024 and slots == 384

    n_rows, n_gains = rows_weights.shape[0], norm_gains.shape[0]
    small = jnp.concatenate([rows_weights, norm_gains]).astype(bf)
    small = jnp.pad(small, (0, -small.shape[0] % 1024)).reshape(-1, 1024)
    small = lax.all_gather(small, "dev", axis=0, tiled=False)
    shard = sets_weights.astype(bf).reshape(-1, width)
    if grid:
        orders, runs = sorted_runs(shard.shape[0])
        order = lax.dynamic_index_in_dim(jnp.asarray(orders), device, 0, keepdims=False)
        hot = (order[:, None] == jnp.arange(shard.shape[0], dtype=jnp.int32)[None, :]).astype(bf)
        flat = lax.all_gather(fwd_mul(hot, shard).astype(bf), "dev", axis=0, tiled=True)
    else:
        flat = lax.all_gather(shard, "dev", axis=0, tiled=True)
        parts = lambda v, n: v.reshape(width, n, width).transpose(1, 0, 2).reshape(n * width, width)
        flat = jnp.concatenate(
            [parts(flat[: 3 * width], 3), flat[3 * width : 4 * width], parts(flat[4 * width : 8 * width], 4), flat[8 * width :]]
        )
        runs = [(i * width, i * width, width) for i in range(12)]
    small = small.reshape(devices, -1)
    full_rows = small[:, :n_rows].reshape(-1)
    full_gains = small[:, n_rows : n_rows + n_gains].reshape(-1).astype(f32)
    square = feat * feat
    wq2 = full_rows[: 3 * square].reshape(feat, 3 * feat)
    wo2 = full_rows[3 * square : 4 * square].reshape(feat, feat)
    wu2 = full_rows[4 * square : 8 * square].reshape(feat, 4 * feat)
    wd2 = full_rows[8 * square :].reshape(4 * feat, feat)
    g1, g2 = full_gains[:width], full_gains[width : 2 * width]
    g3, g4 = full_gains[2 * width : 2 * width + feat], full_gains[2 * width + feat :]

    table = lengths.reshape(devices, SETS_DEV)
    own = lax.dynamic_index_in_dim(table, device, 0, keepdims=False)
    positions = jnp.arange(slots, dtype=jnp.int32)
    labels = jnp.sum((positions[:, None] >= running(own)[None, :]).astype(jnp.int32), axis=1)
    counts = jnp.sum(table, axis=1) // devices
    ends = running(counts)
    spot = jnp.arange(rows_pad, dtype=jnp.int32)
    past = (ends[None, :] <= spot[:, None]).astype(jnp.int32)
    start = jnp.sum(past * counts[None, :], axis=1)
    pick = jnp.where(spot < rows_even, jnp.sum(past, axis=1) * per_peer + spot - start, -1)

    joined, a1, o1, a2, u1, slope, h1, leaving = forward_layer(runs, per_peer, cells_in, g1, g2, labels, flat)

    swap = lambda v: lax.all_to_all(
        v.reshape(devices, -1, LANES), "dev", split_axis=0, concat_axis=0, tiled=True
    ).reshape(slots, width)
    og = jnp.pad(out_grad, ((0, rows_pad - rows_even), (0, 0)))
    rows_out, back, dq2, do2, du2, dd2, dg3, dg4 = rows_layer(
        pick, swap(leaving), og, wq2, wo2, wu2, wd2, g3, g4
    )
    rows_out = rows_out[:rows_even]
    raw = swap(back)

    core = device % 2
    which = core.reshape(1)
    half = width // 2
    pair = lambda v: (v, send(v, CORE))
    if grid:
        raw, *pairs = after(raw, *pair(u1), *pair(a2), *pair(o1), *pair(a1))
        u1, a2, o1, a1 = (tuple(pairs[i : i + 2]) for i in (0, 2, 4, 6))
    *dpre, dh1, low_own, low_peer, gz_own, gz_peer, dg2 = widen_back(runs, per_peer, which, raw, slope, h1, g2, flat)
    *dj, cells_grad, dg1 = attend_back(runs, which, dh1, cells_in, g1, joined, labels, flat)
    if grid:
        chip_runs = sorted_runs(2 * shard.shape[0])[1]
        swapped = lambda own, peer: (own, send(peer, CORE))
        operands = u1 + swapped(gz_own, gz_peer) + a2 + swapped(*dpre) + o1 + swapped(low_own, low_peer)
        operands = operands + a1 + swapped(*dj)
        jobs = ((8, 4, True), (4, 4, False), (3, 1, True), (0, 3, False))
        lanes = half // 2
        blocks = [chip_outer(chip_runs, jobs, operands, shift, lanes).reshape(16, -1, lanes) for shift in (0, lanes)]
        blocks[0], dq2, do2, du2, dd2, dg3, dg4 = after(blocks[0], dq2, do2, du2, dd2, dg3, dg4)
        sums = [sum_blocks(part, device // 2) for part in blocks]
        sets_grad = owned_rows(jnp.concatenate(sums, axis=1), device).reshape(-1)
    else:

        def sides(own, peer, n):
            both = jnp.where(core == 0, jnp.stack([own, peer]), jnp.stack([peer, own]))
            return both.reshape(2, slots, n, half).transpose(1, 2, 0, 3).reshape(slots, -1)

        dq1, du1 = outer(a1, sides(*dj, 3)), outer(a2, sides(*dpre, 4))
        gz = sides(gz_own, gz_peer, 1)
        full = jnp.concatenate([dq1.reshape(-1, width), outer(o1, dh1.astype(bf)), du1.reshape(-1, width), outer(u1, gz)])
        sets_grad = lax.psum_scatter(full.astype(bf), "dev", scatter_dimension=0, tiled=True).astype(f32).reshape(-1)

    rows_flat = jnp.concatenate([v.reshape(-1) for v in (*rows_order(dq2, do2), du2, dd2)])
    dg3, dg4 = jnp.sum(dg3, axis=1), jnp.sum(dg4, axis=1)
    gains = jnp.concatenate([dg1[0], dg2[0], dg3, dg4]).reshape(devices, n_gains)
    extra = jnp.concatenate([rows_flat.reshape(devices, n_rows), gains], axis=1).reshape(devices, 1, -1)
    extra = jnp.sum(lax.all_to_all(extra, "dev", split_axis=0, concat_axis=0, tiled=True), axis=(0, 1))
    rows_grad, gains_grad = extra[:n_rows], extra[n_rows:]

    set_index = device * sets_grad.shape[0] + jnp.arange(sets_grad.shape[0], dtype=jnp.int32)
    row_index = device * n_rows + jnp.arange(n_rows, dtype=jnp.int32)
    set_rates = block_rates(set_index, width, max(1, 3 * width // slots))
    row_rates = block_rates(row_index, feat, max(1, feat // 8))
    sets_new, sets_first_new, sets_second_new = adam_update(
        sets_weights, sets_grad, sets_first, sets_second, set_rates, decay_rate
    )
    rows_new, rows_first_new, rows_second_new = adam_update(
        rows_weights, rows_grad, rows_first, rows_second, row_rates, decay_rate
    )
    gains_new, gains_first_new, gains_second_new = adam_update(
        norm_gains, gains_grad, gains_first, gains_second, gain_rate, 0.0
    )
    return (
        rows_out, cells_grad, sets_grad, rows_grad, gains_grad, sets_new, rows_new, gains_new,
        sets_first_new, rows_first_new, gains_first_new, sets_second_new, rows_second_new, gains_second_new,
        sets_new.astype(bf), rows_new.astype(bf), gains_new.astype(bf),
    )


def solution(mesh):
    flat = P("dev")
    tall = P("dev", None)
    return jax.shard_map(
        local,
        mesh=mesh,
        in_specs=(tall, P()) + (flat,) * 9 + (tall,),
        out_specs=(tall, tall) + (flat,) * 15,
        check_vma=False,
    )
```

```python
import functools

import jax
import jax.numpy as jnp
import numpy as np
from jax import lax
from jax.experimental import pallas as pl
from jax.experimental.pallas import tpu as pltpu
from jax.sharding import PartitionSpec as P

ATTRS = 16
HEADS = 8
SETS_DEV = 2
STEP = 5
LANES = 128

norm_eps = 1e-05
beta_one = 0.5
beta_two = 0.5
adam_eps = 1e-08
decay_rate = 0.1
gain_rate = 0.5


def mm(left, right, dims):
    return lax.dot_general(left, right, (dims, ((), ())), preferred_element_type=jnp.float32)


def gelu_pair(v):
    size = jnp.abs(v) * 0.7071067811865476
    t = 1.0 / (1.0 + 0.3275911 * size)
    bell = jnp.exp(-0.5 * v * v)
    poly = t * (0.254829592 + t * (-0.284496736 + t * (1.421413741 + t * (-1.453152027 + t * 1.061405429))))
    tail = 0.5 * poly * bell
    phi = jnp.where(v < 0.0, tail, 1.0 - tail)
    return v * phi, phi + v * (bell * 0.3989422804014327)


def rows_kernel(
    pick_ref, arrived_ref, og_ref, wq_ref, wqt_ref, wo_ref, wot_ref, wu_ref, wut_ref, wd_ref, wdt_ref, g3_ref, g4_ref,
    out_ref, back_ref, dwq_ref, dwo_ref, dwu_ref, dwd_ref, dg3_ref, dg4_ref,
    joined, prob, dscore, outs, douts, dj, back_acc,
):
    f32, bf = jnp.float32, jnp.bfloat16
    step = pl.program_id(0)
    last = pl.num_programs(0) - 1
    slots = arrived_ref.shape[0]
    scaling = HEADS ** (-0.5)
    feat = 64

    @pl.when(step == 0)
    def _():
        for ref in (dwq_ref, dwo_ref, dwu_ref, dwd_ref, dg3_ref, dg4_ref, back_acc):
            ref[...] = jnp.zeros_like(ref)

    source = lax.broadcasted_iota(jnp.int32, (slots, LANES), 0)
    hot = (source == pick_ref[0]).astype(f32).astype(bf)
    x_t = mm(arrived_ref[...], hot, ((0,), (0,)))

    def to_lanes(tall):
        return jnp.concatenate([tall[a * feat : (a + 1) * feat] for a in range(ATTRS)], axis=1)

    def to_tall(wide):
        return jnp.concatenate([wide[:, a * LANES : (a + 1) * LANES] for a in range(ATTRS)], axis=0)

    def norm(v):
        center = v - jnp.mean(v, axis=0, keepdims=True)
        root = lax.rsqrt(jnp.mean(center * center, axis=0, keepdims=True) + norm_eps)
        return center * root, root

    def norm_back(hat, root, gain, upstream):
        dhat = upstream * gain
        return root * (
            dhat - jnp.mean(dhat, axis=0, keepdims=True) - hat * jnp.mean(dhat * hat, axis=0, keepdims=True)
        )

    def fold(v):
        total = v[:, :LANES]
        for a in range(1, ATTRS):
            total = total + v[:, a * LANES : (a + 1) * LANES]
        return total

    x = to_lanes(x_t)
    g3, g4 = g3_ref[...], g4_ref[...]
    hat3, root3 = norm(x)
    a3 = (hat3 * g3).astype(bf)
    j_t = mm(wqt_ref[...], a3, ((1,), (0,))).astype(bf).astype(f32)
    for a in range(ATTRS):
        joined[a] = j_t[:, a * LANES : (a + 1) * LANES]

    def attend(a, carry):
        q = [joined[a, d * 8 : d * 8 + 8] * scaling for d in range(8)]
        scores = []
        for b in range(ATTRS):
            s = q[0] * joined[b, 64:72]
            for d in range(1, 8):
                s = s + q[d] * joined[b, 64 + d * 8 : 72 + d * 8]
            scores.append(s)
        peak = functools.reduce(jnp.maximum, scores)
        weights = [jnp.exp(s - peak) for s in scores]
        inverse = 1.0 / functools.reduce(jnp.add, weights)
        o = [None] * 8
        for b in range(ATTRS):
            p = weights[b] * inverse
            prob[a, b] = p
            p = p.astype(bf).astype(f32)
            for d in range(8):
                term = p * joined[b, 128 + d * 8 : 136 + d * 8]
                o[d] = term if b == 0 else o[d] + term
        for d in range(8):
            outs[a, d * 8 : d * 8 + 8] = o[d]
        return carry

    lax.fori_loop(0, ATTRS, attend, 0)
    o = jnp.concatenate([outs[a] for a in range(ATTRS)], axis=1).astype(bf)
    h3 = x + mm(wot_ref[...], o, ((1,), (0,)))
    hat4, root4 = norm(h3)
    a4 = (hat4 * g4).astype(bf)
    pre = mm(wut_ref[...], a4, ((1,), (0,)))
    active, slope = gelu_pair(pre)
    u = active.astype(bf)
    y = h3 + mm(wdt_ref[...], u, ((1,), (0,)))
    out_ref[...] = to_tall(y).T.astype(bf)

    grad = to_lanes(og_ref[...].astype(f32).T)
    gz = grad.astype(bf)
    dwd_ref[...] += mm(u, gz, ((1,), (1,)))
    dpre = (slope * mm(wd_ref[...], gz, ((1,), (0,)))).astype(bf)
    dwu_ref[...] += mm(a4, dpre, ((1,), (1,)))
    da4 = mm(wu_ref[...], dpre, ((1,), (0,)))
    dg4_ref[...] += fold(da4 * hat4)
    dh3 = grad + norm_back(hat4, root4, g4, da4)

    gz = dh3.astype(bf)
    dwo_ref[...] += mm(o, gz, ((1,), (1,)))
    do = mm(wo_ref[...], gz, ((1,), (0,))).astype(bf).astype(f32)
    for a in range(ATTRS):
        douts[a] = do[:, a * LANES : (a + 1) * LANES]

    def spread(a, carry):
        up = [douts[a, d * 8 : d * 8 + 8] for d in range(8)]
        dot = None
        slopes = []
        for b in range(ATTRS):
            s = up[0] * joined[b, 128:136]
            for d in range(1, 8):
                s = s + up[d] * joined[b, 128 + d * 8 : 136 + d * 8]
            slopes.append(s)
            term = prob[a, b] * s
            dot = term if b == 0 else dot + term
        dq = [None] * 8
        for b in range(ATTRS):
            ds = (prob[a, b] * (slopes[b] - dot)).astype(bf).astype(f32) * scaling
            dscore[a, b] = ds
            for d in range(8):
                term = ds * joined[b, 64 + d * 8 : 72 + d * 8]
                dq[d] = term if b == 0 else dq[d] + term
        for d in range(8):
            dj[a, d * 8 : d * 8 + 8] = dq[d]
        return carry

    lax.fori_loop(0, ATTRS, spread, 0)

    def collect(b, carry):
        dk, dv = [None] * 8, [None] * 8
        for a in range(ATTRS):
            ds = dscore[a, b]
            p = prob[a, b].astype(bf).astype(f32)
            for d in range(8):
                one = ds * joined[a, d * 8 : d * 8 + 8]
                two = p * douts[a, d * 8 : d * 8 + 8]
                dk[d] = one if a == 0 else dk[d] + one
                dv[d] = two if a == 0 else dv[d] + two
        for d in range(8):
            dj[b, 64 + d * 8 : 72 + d * 8] = dk[d]
            dj[b, 128 + d * 8 : 136 + d * 8] = dv[d]
        return carry

    lax.fori_loop(0, ATTRS, collect, 0)
    djl = jnp.concatenate([dj[a] for a in range(ATTRS)], axis=1).astype(bf)
    dwq_ref[...] += mm(a3, djl, ((1,), (1,)))
    da3 = mm(wq_ref[...], djl, ((1,), (0,)))
    dg3_ref[...] += fold(da3 * hat3)
    dhc = to_tall(dh3 + norm_back(hat3, root3, g3, da3)).astype(bf)
    back_acc[...] += mm(hot, dhc, ((1,), (1,)))

    @pl.when(step == last)
    def _():
        back_ref[...] = back_acc[...].astype(bf)


def rows_layer(pick, arrived, og, wq, wo, wu, wd, g3, g4):
    f32, bf = jnp.float32, jnp.bfloat16
    total, width = og.shape
    slots = arrived.shape[0]
    steps = total // LANES
    feat = 64
    wqp = wq.reshape(feat, 3, HEADS, 8).transpose(0, 1, 3, 2).reshape(feat, 3 * feat)
    wop = wo.reshape(HEADS, 8, feat).transpose(1, 0, 2).reshape(feat, feat)
    whole = lambda *shape: pl.BlockSpec(shape, lambda t: (0,) * len(shape))
    outs = pl.pallas_call(
        rows_kernel,
        grid=(steps,),
        in_specs=[
            pl.BlockSpec((1, 1, LANES), lambda t: (t, 0, 0)),
            whole(slots, width),
            pl.BlockSpec((LANES, width), lambda t: (t, 0)),
            whole(feat, 192), whole(192, feat), whole(feat, feat), whole(feat, feat),
            whole(feat, 256), whole(256, feat), whole(256, feat), whole(feat, 256),
            whole(feat, 1), whole(feat, 1),
        ],
        out_specs=[
            pl.BlockSpec((LANES, width), lambda t: (t, 0)),
            whole(slots, width),
            whole(feat, 192), whole(feat, feat), whole(feat, 256), whole(256, feat),
            whole(feat, LANES), whole(feat, LANES),
        ],
        out_shape=[
            jax.ShapeDtypeStruct((total, width), bf),
            jax.ShapeDtypeStruct((slots, width), bf),
            jax.ShapeDtypeStruct((feat, 192), f32),
            jax.ShapeDtypeStruct((feat, feat), f32),
            jax.ShapeDtypeStruct((feat, 256), f32),
            jax.ShapeDtypeStruct((256, feat), f32),
            jax.ShapeDtypeStruct((feat, LANES), f32),
            jax.ShapeDtypeStruct((feat, LANES), f32),
        ],
        scratch_shapes=[
            pltpu.VMEM((ATTRS, 192, LANES), f32),
            pltpu.VMEM((ATTRS, ATTRS, 8, LANES), f32),
            pltpu.VMEM((ATTRS, ATTRS, 8, LANES), f32),
            pltpu.VMEM((ATTRS, 64, LANES), f32),
            pltpu.VMEM((ATTRS, 64, LANES), f32),
            pltpu.VMEM((ATTRS, 192, LANES), f32),
            pltpu.VMEM((slots, width), f32),
        ],
        compiler_params=pltpu.CompilerParams(vmem_limit_bytes=56 * 2**20),
    )(
        pick.reshape(steps, 1, LANES), arrived, og,
        wqp, wqp.T, wop, wop.T, wu, wu.T, wd, wd.T, g3.reshape(feat, 1), g4.reshape(feat, 1),
    )
    return outs


def rows_order(dwqp, dwop):
    feat = dwop.shape[0]
    dwq = dwqp.reshape(feat, 3, 8, HEADS).transpose(0, 1, 3, 2).reshape(feat, 3 * feat)
    return dwq, dwop.reshape(8, HEADS, feat).transpose(1, 0, 2).reshape(feat, feat)


UNIT = 32


def placed(flat):
    if flat < 3072:
        return flat % 3 * 1024 + flat // 3
    if flat < 4096 or flat >= 8192:
        return flat
    return 4096 + flat % 4 * 1024 + (flat - 4096) // 4


def sorted_runs(per):
    orders, runs = [], []
    for first in range(0, 12288, per):
        places = [placed(first + i) for i in range(per)]
        order = sorted(range(per), key=lambda i: places[i])
        orders.append(order)
        for at, i in enumerate(order):
            if at and places[i] == runs[-1][1] + runs[-1][2] and places[i] % 1024:
                runs[-1][2] += 1
            else:
                runs.append([first + at, places[i], 1])
    return np.array(orders, np.int32), sorted((tuple(run) for run in runs), key=lambda run: run[1])


class Copies:
    def __init__(self, sems):
        self.sems, self.used = sems, 0

    def start(self, src, dst):
        copy = pltpu.make_async_copy(src, dst, self.sems.at[self.used])
        copy.start()
        self.used += 1
        return copy

    def rows(self, src, dst, parts=4):
        count = src.shape[0] // parts
        cuts = [pl.ds(i * count, count) for i in range(parts)]
        return [self.start(src.at[cut], dst.at[cut]) for cut in cuts]


def wait(copies):
    for copy in copies:
        copy.wait()


def load_mats(copies, runs, flat_ref, held, first, width):
    groups = [[] for _ in range(held.shape[0] // width)]
    for src, dst, rows in runs:
        i = dst // width - first
        if 0 <= i < len(groups):
            groups[i].append(copies.start(flat_ref.at[pl.ds(src, rows)], held.at[pl.ds(dst - first * width, rows)]))
    return groups


def low_norm(v, gain):
    center = v - jnp.mean(v, axis=1, keepdims=True)
    root = lax.rsqrt(jnp.mean(center * center, axis=1, keepdims=True) + norm_eps)
    return (center * root * gain).astype(jnp.bfloat16)


def pull_norm(v, gain, upstream):
    center = v - jnp.mean(v, axis=1, keepdims=True)
    root = lax.rsqrt(jnp.mean(center * center, axis=1, keepdims=True) + norm_eps)
    hat = center * root
    dhat = upstream * gain
    inner = jnp.mean(dhat * hat, axis=1, keepdims=True)
    grad = root * (dhat - jnp.mean(dhat, axis=1, keepdims=True) - hat * inner)
    return grad, jnp.sum(upstream * hat, axis=0, keepdims=True)


def forward_kernel(counts, turn, plane_ref, dest_ref, g1_ref, g2_ref, tall_ref, wide_ref, h0_ref, *refs):
    stages = []
    for count in counts:
        stages.append(refs[:count])
        refs = refs[count:]
    forward_body(turn, plane_ref, dest_ref, g1_ref, g2_ref, tall_ref, wide_ref, h0_ref, stages, *refs)


def forward_body(turn, plane_ref, dest_ref, g1_ref, g2_ref, tall_ref, wide_ref, h0_ref, stages,
                   big_out, joined_out, a1_out, o1_out, a2_out, u1_out, slope_out, h1_out, leave_out,
                   mats, bias, h0, joined, a1, o1, a2, u1, slope, h1, leave, load_sems, plane_sems, store_sems):
    f32, bf = jnp.float32, jnp.bfloat16
    slots, width = h0.shape
    head = width // HEADS
    tile = 512
    loads, stores = Copies(load_sems), Copies(store_sems)
    first = loads.rows(h0_ref, h0)
    part = mats.shape[0] // len(stages)

    def load_stage(s, plane):
        number = sum(piece.shape[0] for pieces in stages[:s] for piece in pieces) // UNIT
        for piece in stages[s]:
            for u in range(piece.shape[0] // UNIT):
                place = pl.multiple_of(dest_ref[number] * UNIT, UNIT)
                number += 1
                pltpu.make_async_copy(
                    piece.at[pl.ds(u * UNIT, UNIT)], mats.at[pl.ds(place, UNIT)], plane_sems.at[plane]
                ).start()

    for plane in range(len(stages)):
        for s in range(len(stages)):
            pl.when(plane_ref[0] ^ s == plane)(functools.partial(load_stage, s, plane))

    def arrived(plane):
        rows = mats.at[pl.ds(plane * part, part)]
        pltpu.make_async_copy(rows, rows, plane_sems.at[plane]).wait()

    saves = []
    bias[...] = jnp.where(tall_ref[...] == wide_ref[...], 0.0, -jnp.inf)
    wait(first)
    a1[...] = low_norm(h0[...].astype(f32), g1_ref[...])
    saves += stores.rows(a1, a1_out)
    for plane in range(len(stages) if len(stages) < 4 else 1):
        arrived(plane)
    for i in range(3):
        for t in range(width // tile):
            cols = slice(i * width + t * tile, i * width + (t + 1) * tile)
            joined[:, cols] = mm(a1[...], mats[i * width : (i + 1) * width, t * tile : (t + 1) * tile], ((1,), (0,))).astype(bf)
    saves += stores.rows(joined, joined_out)
    saves += stores.rows(mats.at[pl.ds(0, 3 * width)], big_out.at[pl.ds(0, 3 * width)], 3)

    def attend(h, carry):
        part = lambda i: joined[:, pl.ds(pl.multiple_of(i * width + h * head, head), head)]
        scores = mm(part(0), part(1), ((1,), (1,))) * head ** (-0.5) + bias[...]
        weights = jnp.exp(scores - jnp.max(scores, axis=1, keepdims=True))
        chance = weights * (1.0 / jnp.sum(weights, axis=1, keepdims=True))
        o1[:, pl.ds(pl.multiple_of(h * head, head), head)] = mm(chance.astype(bf), part(2), ((1,), (0,))).astype(bf)
        return carry

    lax.fori_loop(0, HEADS, attend, 0, unroll=2)
    saves += stores.rows(o1, o1_out)
    if len(stages) == 4:
        arrived(1)
    for t in range(width // tile):
        cols = slice(t * tile, (t + 1) * tile)
        h1[:, cols] = h0[:, cols].astype(f32) + mm(o1[...], mats[3 * width : 4 * width, cols], ((1,), (0,)))
    saves += stores.rows(h1, h1_out)
    a2[...] = low_norm(h1[...], g2_ref[...])
    saves += stores.rows(a2, a2_out)
    if len(stages) == 4:
        arrived(2)
    for i in range(4):
        for t in range(width // tile):
            cols = slice(t * tile, (t + 1) * tile)
            active, rise = gelu_pair(mm(a2[...], mats[(4 + i) * width : (5 + i) * width, cols], ((1,), (0,))))
            cols = slice(i * width + t * tile, i * width + (t + 1) * tile)
            u1[:, cols] = active.astype(bf)
            slope[:, cols] = rise.astype(bf)
            saves.append(stores.start(u1.at[:, cols], u1_out.at[:, cols]))
            saves.append(stores.start(slope.at[:, cols], slope_out.at[:, cols]))
    if len(stages) == 4:
        arrived(3)
    saves += stores.rows(mats.at[pl.ds(3 * width, 9 * width)], big_out.at[pl.ds(3 * width, 9 * width)], 9)
    to, source = (lax.broadcasted_iota(jnp.int32, (slots, slots), axis) for axis in (0, 1))
    hot = (source == to % turn * (slots // turn) + to // turn).astype(f32).astype(bf)
    for t in range(width // tile):
        cols = slice(t * tile, (t + 1) * tile)
        h2 = (h1[:, cols] + mm(u1[...], mats[8 * width :, cols], ((1,), (0,)))).astype(bf)
        leave[:, cols] = mm(hot, h2, ((1,), (0,))).astype(bf)
        saves.append(stores.start(leave.at[:, cols], leave_out.at[:, cols]))
    wait(saves)


def own_kernel(kernel, operands, small, outs, scratch, limit, flops):
    def spec(v):
        space = pltpu.SMEM if v.ndim == 1 else pltpu.VMEM
        return pl.BlockSpec(memory_space=space)

    anywhere = pl.BlockSpec(memory_space=pl.ANY)
    tiny = pl.BlockSpec(memory_space=pltpu.VMEM)
    return pl.pallas_call(
        kernel,
        in_specs=[spec(v) if n in small else anywhere for n, v in enumerate(operands)],
        out_specs=[tiny if out.shape[0] == 1 else anywhere for out in outs],
        out_shape=outs,
        scratch_shapes=scratch,
        compiler_params=pltpu.CompilerParams(vmem_limit_bytes=limit * 2**20),
        cost_estimate=pl.CostEstimate(flops=flops, bytes_accessed=40 * 2**20, transcendentals=10**6),
    )(*operands)


def forward_layer(turn, h0, g1, g2, labels, plane, stages, dest):
    f32, bf = jnp.float32, jnp.bfloat16
    slots, width = h0.shape
    shape, vmem = jax.ShapeDtypeStruct, pltpu.VMEM
    sizes = [(3, bf), (1, bf), (1, bf), (1, bf), (4, bf), (4, bf), (1, f32), (1, bf)]
    mats = (12 * width, width)
    return own_kernel(
        functools.partial(forward_kernel, tuple(len(pieces) for pieces in stages), turn),
        (plane, dest, g1.reshape(1, -1), g2.reshape(1, -1), labels.reshape(-1, 1), labels.reshape(1, -1), h0, *sum(stages, ())),
        (0, 1, 2, 3, 4, 5),
        [shape(mats, bf)] + [shape((slots, n * width), kind) for n, kind in sizes],
        [vmem(mats, bf), vmem((slots, slots), f32), vmem((slots, width), bf)]
        + [vmem((slots, n * width), kind) for n, kind in sizes]
        + [pltpu.SemaphoreType.DMA((4,)), pltpu.SemaphoreType.DMA((len(stages),)), pltpu.SemaphoreType.DMA((50,))],
        60,
        10**10,
    )


def widen_back_kernel(runs, turn, core_ref, g2_ref, raw_ref, slope_ref, h1_ref, flat_ref,
                      dpre_own, dpre_peer, dh_out, low_own, low_peer, gz_own, gz_peer, dg_ref,
                      ups, downs, raw, gz, slope, h1, dpre, dh, low, gz_sides, da, load_sems, store_sems):
    f32, bf = jnp.float32, jnp.bfloat16
    width = gz.shape[1]
    half = width // 2
    core = core_ref[0]
    loads, stores = Copies(load_sems), Copies(store_sems)
    raw_copies = loads.rows(raw_ref, raw)
    down_copies = load_mats(loads, runs, flat_ref, downs, 8, width)
    slope_copies = [
        loads.start(slope_ref.at[:, pl.ds(i * width, width)], slope.at[:, pl.ds(i * width, width)]) for i in range(4)
    ]
    up_copies = load_mats(loads, runs, flat_ref, ups, 4, width)
    h1_copies = loads.rows(h1_ref, h1)
    wait(raw_copies)
    slots = gz.shape[0]
    slot, source = (lax.broadcasted_iota(jnp.int32, (slots, slots), axis) for axis in (0, 1))
    devices = slots // turn
    hot = (source == slot % devices * turn + slot // devices).astype(f32).astype(bf)
    gz[...] = mm(hot, raw[...], ((1,), (0,))).astype(bf)
    saves = []
    for s in range(2):
        gz_sides[s ^ core] = gz[:, s * half : (s + 1) * half]
    saves += [stores.start(gz_sides.at[0], gz_own), stores.start(gz_sides.at[1], gz_peer)]
    for i in range(4):
        wait(down_copies[i] + [slope_copies[i]] + up_copies[i])
        for s in range(2):
            hidden = slice(i * width + s * half, i * width + (s + 1) * half)
            du = mm(gz[...], downs[hidden], ((1,), (1,)))
            piece = (slope[:, hidden].astype(f32) * du).astype(bf)
            dpre[s ^ core, :, i * half : (i + 1) * half] = piece
            term = mm(piece, ups[i * width : (i + 1) * width, s * half : (s + 1) * half], ((1,), (1,)))
            da[...] = term if i == s == 0 else da[...] + term
        lanes = pl.ds(i * half, half)
        saves += [stores.start(dpre.at[0, :, lanes], dpre_own.at[:, lanes]), stores.start(dpre.at[1, :, lanes], dpre_peer.at[:, lanes])]
    wait(h1_copies)
    grad, dg_ref[...] = pull_norm(h1[...], g2_ref[...], da[...])
    dh[...] = gz[...].astype(f32) + grad
    saves += stores.rows(dh, dh_out)
    for s in range(2):
        low[s ^ core] = dh[:, s * half : (s + 1) * half].astype(bf)
    saves += [stores.start(low.at[0], low_own), stores.start(low.at[1], low_peer)]
    wait(saves)


def widen_back(runs, turn, core, raw, slope, h1, g2, flat):
    f32, bf = jnp.float32, jnp.bfloat16
    slots, width = raw.shape
    half = width // 2
    shape, vmem = jax.ShapeDtypeStruct, pltpu.VMEM
    side = shape((slots, half), bf)
    ups = sum(4 <= dst // width < 12 for _, dst, _ in runs)
    return own_kernel(
        functools.partial(widen_back_kernel, runs, turn),
        (core, g2.reshape(1, -1), raw, slope, h1, flat),
        (0, 1),
        [shape((slots, 2 * width), bf)] * 2 + [shape((slots, width), f32)] + [side] * 4 + [shape((1, width), f32)],
        [
            vmem((4 * width, width), bf), vmem((4 * width, width), bf), vmem((slots, width), bf), vmem((slots, width), bf),
            vmem((slots, 4 * width), bf),
            vmem((slots, width), f32), vmem((2, slots, 2 * width), bf), vmem((slots, width), f32), vmem((2, slots, half), bf),
            vmem((2, slots, half), bf), vmem((slots, width), f32),
            pltpu.SemaphoreType.DMA((ups + 12,)), pltpu.SemaphoreType.DMA((16,)),
        ],
        60,
        64 * 10**8,
    )


def attend_back_kernel(runs, core_ref, g1_ref, tall_ref, wide_ref, dh_ref, h0_ref, joined_ref, flat_ref,
                       own_out, peer_out, grad_out, dg_ref,
                       mats, bias, dh, h0, joined, dblend, dj, sides, load_sems, store_sems):
    f32, bf = jnp.float32, jnp.bfloat16
    slots, width = dh.shape
    head = width // HEADS
    half = width // 2
    tile = 512
    scaling = head ** (-0.5)
    core = core_ref[0]
    loads, stores = Copies(load_sems), Copies(store_sems)
    dh_copies = loads.rows(dh_ref, dh)
    out_copies = load_mats(loads, runs, flat_ref, mats.at[pl.ds(3 * width, width)], 3, width)
    joined_copies = loads.rows(joined_ref, joined)
    mat_copies = load_mats(loads, runs, flat_ref, mats.at[pl.ds(0, 3 * width)], 0, width)
    h0_copies = loads.rows(h0_ref, h0)
    bias[...] = jnp.where(tall_ref[...] == wide_ref[...], 0.0, -jnp.inf)
    wait(dh_copies)
    gz = dh[...].astype(bf)
    wait(out_copies[0])
    for t in range(width // tile):
        rows = slice(3 * width + t * tile, 3 * width + (t + 1) * tile)
        dblend[:, t * tile : (t + 1) * tile] = mm(gz, mats[rows], ((1,), (1,))).astype(bf)
    wait(joined_copies)

    def attend(h, carry):
        lanes = lambda i: pl.ds(pl.multiple_of(i * width + h * head, head), head)
        q, k, v = (joined[:, lanes(i)] for i in range(3))
        do = dblend[:, pl.ds(pl.multiple_of(h * head, head), head)]
        scores = mm(q, k, ((1,), (1,))) * scaling + bias[...]
        weights = jnp.exp(scores - jnp.max(scores, axis=1, keepdims=True))
        chance = weights * (1.0 / jnp.sum(weights, axis=1, keepdims=True))
        dchance = mm(do, v, ((1,), (1,)))
        dot = jnp.sum(chance * dchance, axis=1, keepdims=True)
        ds = (chance * (dchance - dot)).astype(bf)
        parts = (
            mm(ds, k, ((1,), (0,))) * scaling,
            mm(ds, q, ((0,), (0,))) * scaling,
            mm(chance.astype(bf), do, ((0,), (0,))),
        )
        per_side = HEADS // 2
        for i in range(3):
            part = parts[i].astype(bf)
            dj[:, lanes(i)] = part
            sides[(h // per_side) ^ core, :, pl.ds(pl.multiple_of(i * half + h % per_side * head, head), head)] = part
        return carry

    lax.fori_loop(0, HEADS, attend, 0, unroll=2)
    saves = [stores.start(sides.at[1], peer_out), stores.start(sides.at[0], own_out)]
    da = None
    for i in range(3):
        wait(mat_copies[i])
        term = mm(dj[:, i * width : (i + 1) * width], mats[i * width : (i + 1) * width], ((1,), (1,)))
        da = term if da is None else da + term
    wait(h0_copies)
    grad, dg_ref[...] = pull_norm(h0[...].astype(f32), g1_ref[...], da)
    dh[...] = dh[...] + grad
    wait(saves + stores.rows(dh, grad_out))


def attend_back(runs, core, dh, h0, g1, joined, labels, flat):
    f32, bf = jnp.float32, jnp.bfloat16
    slots, width = dh.shape
    shape, vmem = jax.ShapeDtypeStruct, pltpu.VMEM
    mats = sum(dst // width < 4 for _, dst, _ in runs)
    return own_kernel(
        functools.partial(attend_back_kernel, runs),
        (core, g1.reshape(1, -1), labels.reshape(-1, 1), labels.reshape(1, -1), dh, h0, joined, flat),
        (0, 1, 2, 3),
        [shape((slots, 3 * width // 2), bf)] * 2 + [shape((slots, width), f32), shape((1, width), f32)],
        [
            vmem((4 * width, width), bf), vmem((slots, slots), f32), vmem((slots, width), f32), vmem((slots, width), bf),
            vmem((slots, 3 * width), bf), vmem((slots, width), bf), vmem((slots, 3 * width), bf),
            vmem((2, slots, 3 * width // 2), bf),
            pltpu.SemaphoreType.DMA((mats + 12,)), pltpu.SemaphoreType.DMA((6,)),
        ],
        60,
        64 * 10**8,
    )


def chip_outer_kernel(runs, jobs, shift, *refs):
    bf = jnp.bfloat16
    count = 4 * len(jobs)
    operands, out, held = refs[:count], refs[count], refs[count + 1 : 2 * count + 1]
    result, load_sems, store_sems = refs[2 * count + 1 :]
    loads, stores = Copies(load_sems), Copies(store_sems)
    arrivals = [loads.rows(ref, v, 2) for ref, v in zip(operands, held, strict=True)]
    width, lanes_out = 1024, result.shape[1]
    half, tile = width // 2, 512
    saves, done = [], 0
    for n, (first, matrices, tall) in enumerate(jobs):
        left, left_peer, right, right_peer = held[4 * n : 4 * n + 4]
        for copies in arrivals[4 * n : 4 * n + 4]:
            wait(copies)
        for i in range(matrices):
            from_lane = (0 if tall else i * half) + shift
            lanes = slice(from_lane, from_lane + lanes_out)
            for t in range(width // tile):
                cols = (i if tall else 0) * width + t * tile
                cols = slice(cols, cols + tile)
                term = mm(left[:, cols], right[:, lanes], ((0,), (0,))) + mm(left_peer[:, cols], right_peer[:, lanes], ((0,), (0,)))
                result[done * width + t * tile : done * width + (t + 1) * tile, :] = term.astype(bf)
            for to, place, rows in runs:
                if place // width == first + i:
                    part = result.at[pl.ds(done * width + place % width, rows)]
                    saves.append(stores.start(part, out.at[pl.ds(to, rows)]))
            done += 1
    wait(saves)


def chip_outer(runs, jobs, operands, shift, lanes):
    bf = jnp.bfloat16
    anywhere = pl.BlockSpec(memory_space=pl.ANY)
    return pl.pallas_call(
        functools.partial(chip_outer_kernel, runs, jobs, shift),
        in_specs=[anywhere] * len(operands),
        out_specs=anywhere,
        out_shape=jax.ShapeDtypeStruct((12288, lanes), bf),
        scratch_shapes=[pltpu.VMEM(v.shape, bf) for v in operands]
        + [
            pltpu.VMEM((12288, lanes), bf),
            pltpu.SemaphoreType.DMA((2 * len(operands),)),
            pltpu.SemaphoreType.DMA((len(runs),)),
        ],
        compiler_params=pltpu.CompilerParams(vmem_limit_bytes=60 * 2**20),
        cost_estimate=pl.CostEstimate(flops=6 * 10**9, bytes_accessed=24 * 2**20, transcendentals=0),
    )(*operands)


CORE = 1


def send(v, bit):
    return lax.ppermute(v, "dev", [(d, d ^ bit) for d in range(32)])


def after(*values):
    return lax.optimization_barrier(values)


def sum_blocks(blocks, chip):
    f32, bf = jnp.float32, jnp.bfloat16
    half = blocks.shape[1] // 2
    block = lambda m: lax.dynamic_index_in_dim(blocks, chip ^ (m >> 1), 0, keepdims=False)
    total = lambda *parts: sum(part.astype(f32) for part in parts)
    both = lambda one, two: jnp.concatenate([one.astype(bf), two.astype(bf)])

    across_far, up_far, across = block(30), block(14), block(24)
    a, b, c, d, e = after(
        send(across_far[:half], 4), send(across_far[half:], 2), send(across, 8), send(up_far[:half], 4), send(up_far[half:], 2)
    )
    side, other = block(26), block(28)
    across_x, across_y = both(total(side[:half], a), side[half:]), both(other[:half], total(other[half:], b))
    side, other = block(10), block(12)
    up_x, up_y = both(total(side[:half], d), side[half:]), both(other[:half], total(other[half:], e))
    over = total(block(16), c)

    a, b, c = after(send(across_x, 8), send(up_x, 2), send(up_y, 4))
    over_x, up = total(block(18), a), total(block(8), b, c).astype(bf)
    over_far, own_far = block(22), block(6)
    a, b, c, d, e = after(
        send(across_y, 8), send(over_far[:half], 4), send(over_far[half:], 2), send(own_far[:half], 4), send(own_far[half:], 2)
    )
    other = total(block(20), a)
    over_x, over_y = both(total(over_x[:half], b), over_x[half:]), both(other[:half], total(other[half:], c))
    side, other = block(2), block(4)
    own_x, own_y = both(total(side[:half], d), side[half:]), both(other[:half], total(other[half:], e))

    a, b, c = after(send(over_x, 2), send(over_y, 4), send(up, 8))
    own = total(block(0), c)
    over = total(over, a, b).astype(bf)
    return total(own, send(over, 16), send(own_x, 2), send(own_y, 4))


def owned_rows(own, device):
    core, chip = device % 2, device // 2
    half = own.shape[0] // 2
    orders, _ = sorted_runs(2 * half)
    order = lax.dynamic_index_in_dim(jnp.asarray(np.argsort(orders, axis=1).astype(np.int32)), chip, 0, keepdims=False)
    own = jnp.take(own, order, axis=0)
    mine = lax.dynamic_slice_in_dim(own, core * half, half, 0)
    peer = send(lax.dynamic_slice_in_dim(own, (1 - core) * half, half, 0), CORE)
    return jnp.where(core == 0, jnp.concatenate([mine, peer], axis=1), jnp.concatenate([peer, mine], axis=1))


def gather_all(shard, small, device):
    per = shard.shape[0]
    half, extra = per // 2, small.shape[0]
    orders, runs = sorted_runs(per)
    order = lax.dynamic_index_in_dim(jnp.asarray(orders), device, 0, keepdims=False)
    hot = (order[:, None] == jnp.arange(per, dtype=jnp.int32)[None, :]).astype(jnp.bfloat16)
    own = jnp.concatenate([fwd_mul(hot, shard).astype(jnp.bfloat16), small])
    table = np.zeros((32 * per // UNIT,), np.int32)
    for src, dst, rows in runs:
        table[src // UNIT : (src + rows) // UNIT] = range(dst // UNIT, (dst + rows) // UNIT)
    by_mask = jnp.take(jnp.asarray(table.reshape(32, -1)), device ^ jnp.arange(32, dtype=jnp.int32), axis=0)
    stack = lambda *parts: jnp.concatenate([part[:per] for part in parts])

    own, own_x, own_y, up = after(own, send(own, 2), send(own, 4), send(own, 8))
    a, b, up_x, up_y, over = after(
        send(own_x[:half], 4), send(own_y[half:], 2), send(up, 2), send(up, 4), send(own, 16)
    )
    own_far = jnp.concatenate([a, b])
    own_stack = stack(own, own_x, own_y, own_far)
    a, b, over_x, over_y, across, own_stack = after(
        send(up_x[:half], 4), send(up_y[half:], 2), send(over, 2), send(over, 4), send(over, 8), own_stack
    )
    up_far = jnp.concatenate([a, b])
    up_stack = stack(up, up_x, up_y, up_far)
    over_far, across_x, across_y, own_peer, up_peer = after(
        send(over_y, 2), send(over_x, 8), send(across, 4), send(own_stack, CORE), send(up_stack, CORE)
    )
    a, b, over_far = after(across_x[:half], across_y[half:], over_far)
    over_stack, across_stack = stack(over, over_x, over_y, over_far), stack(across, across_x, across_y)
    a, b, over_peer, across_peer = after(send(a, 4), send(b, 2), send(over_stack, CORE), send(across_stack, CORE))
    plane = (own, own_x, own_y, own_far, up, up_x, up_y, up_far, over, over_x, over_y, over_far, across, across_x, across_y)
    small = jnp.concatenate([v[per:] for v in plane] + [b[per - half :]])
    last = (a, b[: per - half])
    last_peer, small_peer = tuple(send(v, CORE) for v in last), send(small, CORE)
    stages = (
        (own_stack, own_peer), (up_stack, up_peer), (over_stack, over_peer), (across_stack, across_peer, *last, *last_peer)
    )
    masks = [z + m + c for z in (0, 8, 16) for c in (0, 1) for m in (0, 2, 4, 6)] + [24, 26, 28, 25, 27, 29, 30, 31]
    dest = jnp.concatenate([by_mask[m] for m in masks])
    small = jnp.stack([small.reshape(16, -1), small_peer.reshape(16, -1)], axis=1).reshape(32, -1)
    number = jnp.arange(32, dtype=jnp.int32)
    hot = (number[None, :] == (number ^ device)[:, None]).astype(jnp.bfloat16)
    return stages, dest, fwd_mul(hot, small).astype(jnp.bfloat16)


def fwd_mul(left, right):
    return mm(left, right, ((1,), (0,)))


def outer(left, right):
    return mm(left, right, ((0,), (0,)))


def running(values):
    number = jnp.arange(values.shape[0], dtype=jnp.int32)
    return jnp.sum(jnp.where(number[None, :] <= number[:, None], values[None, :], 0), axis=1)


def block_rates(position, feature, out_fan):
    cut_one = 3 * feature * feature
    cut_two = cut_one + feature * feature
    cut_three = cut_two + 4 * feature * feature
    fans = (feature, out_fan, feature, 4 * feature)
    rates = [0.5 * fan ** (-0.5) for fan in fans]
    return jnp.where(
        position < cut_one,
        rates[0],
        jnp.where(position < cut_two, rates[1], jnp.where(position < cut_three, rates[2], rates[3])),
    ).astype(jnp.float32)


def adam_update(weight, gradient, first, second, rates, decay):
    first_new = beta_one * first + (1.0 - beta_one) * gradient
    second_new = beta_two * second + (1.0 - beta_two) * gradient * gradient
    corrected = first_new / (1.0 - beta_one**STEP)
    scaled = second_new / (1.0 - beta_two**STEP)
    weight_new = weight - rates * (corrected / (jnp.sqrt(scaled) + adam_eps) + decay * weight)
    return (weight_new, first_new, second_new)


def local(
    cells_in, lengths, sets_weights, rows_weights, norm_gains, sets_first, rows_first, gains_first,
    sets_second, rows_second, gains_second, out_grad,
):
    f32, bf = jnp.float32, jnp.bfloat16
    devices = lax.axis_size("dev")
    device = lax.axis_index("dev")
    slots, width = cells_in.shape
    feat = width // ATTRS
    per_peer = slots // devices
    rows_even = out_grad.shape[0]
    rows_pad = -(-rows_even // LANES) * LANES
    grid = devices == 32 and width == 1024 and slots == 384

    n_rows, n_gains = rows_weights.shape[0], norm_gains.shape[0]
    small = jnp.concatenate([rows_weights, norm_gains]).astype(bf)
    small = jnp.pad(small, (0, -small.shape[0] % 1024)).reshape(-1, 1024)
    shard = sets_weights.astype(bf).reshape(-1, width)
    if grid:
        stages, dest, small = gather_all(shard, small, device)
    else:
        small = lax.all_gather(small, "dev", axis=0, tiled=False)
        flat = lax.all_gather(shard, "dev", axis=0, tiled=True)
        parts = lambda v, n: v.reshape(width, n, width).transpose(1, 0, 2).reshape(n * width, width)
        flat = jnp.concatenate(
            [parts(flat[: 3 * width], 3), flat[3 * width : 4 * width], parts(flat[4 * width : 8 * width], 4), flat[8 * width :]]
        )
        stages, dest = ((flat,),), jnp.arange(12 * width // UNIT, dtype=jnp.int32)
    plane = device // 8 if grid else jnp.int32(0)
    runs = [(i * width, i * width, width) for i in range(12)]
    small = small.reshape(devices, -1)
    full_rows = small[:, :n_rows].reshape(-1)
    full_gains = small[:, n_rows : n_rows + n_gains].reshape(-1).astype(f32)
    square = feat * feat
    wq2 = full_rows[: 3 * square].reshape(feat, 3 * feat)
    wo2 = full_rows[3 * square : 4 * square].reshape(feat, feat)
    wu2 = full_rows[4 * square : 8 * square].reshape(feat, 4 * feat)
    wd2 = full_rows[8 * square :].reshape(4 * feat, feat)
    g1, g2 = full_gains[:width], full_gains[width : 2 * width]
    g3, g4 = full_gains[2 * width : 2 * width + feat], full_gains[2 * width + feat :]

    table = lengths.reshape(devices, SETS_DEV)
    own = lax.dynamic_index_in_dim(table, device, 0, keepdims=False)
    positions = jnp.arange(slots, dtype=jnp.int32)
    labels = jnp.sum((positions[:, None] >= running(own)[None, :]).astype(jnp.int32), axis=1)
    counts = jnp.sum(table, axis=1) // devices
    ends = running(counts)
    spot = jnp.arange(rows_pad, dtype=jnp.int32)
    past = (ends[None, :] <= spot[:, None]).astype(jnp.int32)
    start = jnp.sum(past * counts[None, :], axis=1)
    pick = jnp.where(spot < rows_even, jnp.sum(past, axis=1) * per_peer + spot - start, -1)

    flat, joined, a1, o1, a2, u1, slope, h1, leaving = forward_layer(
        per_peer, cells_in, g1, g2, labels, plane.reshape(1), stages, dest
    )

    swap = lambda v: lax.all_to_all(
        v.reshape(devices, -1, LANES), "dev", split_axis=0, concat_axis=0, tiled=True
    ).reshape(slots, width)
    og = jnp.pad(out_grad, ((0, rows_pad - rows_even), (0, 0)))
    rows_out, back, dq2, do2, du2, dd2, dg3, dg4 = rows_layer(
        pick, swap(leaving), og, wq2, wo2, wu2, wd2, g3, g4
    )
    rows_out = rows_out[:rows_even]
    raw = swap(back)

    core = device % 2
    which = core.reshape(1)
    half = width // 2
    pair = lambda v: (v, send(v, CORE))
    if grid:
        raw, *pairs = after(raw, *pair(u1), *pair(a2), *pair(o1), *pair(a1))
        u1, a2, o1, a1 = (tuple(pairs[i : i + 2]) for i in (0, 2, 4, 6))
    *dpre, dh1, low_own, low_peer, gz_own, gz_peer, dg2 = widen_back(runs, per_peer, which, raw, slope, h1, g2, flat)
    *dj, cells_grad, dg1 = attend_back(runs, which, dh1, cells_in, g1, joined, labels, flat)
    if grid:
        chip_runs = sorted_runs(2 * shard.shape[0])[1]
        swapped = lambda own, peer: (own, send(peer, CORE))
        operands = u1 + swapped(gz_own, gz_peer) + a2 + swapped(*dpre) + o1 + swapped(low_own, low_peer)
        operands = operands + a1 + swapped(*dj)
        jobs = ((8, 4, True), (4, 4, False), (3, 1, True), (0, 3, False))
        lanes = half // 2
        blocks = [chip_outer(chip_runs, jobs, operands, shift, lanes).reshape(16, -1, lanes) for shift in (0, lanes)]
        blocks[0], dq2, do2, du2, dd2, dg3, dg4 = after(blocks[0], dq2, do2, du2, dd2, dg3, dg4)
        sums = [sum_blocks(part, device // 2) for part in blocks]
        sets_grad = owned_rows(jnp.concatenate(sums, axis=1), device).reshape(-1)
    else:

        def sides(own, peer, n):
            both = jnp.where(core == 0, jnp.stack([own, peer]), jnp.stack([peer, own]))
            return both.reshape(2, slots, n, half).transpose(1, 2, 0, 3).reshape(slots, -1)

        dq1, du1 = outer(a1, sides(*dj, 3)), outer(a2, sides(*dpre, 4))
        gz = sides(gz_own, gz_peer, 1)
        full = jnp.concatenate([dq1.reshape(-1, width), outer(o1, dh1.astype(bf)), du1.reshape(-1, width), outer(u1, gz)])
        sets_grad = lax.psum_scatter(full.astype(bf), "dev", scatter_dimension=0, tiled=True).astype(f32).reshape(-1)

    rows_flat = jnp.concatenate([v.reshape(-1) for v in (*rows_order(dq2, do2), du2, dd2)])
    dg3, dg4 = jnp.sum(dg3, axis=1), jnp.sum(dg4, axis=1)
    gains = jnp.concatenate([dg1[0], dg2[0], dg3, dg4]).reshape(devices, n_gains)
    extra = jnp.concatenate([rows_flat.reshape(devices, n_rows), gains], axis=1).reshape(devices, 1, -1)
    extra = jnp.sum(lax.all_to_all(extra, "dev", split_axis=0, concat_axis=0, tiled=True), axis=(0, 1))
    rows_grad, gains_grad = extra[:n_rows], extra[n_rows:]

    set_index = device * sets_grad.shape[0] + jnp.arange(sets_grad.shape[0], dtype=jnp.int32)
    row_index = device * n_rows + jnp.arange(n_rows, dtype=jnp.int32)
    set_rates = block_rates(set_index, width, max(1, 3 * width // slots))
    row_rates = block_rates(row_index, feat, max(1, feat // 8))
    sets_new, sets_first_new, sets_second_new = adam_update(
        sets_weights, sets_grad, sets_first, sets_second, set_rates, decay_rate
    )
    rows_new, rows_first_new, rows_second_new = adam_update(
        rows_weights, rows_grad, rows_first, rows_second, row_rates, decay_rate
    )
    gains_new, gains_first_new, gains_second_new = adam_update(
        norm_gains, gains_grad, gains_first, gains_second, gain_rate, 0.0
    )
    return (
        rows_out, cells_grad, sets_grad, rows_grad, gains_grad, sets_new, rows_new, gains_new,
        sets_first_new, rows_first_new, gains_first_new, sets_second_new, rows_second_new, gains_second_new,
        sets_new.astype(bf), rows_new.astype(bf), gains_new.astype(bf),
    )


def solution(mesh):
    flat = P("dev")
    tall = P("dev", None)
    return jax.shard_map(
        local,
        mesh=mesh,
        in_specs=(tall, P()) + (flat,) * 9 + (tall,),
        out_specs=(tall, tall) + (flat,) * 15,
        check_vma=False,
    )
```

```python
import functools

import jax
import jax.numpy as jnp
import numpy as np
from jax import lax
from jax.experimental import pallas as pl
from jax.experimental.pallas import tpu as pltpu
from jax.sharding import PartitionSpec as P

ATTRS = 16
HEADS = 8
SETS_DEV = 2
STEP = 5
LANES = 128

norm_eps = 1e-05
beta_one = 0.5
beta_two = 0.5
adam_eps = 1e-08
decay_rate = 0.1
gain_rate = 0.5


BLOCK = 2


def mm(left, right, dims):
    return lax.dot_general(left, right, (dims, ((), ())), preferred_element_type=jnp.float32)


def gelu_pair(v):
    size = jnp.abs(v) * 0.7071067811865476
    t = 1.0 / (1.0 + 0.3275911 * size)
    bell = jnp.exp(-0.5 * v * v)
    poly = t * (0.254829592 + t * (-0.284496736 + t * (1.421413741 + t * (-1.453152027 + t * 1.061405429))))
    tail = 0.5 * poly * bell
    phi = jnp.where(v < 0.0, tail, 1.0 - tail)
    return v * phi, phi + v * (bell * 0.3989422804014327)


def rows_kernel(
    pick_ref, arrived_ref, og_ref, wq_ref, wqt_ref, wo_ref, wot_ref, wu_ref, wut_ref, wd_ref, wdt_ref, g3_ref, g4_ref,
    out_ref, back_ref, dwq_ref, dwo_ref, dwu_ref, dwd_ref, dg3_ref, dg4_ref,
    joined, prob, dscore, outs, douts, dj, back_acc,
):
    f32, bf = jnp.float32, jnp.bfloat16
    step = pl.program_id(0)
    last = pl.num_programs(0) - 1
    slots = arrived_ref.shape[0]
    scaling = HEADS ** (-0.5)
    feat = 64

    @pl.when(step == 0)
    def _():
        for ref in (dwq_ref, dwo_ref, dwu_ref, dwd_ref, dg3_ref, dg4_ref, back_acc):
            ref[...] = jnp.zeros_like(ref)

    source = lax.broadcasted_iota(jnp.int32, (slots, LANES), 0)
    hot = (source == pick_ref[0]).astype(f32).astype(bf)
    x_t = mm(arrived_ref[...], hot, ((0,), (0,)))

    def to_lanes(tall):
        return jnp.concatenate([tall[a * feat : (a + 1) * feat] for a in range(ATTRS)], axis=1)

    def to_tall(wide):
        return jnp.concatenate([wide[:, a * LANES : (a + 1) * LANES] for a in range(ATTRS)], axis=0)

    def norm(v):
        center = v - jnp.mean(v, axis=0, keepdims=True)
        root = lax.rsqrt(jnp.mean(center * center, axis=0, keepdims=True) + norm_eps)
        return center * root, root

    def norm_back(hat, root, gain, upstream):
        dhat = upstream * gain
        return root * (
            dhat - jnp.mean(dhat, axis=0, keepdims=True) - hat * jnp.mean(dhat * hat, axis=0, keepdims=True)
        )

    def fold(v):
        total = v[:, :LANES]
        for a in range(1, ATTRS):
            total = total + v[:, a * LANES : (a + 1) * LANES]
        return total

    x = to_lanes(x_t)
    g3, g4 = g3_ref[...], g4_ref[...]
    hat3, root3 = norm(x)
    a3 = (hat3 * g3).astype(bf)
    j_t = mm(wqt_ref[...], a3, ((1,), (0,))).astype(bf).astype(f32)
    for a in range(ATTRS):
        joined[a] = j_t[:, a * LANES : (a + 1) * LANES]

    def attend(n, carry):
        group = [n * BLOCK + i for i in range(BLOCK)]
        q = [[joined[a, d * 8 : d * 8 + 8] * scaling for d in range(8)] for a in group]
        scores = [[] for _ in group]
        for b in range(ATTRS):
            k = [joined[b, 64 + d * 8 : 72 + d * 8] for d in range(8)]
            for i in range(BLOCK):
                scores[i].append(functools.reduce(jnp.add, [q[i][d] * k[d] for d in range(8)]))
        inverse = []
        for i in range(BLOCK):
            peak = functools.reduce(jnp.maximum, scores[i])
            scores[i] = [jnp.exp(s - peak) for s in scores[i]]
            inverse.append(1.0 / functools.reduce(jnp.add, scores[i]))
        o = [[None] * 8 for _ in group]
        for b in range(ATTRS):
            v = [joined[b, 128 + d * 8 : 136 + d * 8] for d in range(8)]
            for i, a in enumerate(group):
                p = scores[i][b] * inverse[i]
                prob[a, b] = p
                p = p.astype(bf).astype(f32)
                for d in range(8):
                    o[i][d] = p * v[d] if b == 0 else o[i][d] + p * v[d]
        for i, a in enumerate(group):
            for d in range(8):
                outs[a, d * 8 : d * 8 + 8] = o[i][d]
        return carry

    lax.fori_loop(0, ATTRS // BLOCK, attend, 0, unroll=2)
    o = jnp.concatenate([outs[a] for a in range(ATTRS)], axis=1).astype(bf)
    h3 = x + mm(wot_ref[...], o, ((1,), (0,)))
    hat4, root4 = norm(h3)
    a4 = (hat4 * g4).astype(bf)
    pre = mm(wut_ref[...], a4, ((1,), (0,)))
    active, slope = gelu_pair(pre)
    u = active.astype(bf)
    y = h3 + mm(wdt_ref[...], u, ((1,), (0,)))
    out_ref[...] = to_tall(y).T.astype(bf)

    grad = to_lanes(og_ref[...].astype(f32).T)
    gz = grad.astype(bf)
    dwd_ref[...] += mm(u, gz, ((1,), (1,)))
    dpre = (slope * mm(wd_ref[...], gz, ((1,), (0,)))).astype(bf)
    dwu_ref[...] += mm(a4, dpre, ((1,), (1,)))
    da4 = mm(wu_ref[...], dpre, ((1,), (0,)))
    dg4_ref[...] += fold(da4 * hat4)
    dh3 = grad + norm_back(hat4, root4, g4, da4)

    gz = dh3.astype(bf)
    dwo_ref[...] += mm(o, gz, ((1,), (1,)))
    do = mm(wo_ref[...], gz, ((1,), (0,))).astype(bf).astype(f32)
    for a in range(ATTRS):
        douts[a] = do[:, a * LANES : (a + 1) * LANES]

    def spread(n, carry):
        group = [n * BLOCK + i for i in range(BLOCK)]
        up = [[douts[a, d * 8 : d * 8 + 8] for d in range(8)] for a in group]
        dot, slopes = [None] * BLOCK, [[] for _ in group]
        for b in range(ATTRS):
            v = [joined[b, 128 + d * 8 : 136 + d * 8] for d in range(8)]
            for i, a in enumerate(group):
                s = functools.reduce(jnp.add, [up[i][d] * v[d] for d in range(8)])
                slopes[i].append(s)
                term = prob[a, b] * s
                dot[i] = term if b == 0 else dot[i] + term
        dq = [[None] * 8 for _ in group]
        for b in range(ATTRS):
            k = [joined[b, 64 + d * 8 : 72 + d * 8] for d in range(8)]
            for i, a in enumerate(group):
                ds = (prob[a, b] * (slopes[i][b] - dot[i])).astype(bf).astype(f32) * scaling
                dscore[a, b] = ds
                for d in range(8):
                    dq[i][d] = ds * k[d] if b == 0 else dq[i][d] + ds * k[d]
        for i, a in enumerate(group):
            for d in range(8):
                dj[a, d * 8 : d * 8 + 8] = dq[i][d]
        return carry

    lax.fori_loop(0, ATTRS // BLOCK, spread, 0, unroll=2)

    def collect(n, carry):
        group = [n * BLOCK + i for i in range(BLOCK)]
        dk, dv = [[None] * 8 for _ in group], [[None] * 8 for _ in group]
        for a in range(ATTRS):
            q = [joined[a, d * 8 : d * 8 + 8] for d in range(8)]
            up = [douts[a, d * 8 : d * 8 + 8] for d in range(8)]
            for i, b in enumerate(group):
                ds = dscore[a, b]
                p = prob[a, b].astype(bf).astype(f32)
                for d in range(8):
                    dk[i][d] = ds * q[d] if a == 0 else dk[i][d] + ds * q[d]
                    dv[i][d] = p * up[d] if a == 0 else dv[i][d] + p * up[d]
        for i, b in enumerate(group):
            for d in range(8):
                dj[b, 64 + d * 8 : 72 + d * 8] = dk[i][d]
                dj[b, 128 + d * 8 : 136 + d * 8] = dv[i][d]
        return carry

    lax.fori_loop(0, ATTRS // BLOCK, collect, 0, unroll=2)
    djl = jnp.concatenate([dj[a] for a in range(ATTRS)], axis=1).astype(bf)
    dwq_ref[...] += mm(a3, djl, ((1,), (1,)))
    da3 = mm(wq_ref[...], djl, ((1,), (0,)))
    dg3_ref[...] += fold(da3 * hat3)
    dhc = to_tall(dh3 + norm_back(hat3, root3, g3, da3)).astype(bf)
    back_acc[...] += mm(hot, dhc, ((1,), (1,)))

    @pl.when(step == last)
    def _():
        back_ref[...] = back_acc[...].astype(bf)


def rows_layer(pick, arrived, og, wq, wo, wu, wd, g3, g4):
    f32, bf = jnp.float32, jnp.bfloat16
    total, width = og.shape
    slots = arrived.shape[0]
    steps = total // LANES
    feat = 64
    wqp = wq.reshape(feat, 3, HEADS, 8).transpose(0, 1, 3, 2).reshape(feat, 3 * feat)
    wop = wo.reshape(HEADS, 8, feat).transpose(1, 0, 2).reshape(feat, feat)
    whole = lambda *shape: pl.BlockSpec(shape, lambda t: (0,) * len(shape))
    outs = pl.pallas_call(
        rows_kernel,
        grid=(steps,),
        in_specs=[
            pl.BlockSpec((1, 1, LANES), lambda t: (t, 0, 0)),
            whole(slots, width),
            pl.BlockSpec((LANES, width), lambda t: (t, 0)),
            whole(feat, 192), whole(192, feat), whole(feat, feat), whole(feat, feat),
            whole(feat, 256), whole(256, feat), whole(256, feat), whole(feat, 256),
            whole(feat, 1), whole(feat, 1),
        ],
        out_specs=[
            pl.BlockSpec((LANES, width), lambda t: (t, 0)),
            whole(slots, width),
            whole(feat, 192), whole(feat, feat), whole(feat, 256), whole(256, feat),
            whole(feat, LANES), whole(feat, LANES),
        ],
        out_shape=[
            jax.ShapeDtypeStruct((total, width), bf),
            jax.ShapeDtypeStruct((slots, width), bf),
            jax.ShapeDtypeStruct((feat, 192), f32),
            jax.ShapeDtypeStruct((feat, feat), f32),
            jax.ShapeDtypeStruct((feat, 256), f32),
            jax.ShapeDtypeStruct((256, feat), f32),
            jax.ShapeDtypeStruct((feat, LANES), f32),
            jax.ShapeDtypeStruct((feat, LANES), f32),
        ],
        scratch_shapes=[
            pltpu.VMEM((ATTRS, 192, LANES), f32),
            pltpu.VMEM((ATTRS, ATTRS, 8, LANES), f32),
            pltpu.VMEM((ATTRS, ATTRS, 8, LANES), f32),
            pltpu.VMEM((ATTRS, 64, LANES), f32),
            pltpu.VMEM((ATTRS, 64, LANES), f32),
            pltpu.VMEM((ATTRS, 192, LANES), f32),
            pltpu.VMEM((slots, width), f32),
        ],
        compiler_params=pltpu.CompilerParams(vmem_limit_bytes=56 * 2**20),
    )(
        pick.reshape(steps, 1, LANES), arrived, og,
        wqp, wqp.T, wop, wop.T, wu, wu.T, wd, wd.T, g3.reshape(feat, 1), g4.reshape(feat, 1),
    )
    return outs


def rows_order(dwqp, dwop):
    feat = dwop.shape[0]
    dwq = dwqp.reshape(feat, 3, 8, HEADS).transpose(0, 1, 3, 2).reshape(feat, 3 * feat)
    return dwq, dwop.reshape(8, HEADS, feat).transpose(1, 0, 2).reshape(feat, feat)


UNIT = 32


def placed(flat):
    if flat < 3072:
        return flat % 3 * 1024 + flat // 3
    if flat < 4096 or flat >= 8192:
        return flat
    return 4096 + flat % 4 * 1024 + (flat - 4096) // 4


def sorted_runs(per):
    orders, runs = [], []
    for first in range(0, 12288, per):
        places = [placed(first + i) for i in range(per)]
        order = sorted(range(per), key=lambda i: places[i])
        orders.append(order)
        for at, i in enumerate(order):
            if at and places[i] == runs[-1][1] + runs[-1][2] and places[i] % 1024:
                runs[-1][2] += 1
            else:
                runs.append([first + at, places[i], 1])
    return np.array(orders, np.int32), sorted((tuple(run) for run in runs), key=lambda run: run[1])


class Copies:
    def __init__(self, sems):
        self.sems, self.used = sems, 0

    def start(self, src, dst):
        copy = pltpu.make_async_copy(src, dst, self.sems.at[self.used])
        copy.start()
        self.used += 1
        return copy

    def rows(self, src, dst, parts=4):
        count = src.shape[0] // parts
        cuts = [pl.ds(i * count, count) for i in range(parts)]
        return [self.start(src.at[cut], dst.at[cut]) for cut in cuts]


def wait(copies):
    for copy in copies:
        copy.wait()


def load_mats(copies, runs, flat_ref, held, first, width):
    groups = [[] for _ in range(held.shape[0] // width)]
    for src, dst, rows in runs:
        i = dst // width - first
        if 0 <= i < len(groups):
            groups[i].append(copies.start(flat_ref.at[pl.ds(src, rows)], held.at[pl.ds(dst - first * width, rows)]))
    return groups


def low_norm(v, gain):
    center = v - jnp.mean(v, axis=1, keepdims=True)
    root = lax.rsqrt(jnp.mean(center * center, axis=1, keepdims=True) + norm_eps)
    return (center * root * gain).astype(jnp.bfloat16)


def pull_norm(v, gain, upstream):
    center = v - jnp.mean(v, axis=1, keepdims=True)
    root = lax.rsqrt(jnp.mean(center * center, axis=1, keepdims=True) + norm_eps)
    hat = center * root
    dhat = upstream * gain
    inner = jnp.mean(dhat * hat, axis=1, keepdims=True)
    grad = root * (dhat - jnp.mean(dhat, axis=1, keepdims=True) - hat * inner)
    return grad, jnp.sum(upstream * hat, axis=0, keepdims=True)


def forward_kernel(counts, turn, plane_ref, dest_ref, g1_ref, g2_ref, tall_ref, wide_ref, h0_ref, *refs):
    stages = []
    for count in counts:
        stages.append(refs[:count])
        refs = refs[count:]
    forward_body(turn, plane_ref, dest_ref, g1_ref, g2_ref, tall_ref, wide_ref, h0_ref, stages, *refs)


def forward_body(turn, plane_ref, dest_ref, g1_ref, g2_ref, tall_ref, wide_ref, h0_ref, stages,
                   big_out, joined_out, a1_out, o1_out, a2_out, u1_out, slope_out, h1_out, leave_out,
                   mats, bias, h0, joined, a1, o1, a2, u1, slope, h1, leave, load_sems, plane_sems, store_sems):
    f32, bf = jnp.float32, jnp.bfloat16
    slots, width = h0.shape
    head = width // HEADS
    tile = 512
    loads, stores = Copies(load_sems), Copies(store_sems)
    first = loads.rows(h0_ref, h0)
    part = mats.shape[0] // len(stages)

    def load_stage(s, plane):
        number = sum(piece.shape[0] for pieces in stages[:s] for piece in pieces) // UNIT
        for piece in stages[s]:
            for u in range(piece.shape[0] // UNIT):
                place = pl.multiple_of(dest_ref[number] * UNIT, UNIT)
                number += 1
                pltpu.make_async_copy(
                    piece.at[pl.ds(u * UNIT, UNIT)], mats.at[pl.ds(place, UNIT)], plane_sems.at[plane]
                ).start()

    for plane in range(len(stages)):
        for s in range(len(stages)):
            pl.when(plane_ref[0] ^ s == plane)(functools.partial(load_stage, s, plane))

    def arrived(plane):
        rows = mats.at[pl.ds(plane * part, part)]
        pltpu.make_async_copy(rows, rows, plane_sems.at[plane]).wait()

    saves = []
    bias[...] = jnp.where(tall_ref[...] == wide_ref[...], 0.0, -jnp.inf)
    wait(first)
    a1[...] = low_norm(h0[...].astype(f32), g1_ref[...])
    saves += stores.rows(a1, a1_out)
    for plane in range(len(stages) if len(stages) < 4 else 1):
        arrived(plane)
    for i in range(3):
        for t in range(width // tile):
            cols = slice(i * width + t * tile, i * width + (t + 1) * tile)
            joined[:, cols] = mm(a1[...], mats[i * width : (i + 1) * width, t * tile : (t + 1) * tile], ((1,), (0,))).astype(bf)
    saves += stores.rows(joined, joined_out)
    saves += stores.rows(mats.at[pl.ds(0, 3 * width)], big_out.at[pl.ds(0, 3 * width)], 3)

    def attend(h, carry):
        part = lambda i: joined[:, pl.ds(pl.multiple_of(i * width + h * head, head), head)]
        scores = mm(part(0), part(1), ((1,), (1,))) * head ** (-0.5) + bias[...]
        weights = jnp.exp(scores - jnp.max(scores, axis=1, keepdims=True))
        chance = weights * (1.0 / jnp.sum(weights, axis=1, keepdims=True))
        o1[:, pl.ds(pl.multiple_of(h * head, head), head)] = mm(chance.astype(bf), part(2), ((1,), (0,))).astype(bf)
        return carry

    lax.fori_loop(0, HEADS, attend, 0, unroll=2)
    saves += stores.rows(o1, o1_out)
    if len(stages) == 4:
        arrived(1)
    for t in range(width // tile):
        cols = slice(t * tile, (t + 1) * tile)
        h1[:, cols] = h0[:, cols].astype(f32) + mm(o1[...], mats[3 * width : 4 * width, cols], ((1,), (0,)))
    saves += stores.rows(h1, h1_out)
    a2[...] = low_norm(h1[...], g2_ref[...])
    saves += stores.rows(a2, a2_out)
    if len(stages) == 4:
        arrived(2)
    for i in range(4):
        for t in range(width // tile):
            cols = slice(t * tile, (t + 1) * tile)
            active, rise = gelu_pair(mm(a2[...], mats[(4 + i) * width : (5 + i) * width, cols], ((1,), (0,))))
            cols = slice(i * width + t * tile, i * width + (t + 1) * tile)
            u1[:, cols] = active.astype(bf)
            slope[:, cols] = rise.astype(bf)
            saves.append(stores.start(u1.at[:, cols], u1_out.at[:, cols]))
            saves.append(stores.start(slope.at[:, cols], slope_out.at[:, cols]))
    if len(stages) == 4:
        arrived(3)
    saves += stores.rows(mats.at[pl.ds(3 * width, 9 * width)], big_out.at[pl.ds(3 * width, 9 * width)], 9)
    to, source = (lax.broadcasted_iota(jnp.int32, (slots, slots), axis) for axis in (0, 1))
    hot = (source == to % turn * (slots // turn) + to // turn).astype(f32).astype(bf)
    for t in range(width // tile):
        cols = slice(t * tile, (t + 1) * tile)
        h2 = (h1[:, cols] + mm(u1[...], mats[8 * width :, cols], ((1,), (0,)))).astype(bf)
        leave[:, cols] = mm(hot, h2, ((1,), (0,))).astype(bf)
        saves.append(stores.start(leave.at[:, cols], leave_out.at[:, cols]))
    wait(saves)


def own_kernel(kernel, operands, small, outs, scratch, limit, flops):
    def spec(v):
        space = pltpu.SMEM if v.ndim == 1 else pltpu.VMEM
        return pl.BlockSpec(memory_space=space)

    anywhere = pl.BlockSpec(memory_space=pl.ANY)
    tiny = pl.BlockSpec(memory_space=pltpu.VMEM)
    return pl.pallas_call(
        kernel,
        in_specs=[spec(v) if n in small else anywhere for n, v in enumerate(operands)],
        out_specs=[tiny if out.shape[0] == 1 else anywhere for out in outs],
        out_shape=outs,
        scratch_shapes=scratch,
        compiler_params=pltpu.CompilerParams(vmem_limit_bytes=limit * 2**20),
        cost_estimate=pl.CostEstimate(flops=flops, bytes_accessed=40 * 2**20, transcendentals=10**6),
    )(*operands)


def forward_layer(turn, h0, g1, g2, labels, plane, stages, dest):
    f32, bf = jnp.float32, jnp.bfloat16
    slots, width = h0.shape
    shape, vmem = jax.ShapeDtypeStruct, pltpu.VMEM
    sizes = [(3, bf), (1, bf), (1, bf), (1, bf), (4, bf), (4, bf), (1, f32), (1, bf)]
    mats = (12 * width, width)
    return own_kernel(
        functools.partial(forward_kernel, tuple(len(pieces) for pieces in stages), turn),
        (plane, dest, g1.reshape(1, -1), g2.reshape(1, -1), labels.reshape(-1, 1), labels.reshape(1, -1), h0, *sum(stages, ())),
        (0, 1, 2, 3, 4, 5),
        [shape(mats, bf)] + [shape((slots, n * width), kind) for n, kind in sizes],
        [vmem(mats, bf), vmem((slots, slots), f32), vmem((slots, width), bf)]
        + [vmem((slots, n * width), kind) for n, kind in sizes]
        + [pltpu.SemaphoreType.DMA((4,)), pltpu.SemaphoreType.DMA((len(stages),)), pltpu.SemaphoreType.DMA((50,))],
        60,
        10**10,
    )


def widen_back_kernel(runs, turn, core_ref, g2_ref, raw_ref, slope_ref, h1_ref, flat_ref,
                      dpre_own, dpre_peer, dh_out, low_own, low_peer, gz_own, gz_peer, dg_ref,
                      ups, downs, raw, gz, slope, h1, dpre, dh, low, gz_sides, da, load_sems, store_sems):
    f32, bf = jnp.float32, jnp.bfloat16
    width = gz.shape[1]
    half = width // 2
    core = core_ref[0]
    loads, stores = Copies(load_sems), Copies(store_sems)
    raw_copies = loads.rows(raw_ref, raw)
    down_copies, slope_copies, up_copies = [], [], []
    for i in range(4):
        part, cols = pl.ds(i * width, width), pl.ds(i * width, width)
        down_copies += load_mats(loads, runs, flat_ref, downs.at[part], 8 + i, width)
        slope_copies.append(loads.start(slope_ref.at[:, cols], slope.at[:, cols]))
        up_copies += load_mats(loads, runs, flat_ref, ups.at[part], 4 + i, width)
    h1_copies = loads.rows(h1_ref, h1)
    wait(raw_copies)
    slots = gz.shape[0]
    slot, source = (lax.broadcasted_iota(jnp.int32, (slots, slots), axis) for axis in (0, 1))
    devices = slots // turn
    hot = (source == slot % devices * turn + slot // devices).astype(f32).astype(bf)
    gz[...] = mm(hot, raw[...], ((1,), (0,))).astype(bf)
    saves = []
    for s in range(2):
        gz_sides[s ^ core] = gz[:, s * half : (s + 1) * half]
    saves += [stores.start(gz_sides.at[0], gz_own), stores.start(gz_sides.at[1], gz_peer)]
    for i in range(4):
        wait(down_copies[i] + [slope_copies[i]] + up_copies[i])
        for s in range(2):
            hidden = slice(i * width + s * half, i * width + (s + 1) * half)
            du = mm(gz[...], downs[hidden], ((1,), (1,)))
            piece = (slope[:, hidden].astype(f32) * du).astype(bf)
            dpre[s ^ core, :, i * half : (i + 1) * half] = piece
            term = mm(piece, ups[i * width : (i + 1) * width, s * half : (s + 1) * half], ((1,), (1,)))
            da[...] = term if i == s == 0 else da[...] + term
        lanes = pl.ds(i * half, half)
        saves += [stores.start(dpre.at[0, :, lanes], dpre_own.at[:, lanes]), stores.start(dpre.at[1, :, lanes], dpre_peer.at[:, lanes])]
    wait(h1_copies)
    grad, dg_ref[...] = pull_norm(h1[...], g2_ref[...], da[...])
    dh[...] = gz[...].astype(f32) + grad
    saves += stores.rows(dh, dh_out)
    for s in range(2):
        low[s ^ core] = dh[:, s * half : (s + 1) * half].astype(bf)
    saves += [stores.start(low.at[0], low_own), stores.start(low.at[1], low_peer)]
    wait(saves)


def widen_back(runs, turn, core, raw, slope, h1, g2, flat):
    f32, bf = jnp.float32, jnp.bfloat16
    slots, width = raw.shape
    half = width // 2
    shape, vmem = jax.ShapeDtypeStruct, pltpu.VMEM
    side = shape((slots, half), bf)
    ups = sum(4 <= dst // width < 12 for _, dst, _ in runs)
    return own_kernel(
        functools.partial(widen_back_kernel, runs, turn),
        (core, g2.reshape(1, -1), raw, slope, h1, flat),
        (0, 1),
        [shape((slots, 2 * width), bf)] * 2 + [shape((slots, width), f32)] + [side] * 4 + [shape((1, width), f32)],
        [
            vmem((4 * width, width), bf), vmem((4 * width, width), bf), vmem((slots, width), bf), vmem((slots, width), bf),
            vmem((slots, 4 * width), bf),
            vmem((slots, width), f32), vmem((2, slots, 2 * width), bf), vmem((slots, width), f32), vmem((2, slots, half), bf),
            vmem((2, slots, half), bf), vmem((slots, width), f32),
            pltpu.SemaphoreType.DMA((ups + 12,)), pltpu.SemaphoreType.DMA((16,)),
        ],
        60,
        64 * 10**8,
    )


def attend_back_kernel(runs, core_ref, g1_ref, tall_ref, wide_ref, dh_ref, h0_ref, joined_ref, flat_ref,
                       own_out, peer_out, grad_out, dg_ref,
                       mats, bias, dh, h0, joined, dblend, dj, sides, load_sems, store_sems):
    f32, bf = jnp.float32, jnp.bfloat16
    slots, width = dh.shape
    head = width // HEADS
    half = width // 2
    tile = 512
    scaling = head ** (-0.5)
    core = core_ref[0]
    loads, stores = Copies(load_sems), Copies(store_sems)
    dh_copies = loads.rows(dh_ref, dh)
    out_copies = load_mats(loads, runs, flat_ref, mats.at[pl.ds(3 * width, width)], 3, width)
    joined_copies = loads.rows(joined_ref, joined)
    mat_copies = load_mats(loads, runs, flat_ref, mats.at[pl.ds(0, 3 * width)], 0, width)
    h0_copies = loads.rows(h0_ref, h0)
    bias[...] = jnp.where(tall_ref[...] == wide_ref[...], 0.0, -jnp.inf)
    wait(dh_copies)
    gz = dh[...].astype(bf)
    wait(out_copies[0])
    for t in range(width // tile):
        rows = slice(3 * width + t * tile, 3 * width + (t + 1) * tile)
        dblend[:, t * tile : (t + 1) * tile] = mm(gz, mats[rows], ((1,), (1,))).astype(bf)
    wait(joined_copies)

    def attend(h, carry):
        lanes = lambda i: pl.ds(pl.multiple_of(i * width + h * head, head), head)
        q, k, v = (joined[:, lanes(i)] for i in range(3))
        do = dblend[:, pl.ds(pl.multiple_of(h * head, head), head)]
        scores = mm(q, k, ((1,), (1,))) * scaling + bias[...]
        weights = jnp.exp(scores - jnp.max(scores, axis=1, keepdims=True))
        chance = weights * (1.0 / jnp.sum(weights, axis=1, keepdims=True))
        dchance = mm(do, v, ((1,), (1,)))
        dot = jnp.sum(chance * dchance, axis=1, keepdims=True)
        ds = (chance * (dchance - dot)).astype(bf)
        parts = (
            mm(ds, k, ((1,), (0,))) * scaling,
            mm(ds, q, ((0,), (0,))) * scaling,
            mm(chance.astype(bf), do, ((0,), (0,))),
        )
        per_side = HEADS // 2
        for i in range(3):
            part = parts[i].astype(bf)
            dj[:, lanes(i)] = part
            sides[(h // per_side) ^ core, :, pl.ds(pl.multiple_of(i * half + h % per_side * head, head), head)] = part
        return carry

    lax.fori_loop(0, HEADS, attend, 0, unroll=2)
    saves = [stores.start(sides.at[1], peer_out), stores.start(sides.at[0], own_out)]
    da = None
    for i in range(3):
        wait(mat_copies[i])
        term = mm(dj[:, i * width : (i + 1) * width], mats[i * width : (i + 1) * width], ((1,), (1,)))
        da = term if da is None else da + term
    wait(h0_copies)
    grad, dg_ref[...] = pull_norm(h0[...].astype(f32), g1_ref[...], da)
    dh[...] = dh[...] + grad
    wait(saves + stores.rows(dh, grad_out))


def attend_back(runs, core, dh, h0, g1, joined, labels, flat):
    f32, bf = jnp.float32, jnp.bfloat16
    slots, width = dh.shape
    shape, vmem = jax.ShapeDtypeStruct, pltpu.VMEM
    mats = sum(dst // width < 4 for _, dst, _ in runs)
    return own_kernel(
        functools.partial(attend_back_kernel, runs),
        (core, g1.reshape(1, -1), labels.reshape(-1, 1), labels.reshape(1, -1), dh, h0, joined, flat),
        (0, 1, 2, 3),
        [shape((slots, 3 * width // 2), bf)] * 2 + [shape((slots, width), f32), shape((1, width), f32)],
        [
            vmem((4 * width, width), bf), vmem((slots, slots), f32), vmem((slots, width), f32), vmem((slots, width), bf),
            vmem((slots, 3 * width), bf), vmem((slots, width), bf), vmem((slots, 3 * width), bf),
            vmem((2, slots, 3 * width // 2), bf),
            pltpu.SemaphoreType.DMA((mats + 12,)), pltpu.SemaphoreType.DMA((6,)),
        ],
        60,
        64 * 10**8,
    )


def chip_outer_kernel(runs, jobs, shift, *refs):
    bf = jnp.bfloat16
    count = 4 * len(jobs)
    operands, refs = refs[:count], refs[-(count + 4) :]
    out, held, (result, load_sems, store_sems) = refs[0], refs[1 : count + 1], refs[count + 1 :]
    loads, stores = Copies(load_sems), Copies(store_sems)
    arrivals = [loads.rows(ref, v, 2) for ref, v in zip(operands, held, strict=True)]
    width, lanes_out = 1024, result.shape[1]
    half, tile = width // 2, 512
    saves, done = [], 0
    for n, (first, matrices, tall) in enumerate(jobs):
        left, left_peer, right, right_peer = held[4 * n : 4 * n + 4]
        for copies in arrivals[4 * n : 4 * n + 4]:
            wait(copies)
        for i in range(matrices):
            from_lane = (0 if tall else i * half) + shift
            lanes = slice(from_lane, from_lane + lanes_out)
            for t in range(width // tile):
                cols = (i if tall else 0) * width + t * tile
                cols = slice(cols, cols + tile)
                term = mm(left[:, cols], right[:, lanes], ((0,), (0,))) + mm(left_peer[:, cols], right_peer[:, lanes], ((0,), (0,)))
                result[done * width + t * tile : done * width + (t + 1) * tile, :] = term.astype(bf)
            for to, place, rows in runs:
                if place // width == first + i:
                    part = result.at[pl.ds(done * width + place % width, rows)]
                    saves.append(stores.start(part, out.at[pl.ds(to, rows)]))
            done += 1
    wait(saves)


def chip_outer(runs, jobs, operands, shift, lanes, onto=()):
    bf = jnp.bfloat16
    anywhere = pl.BlockSpec(memory_space=pl.ANY)
    matrices = [first + i for first, n, _ in jobs for i in range(n)]
    saves = sum(place // 1024 in matrices for _, place, _ in runs)
    return pl.pallas_call(
        functools.partial(chip_outer_kernel, runs, jobs, shift),
        in_specs=[anywhere] * (len(operands) + len(onto)),
        out_specs=anywhere,
        out_shape=jax.ShapeDtypeStruct((12288, lanes), bf),
        input_output_aliases={len(operands): 0} if onto else {},
        scratch_shapes=[pltpu.VMEM(v.shape, bf) for v in operands]
        + [
            pltpu.VMEM((len(matrices) * 1024, lanes), bf),
            pltpu.SemaphoreType.DMA((2 * len(operands),)),
            pltpu.SemaphoreType.DMA((saves,)),
        ],
        compiler_params=pltpu.CompilerParams(vmem_limit_bytes=60 * 2**20),
        cost_estimate=pl.CostEstimate(
            flops=len(matrices) * 5 * 10**8, bytes_accessed=len(matrices) * 2 * 2**20, transcendentals=0
        ),
    )(*operands, *onto)


CORE = 1


def send(v, bit):
    return lax.ppermute(v, "dev", [(d, d ^ bit) for d in range(32)])


def after(*values):
    return lax.optimization_barrier(values)


def sum_blocks(blocks, chip):
    f32, bf = jnp.float32, jnp.bfloat16
    half = blocks.shape[1] // 2
    block = lambda m: lax.dynamic_index_in_dim(blocks, chip ^ (m >> 1), 0, keepdims=False)
    total = lambda *parts: sum(part.astype(f32) for part in parts)
    both = lambda one, two: jnp.concatenate([one.astype(bf), two.astype(bf)])

    across_far, up_far, across = block(30), block(14), block(24)
    a, b, c, d, e = after(
        send(across_far[:half], 4), send(across_far[half:], 2), send(across, 8), send(up_far[:half], 4), send(up_far[half:], 2)
    )
    side, other = block(26), block(28)
    across_x, across_y = both(total(side[:half], a), side[half:]), both(other[:half], total(other[half:], b))
    side, other = block(10), block(12)
    up_x, up_y = both(total(side[:half], d), side[half:]), both(other[:half], total(other[half:], e))
    over = total(block(16), c)

    a, b, c = after(send(across_x, 8), send(up_x, 2), send(up_y, 4))
    over_x, up = total(block(18), a), total(block(8), b, c).astype(bf)
    over_far, own_far = block(22), block(6)
    a, b, c, d, e = after(
        send(across_y, 8), send(over_far[:half], 4), send(over_far[half:], 2), send(own_far[:half], 4), send(own_far[half:], 2)
    )
    other = total(block(20), a)
    over_x, over_y = both(total(over_x[:half], b), over_x[half:]), both(other[:half], total(other[half:], c))
    side, other = block(2), block(4)
    own_x, own_y = both(total(side[:half], d), side[half:]), both(other[:half], total(other[half:], e))

    a, b, c = after(send(over_x, 2), send(over_y, 4), send(up, 8))
    own = total(block(0), c)
    over = total(over, a, b).astype(bf)
    return total(own, send(over, 16), send(own_x, 2), send(own_y, 4))


def owned_rows(own, device):
    core, chip = device % 2, device // 2
    half = own.shape[0] // 2
    orders, _ = sorted_runs(2 * half)
    order = lax.dynamic_index_in_dim(jnp.asarray(np.argsort(orders, axis=1).astype(np.int32)), chip, 0, keepdims=False)
    own = jnp.take(own, order, axis=0)
    mine = lax.dynamic_slice_in_dim(own, core * half, half, 0)
    peer = send(lax.dynamic_slice_in_dim(own, (1 - core) * half, half, 0), CORE)
    return jnp.where(core == 0, jnp.concatenate([mine, peer], axis=1), jnp.concatenate([peer, mine], axis=1))


def gather_all(shard, small, device):
    per = shard.shape[0]
    half, extra = per // 2, small.shape[0]
    orders, runs = sorted_runs(per)
    order = lax.dynamic_index_in_dim(jnp.asarray(orders), device, 0, keepdims=False)
    hot = (order[:, None] == jnp.arange(per, dtype=jnp.int32)[None, :]).astype(jnp.bfloat16)
    own = jnp.concatenate([fwd_mul(hot, shard).astype(jnp.bfloat16), small])
    table = np.zeros((32 * per // UNIT,), np.int32)
    for src, dst, rows in runs:
        table[src // UNIT : (src + rows) // UNIT] = range(dst // UNIT, (dst + rows) // UNIT)
    by_mask = jnp.take(jnp.asarray(table.reshape(32, -1)), device ^ jnp.arange(32, dtype=jnp.int32), axis=0)
    stack = lambda *parts: jnp.concatenate([part[:per] for part in parts])

    own, own_x, own_y, up = after(own, send(own, 2), send(own, 4), send(own, 8))
    a, b, up_x, up_y, over = after(
        send(own_x[:half], 4), send(own_y[half:], 2), send(up, 2), send(up, 4), send(own, 16)
    )
    own_far = jnp.concatenate([a, b])
    own_stack = stack(own, own_x, own_y, own_far)
    a, b, over_x, over_y, across, own_stack = after(
        send(up_x[:half], 4), send(up_y[half:], 2), send(over, 2), send(over, 4), send(over, 8), own_stack
    )
    up_far = jnp.concatenate([a, b])
    up_stack = stack(up, up_x, up_y, up_far)
    over_far, across_x, across_y, own_peer, up_peer = after(
        send(over_y, 2), send(over_x, 8), send(across, 4), send(own_stack, CORE), send(up_stack, CORE)
    )
    a, b, over_far = after(across_x[:half], across_y[half:], over_far)
    over_stack, across_stack = stack(over, over_x, over_y, over_far), stack(across, across_x, across_y)
    a, b, over_peer, across_peer = after(send(a, 4), send(b, 2), send(over_stack, CORE), send(across_stack, CORE))
    plane = (own, own_x, own_y, own_far, up, up_x, up_y, up_far, over, over_x, over_y, over_far, across, across_x, across_y)
    small = jnp.concatenate([v[per:] for v in plane] + [b[per - half :]])
    last = (a, b[: per - half])
    last_peer, small_peer = tuple(send(v, CORE) for v in last), send(small, CORE)
    stages = (
        (own_stack, own_peer), (up_stack, up_peer), (over_stack, over_peer), (across_stack, across_peer, *last, *last_peer)
    )
    masks = [z + m + c for z in (0, 8, 16) for c in (0, 1) for m in (0, 2, 4, 6)] + [24, 26, 28, 25, 27, 29, 30, 31]
    dest = jnp.concatenate([by_mask[m] for m in masks])
    small = jnp.stack([small.reshape(16, -1), small_peer.reshape(16, -1)], axis=1).reshape(32, -1)
    number = jnp.arange(32, dtype=jnp.int32)
    hot = (number[None, :] == (number ^ device)[:, None]).astype(jnp.bfloat16)
    return stages, dest, fwd_mul(hot, small).astype(jnp.bfloat16)


def fwd_mul(left, right):
    return mm(left, right, ((1,), (0,)))


def outer(left, right):
    return mm(left, right, ((0,), (0,)))


def running(values):
    number = jnp.arange(values.shape[0], dtype=jnp.int32)
    return jnp.sum(jnp.where(number[None, :] <= number[:, None], values[None, :], 0), axis=1)


def block_rates(position, feature, out_fan):
    cut_one = 3 * feature * feature
    cut_two = cut_one + feature * feature
    cut_three = cut_two + 4 * feature * feature
    fans = (feature, out_fan, feature, 4 * feature)
    rates = [0.5 * fan ** (-0.5) for fan in fans]
    return jnp.where(
        position < cut_one,
        rates[0],
        jnp.where(position < cut_two, rates[1], jnp.where(position < cut_three, rates[2], rates[3])),
    ).astype(jnp.float32)


def adam_update(weight, gradient, first, second, rates, decay):
    first_new = beta_one * first + (1.0 - beta_one) * gradient
    second_new = beta_two * second + (1.0 - beta_two) * gradient * gradient
    corrected = first_new / (1.0 - beta_one**STEP)
    scaled = second_new / (1.0 - beta_two**STEP)
    weight_new = weight - rates * (corrected / (jnp.sqrt(scaled) + adam_eps) + decay * weight)
    return (weight_new, first_new, second_new)


def local(
    cells_in, lengths, sets_weights, rows_weights, norm_gains, sets_first, rows_first, gains_first,
    sets_second, rows_second, gains_second, out_grad,
):
    f32, bf = jnp.float32, jnp.bfloat16
    devices = lax.axis_size("dev")
    device = lax.axis_index("dev")
    slots, width = cells_in.shape
    feat = width // ATTRS
    per_peer = slots // devices
    rows_even = out_grad.shape[0]
    rows_pad = -(-rows_even // LANES) * LANES
    grid = devices == 32 and width == 1024 and slots == 384

    n_rows, n_gains = rows_weights.shape[0], norm_gains.shape[0]
    small = jnp.concatenate([rows_weights, norm_gains]).astype(bf)
    small = jnp.pad(small, (0, -small.shape[0] % 1024)).reshape(-1, 1024)
    shard = sets_weights.astype(bf).reshape(-1, width)
    if grid:
        stages, dest, small = gather_all(shard, small, device)
    else:
        small = lax.all_gather(small, "dev", axis=0, tiled=False)
        flat = lax.all_gather(shard, "dev", axis=0, tiled=True)
        parts = lambda v, n: v.reshape(width, n, width).transpose(1, 0, 2).reshape(n * width, width)
        flat = jnp.concatenate(
            [parts(flat[: 3 * width], 3), flat[3 * width : 4 * width], parts(flat[4 * width : 8 * width], 4), flat[8 * width :]]
        )
        stages, dest = ((flat,),), jnp.arange(12 * width // UNIT, dtype=jnp.int32)
    plane = device // 8 if grid else jnp.int32(0)
    runs = [(i * width, i * width, width) for i in range(12)]
    small = small.reshape(devices, -1)
    full_rows = small[:, :n_rows].reshape(-1)
    full_gains = small[:, n_rows : n_rows + n_gains].reshape(-1).astype(f32)
    square = feat * feat
    wq2 = full_rows[: 3 * square].reshape(feat, 3 * feat)
    wo2 = full_rows[3 * square : 4 * square].reshape(feat, feat)
    wu2 = full_rows[4 * square : 8 * square].reshape(feat, 4 * feat)
    wd2 = full_rows[8 * square :].reshape(4 * feat, feat)
    g1, g2 = full_gains[:width], full_gains[width : 2 * width]
    g3, g4 = full_gains[2 * width : 2 * width + feat], full_gains[2 * width + feat :]

    table = lengths.reshape(devices, SETS_DEV)
    own = lax.dynamic_index_in_dim(table, device, 0, keepdims=False)
    positions = jnp.arange(slots, dtype=jnp.int32)
    labels = jnp.sum((positions[:, None] >= running(own)[None, :]).astype(jnp.int32), axis=1)
    counts = jnp.sum(table, axis=1) // devices
    ends = running(counts)
    spot = jnp.arange(rows_pad, dtype=jnp.int32)
    past = (ends[None, :] <= spot[:, None]).astype(jnp.int32)
    start = jnp.sum(past * counts[None, :], axis=1)
    pick = jnp.where(spot < rows_even, jnp.sum(past, axis=1) * per_peer + spot - start, -1)

    flat, joined, a1, o1, a2, u1, slope, h1, leaving = forward_layer(
        per_peer, cells_in, g1, g2, labels, plane.reshape(1), stages, dest
    )

    swap = lambda v: lax.all_to_all(
        v.reshape(devices, -1, LANES), "dev", split_axis=0, concat_axis=0, tiled=True
    ).reshape(slots, width)
    og = jnp.pad(out_grad, ((0, rows_pad - rows_even), (0, 0)))
    rows_out, back, dq2, do2, du2, dd2, dg3, dg4 = rows_layer(
        pick, swap(leaving), og, wq2, wo2, wu2, wd2, g3, g4
    )
    rows_out = rows_out[:rows_even]
    raw = swap(back)

    core = device % 2
    which = core.reshape(1)
    half = width // 2
    pair = lambda v: (v, send(v, CORE))
    if grid:
        raw, *pairs = after(raw, *pair(u1), *pair(a2), *pair(o1), *pair(a1))
        u1, a2, o1, a1 = (tuple(pairs[i : i + 2]) for i in (0, 2, 4, 6))
    *dpre, dh1, low_own, low_peer, gz_own, gz_peer, dg2 = widen_back(runs, per_peer, which, raw, slope, h1, g2, flat)
    *dj, cells_grad, dg1 = attend_back(runs, which, dh1, cells_in, g1, joined, labels, flat)
    if grid:
        chip_runs = sorted_runs(2 * shard.shape[0])[1]
        swapped = lambda own, peer: (own, send(peer, CORE))
        many = u1 + swapped(gz_own, gz_peer) + a2 + swapped(*dpre) + o1 + swapped(low_own, low_peer)
        few = a1 + swapped(*dj)
        lanes = half // 2
        many_jobs, few_jobs = ((8, 4, True), (4, 4, False), (3, 1, True)), ((0, 3, False),)
        blocks = chip_outer(chip_runs, few_jobs, few, 0, lanes, (chip_outer(chip_runs, many_jobs, many, 0, lanes),))
        blocks, *operands = after(blocks, *many, *few)
        blocks = [blocks, chip_outer(chip_runs, many_jobs + few_jobs, tuple(operands), lanes, lanes)]
        blocks = [v.reshape(16, -1, lanes) for v in blocks]
        blocks[0], dq2, do2, du2, dd2, dg3, dg4 = after(blocks[0], dq2, do2, du2, dd2, dg3, dg4)
        sums = [sum_blocks(part, device // 2) for part in blocks]
        sets_grad = owned_rows(jnp.concatenate(sums, axis=1), device).reshape(-1)
    else:

        def sides(own, peer, n):
            both = jnp.where(core == 0, jnp.stack([own, peer]), jnp.stack([peer, own]))
            return both.reshape(2, slots, n, half).transpose(1, 2, 0, 3).reshape(slots, -1)

        dq1, du1 = outer(a1, sides(*dj, 3)), outer(a2, sides(*dpre, 4))
        gz = sides(gz_own, gz_peer, 1)
        full = jnp.concatenate([dq1.reshape(-1, width), outer(o1, dh1.astype(bf)), du1.reshape(-1, width), outer(u1, gz)])
        sets_grad = lax.psum_scatter(full.astype(bf), "dev", scatter_dimension=0, tiled=True).astype(f32).reshape(-1)

    rows_flat = jnp.concatenate([v.reshape(-1) for v in (*rows_order(dq2, do2), du2, dd2)])
    dg3, dg4 = jnp.sum(dg3, axis=1), jnp.sum(dg4, axis=1)
    gains = jnp.concatenate([dg1[0], dg2[0], dg3, dg4]).reshape(devices, n_gains)
    extra = jnp.concatenate([rows_flat.reshape(devices, n_rows), gains], axis=1).reshape(devices, 1, -1)
    extra = jnp.sum(lax.all_to_all(extra, "dev", split_axis=0, concat_axis=0, tiled=True), axis=(0, 1))
    rows_grad, gains_grad = extra[:n_rows], extra[n_rows:]

    set_index = device * sets_grad.shape[0] + jnp.arange(sets_grad.shape[0], dtype=jnp.int32)
    row_index = device * n_rows + jnp.arange(n_rows, dtype=jnp.int32)
    set_rates = block_rates(set_index, width, max(1, 3 * width // slots))
    row_rates = block_rates(row_index, feat, max(1, feat // 8))
    sets_new, sets_first_new, sets_second_new = adam_update(
        sets_weights, sets_grad, sets_first, sets_second, set_rates, decay_rate
    )
    rows_new, rows_first_new, rows_second_new = adam_update(
        rows_weights, rows_grad, rows_first, rows_second, row_rates, decay_rate
    )
    gains_new, gains_first_new, gains_second_new = adam_update(
        norm_gains, gains_grad, gains_first, gains_second, gain_rate, 0.0
    )
    return (
        rows_out, cells_grad, sets_grad, rows_grad, gains_grad, sets_new, rows_new, gains_new,
        sets_first_new, rows_first_new, gains_first_new, sets_second_new, rows_second_new, gains_second_new,
        sets_new.astype(bf), rows_new.astype(bf), gains_new.astype(bf),
    )


def solution(mesh):
    flat = P("dev")
    tall = P("dev", None)
    return jax.shard_map(
        local,
        mesh=mesh,
        in_specs=(tall, P()) + (flat,) * 9 + (tall,),
        out_specs=(tall, tall) + (flat,) * 15,
        check_vma=False,
    )
```

```python
import functools

import jax
import jax.numpy as jnp
import numpy as np
from jax import lax
from jax.experimental import pallas as pl
from jax.experimental.pallas import tpu as pltpu
from jax.sharding import PartitionSpec as P

ATTRS = 16
HEADS = 8
SETS_DEV = 2
STEP = 5
LANES = 128

norm_eps = 1e-05
beta_one = 0.5
beta_two = 0.5
adam_eps = 1e-08
decay_rate = 0.1
gain_rate = 0.5


BLOCK = 2


def mm(left, right, dims):
    return lax.dot_general(left, right, (dims, ((), ())), preferred_element_type=jnp.float32)


def gelu_pair(v):
    size = jnp.abs(v) * 0.7071067811865476
    t = 1.0 / (1.0 + 0.3275911 * size)
    bell = jnp.exp(-0.5 * v * v)
    poly = t * (0.254829592 + t * (-0.284496736 + t * (1.421413741 + t * (-1.453152027 + t * 1.061405429))))
    tail = 0.5 * poly * bell
    phi = jnp.where(v < 0.0, tail, 1.0 - tail)
    return v * phi, phi + v * (bell * 0.3989422804014327)


def rows_kernel(
    pick_ref, arrived_ref, og_ref, wq_ref, wqt_ref, wo_ref, wot_ref, wu_ref, wut_ref, wd_ref, wdt_ref, g3_ref, g4_ref,
    out_ref, back_ref, dwq_ref, dwo_ref, dwu_ref, dwd_ref, dg3_ref, dg4_ref,
    joined, prob, dscore, outs, douts, dj, back_acc,
):
    f32, bf = jnp.float32, jnp.bfloat16
    step = pl.program_id(0)
    last = pl.num_programs(0) - 1
    slots = arrived_ref.shape[0]
    scaling = HEADS ** (-0.5)
    feat = 64

    @pl.when(step == 0)
    def _():
        for ref in (dwq_ref, dwo_ref, dwu_ref, dwd_ref, dg3_ref, dg4_ref, back_acc):
            ref[...] = jnp.zeros_like(ref)

    source = lax.broadcasted_iota(jnp.int32, (slots, LANES), 0)
    hot = (source == pick_ref[0]).astype(f32).astype(bf)
    x_t = mm(arrived_ref[...], hot, ((0,), (0,)))

    def to_lanes(tall):
        return jnp.concatenate([tall[a * feat : (a + 1) * feat] for a in range(ATTRS)], axis=1)

    def to_tall(wide):
        return jnp.concatenate([wide[:, a * LANES : (a + 1) * LANES] for a in range(ATTRS)], axis=0)

    def norm(v):
        center = v - jnp.mean(v, axis=0, keepdims=True)
        root = lax.rsqrt(jnp.mean(center * center, axis=0, keepdims=True) + norm_eps)
        return center * root, root

    def norm_back(hat, root, gain, upstream):
        dhat = upstream * gain
        return root * (
            dhat - jnp.mean(dhat, axis=0, keepdims=True) - hat * jnp.mean(dhat * hat, axis=0, keepdims=True)
        )

    def fold(v):
        total = v[:, :LANES]
        for a in range(1, ATTRS):
            total = total + v[:, a * LANES : (a + 1) * LANES]
        return total

    x = to_lanes(x_t)
    g3, g4 = g3_ref[...], g4_ref[...]
    hat3, root3 = norm(x)
    a3 = (hat3 * g3).astype(bf)
    j_t = mm(wqt_ref[...], a3, ((1,), (0,))).astype(bf).astype(f32)
    for a in range(ATTRS):
        joined[a] = j_t[:, a * LANES : (a + 1) * LANES]

    def attend(n, carry):
        group = [n * BLOCK + i for i in range(BLOCK)]
        q = [[joined[a, d * 8 : d * 8 + 8] * scaling for d in range(8)] for a in group]
        scores = [[] for _ in group]
        for b in range(ATTRS):
            k = [joined[b, 64 + d * 8 : 72 + d * 8] for d in range(8)]
            for i in range(BLOCK):
                scores[i].append(functools.reduce(jnp.add, [q[i][d] * k[d] for d in range(8)]))
        inverse = []
        for i in range(BLOCK):
            peak = functools.reduce(jnp.maximum, scores[i])
            scores[i] = [jnp.exp(s - peak) for s in scores[i]]
            inverse.append(1.0 / functools.reduce(jnp.add, scores[i]))
        o = [[None] * 8 for _ in group]
        for b in range(ATTRS):
            v = [joined[b, 128 + d * 8 : 136 + d * 8] for d in range(8)]
            for i, a in enumerate(group):
                p = scores[i][b] * inverse[i]
                prob[a, b] = p
                p = p.astype(bf).astype(f32)
                for d in range(8):
                    o[i][d] = p * v[d] if b == 0 else o[i][d] + p * v[d]
        for i, a in enumerate(group):
            for d in range(8):
                outs[a, d * 8 : d * 8 + 8] = o[i][d]
        return carry

    lax.fori_loop(0, ATTRS // BLOCK, attend, 0, unroll=2)
    o = jnp.concatenate([outs[a] for a in range(ATTRS)], axis=1).astype(bf)
    h3 = x + mm(wot_ref[...], o, ((1,), (0,)))
    hat4, root4 = norm(h3)
    a4 = (hat4 * g4).astype(bf)
    pre = mm(wut_ref[...], a4, ((1,), (0,)))
    active, slope = gelu_pair(pre)
    u = active.astype(bf)
    y = h3 + mm(wdt_ref[...], u, ((1,), (0,)))
    out_ref[...] = to_tall(y).T.astype(bf)

    grad = to_lanes(og_ref[...].astype(f32).T)
    gz = grad.astype(bf)
    dwd_ref[...] += mm(u, gz, ((1,), (1,)))
    dpre = (slope * mm(wd_ref[...], gz, ((1,), (0,)))).astype(bf)
    dwu_ref[...] += mm(a4, dpre, ((1,), (1,)))
    da4 = mm(wu_ref[...], dpre, ((1,), (0,)))
    dg4_ref[...] += fold(da4 * hat4)
    dh3 = grad + norm_back(hat4, root4, g4, da4)

    gz = dh3.astype(bf)
    dwo_ref[...] += mm(o, gz, ((1,), (1,)))
    do = mm(wo_ref[...], gz, ((1,), (0,))).astype(bf).astype(f32)
    for a in range(ATTRS):
        douts[a] = do[:, a * LANES : (a + 1) * LANES]

    def spread(n, carry):
        group = [n * BLOCK + i for i in range(BLOCK)]
        up = [[douts[a, d * 8 : d * 8 + 8] for d in range(8)] for a in group]
        dot, slopes = [None] * BLOCK, [[] for _ in group]
        for b in range(ATTRS):
            v = [joined[b, 128 + d * 8 : 136 + d * 8] for d in range(8)]
            for i, a in enumerate(group):
                s = functools.reduce(jnp.add, [up[i][d] * v[d] for d in range(8)])
                slopes[i].append(s)
                term = prob[a, b] * s
                dot[i] = term if b == 0 else dot[i] + term
        dq = [[None] * 8 for _ in group]
        for b in range(ATTRS):
            k = [joined[b, 64 + d * 8 : 72 + d * 8] for d in range(8)]
            for i, a in enumerate(group):
                ds = (prob[a, b] * (slopes[i][b] - dot[i])).astype(bf).astype(f32) * scaling
                dscore[a, b] = ds
                for d in range(8):
                    dq[i][d] = ds * k[d] if b == 0 else dq[i][d] + ds * k[d]
        for i, a in enumerate(group):
            for d in range(8):
                dj[a, d * 8 : d * 8 + 8] = dq[i][d]
        return carry

    lax.fori_loop(0, ATTRS // BLOCK, spread, 0, unroll=2)

    def collect(n, carry):
        group = [n * BLOCK + i for i in range(BLOCK)]
        dk, dv = [[None] * 8 for _ in group], [[None] * 8 for _ in group]
        for a in range(ATTRS):
            q = [joined[a, d * 8 : d * 8 + 8] for d in range(8)]
            up = [douts[a, d * 8 : d * 8 + 8] for d in range(8)]
            for i, b in enumerate(group):
                ds = dscore[a, b]
                p = prob[a, b].astype(bf).astype(f32)
                for d in range(8):
                    dk[i][d] = ds * q[d] if a == 0 else dk[i][d] + ds * q[d]
                    dv[i][d] = p * up[d] if a == 0 else dv[i][d] + p * up[d]
        for i, b in enumerate(group):
            for d in range(8):
                dj[b, 64 + d * 8 : 72 + d * 8] = dk[i][d]
                dj[b, 128 + d * 8 : 136 + d * 8] = dv[i][d]
        return carry

    lax.fori_loop(0, ATTRS // BLOCK, collect, 0, unroll=2)
    djl = jnp.concatenate([dj[a] for a in range(ATTRS)], axis=1).astype(bf)
    dwq_ref[...] += mm(a3, djl, ((1,), (1,)))
    da3 = mm(wq_ref[...], djl, ((1,), (0,)))
    dg3_ref[...] += fold(da3 * hat3)
    dhc = to_tall(dh3 + norm_back(hat3, root3, g3, da3)).astype(bf)
    back_acc[...] += mm(hot, dhc, ((1,), (1,)))

    @pl.when(step == last)
    def _():
        back_ref[...] = back_acc[...].astype(bf)


def rows_layer(pick, arrived, og, wq, wo, wu, wd, g3, g4):
    f32, bf = jnp.float32, jnp.bfloat16
    total, width = og.shape
    slots = arrived.shape[0]
    steps = total // LANES
    feat = 64
    wqp = wq.reshape(feat, 3, HEADS, 8).transpose(0, 1, 3, 2).reshape(feat, 3 * feat)
    wop = wo.reshape(HEADS, 8, feat).transpose(1, 0, 2).reshape(feat, feat)
    whole = lambda *shape: pl.BlockSpec(shape, lambda t: (0,) * len(shape))
    outs = pl.pallas_call(
        rows_kernel,
        grid=(steps,),
        in_specs=[
            pl.BlockSpec((1, 1, LANES), lambda t: (t, 0, 0)),
            whole(slots, width),
            pl.BlockSpec((LANES, width), lambda t: (t, 0)),
            whole(feat, 192), whole(192, feat), whole(feat, feat), whole(feat, feat),
            whole(feat, 256), whole(256, feat), whole(256, feat), whole(feat, 256),
            whole(feat, 1), whole(feat, 1),
        ],
        out_specs=[
            pl.BlockSpec((LANES, width), lambda t: (t, 0)),
            whole(slots, width),
            whole(feat, 192), whole(feat, feat), whole(feat, 256), whole(256, feat),
            whole(feat, LANES), whole(feat, LANES),
        ],
        out_shape=[
            jax.ShapeDtypeStruct((total, width), bf),
            jax.ShapeDtypeStruct((slots, width), bf),
            jax.ShapeDtypeStruct((feat, 192), f32),
            jax.ShapeDtypeStruct((feat, feat), f32),
            jax.ShapeDtypeStruct((feat, 256), f32),
            jax.ShapeDtypeStruct((256, feat), f32),
            jax.ShapeDtypeStruct((feat, LANES), f32),
            jax.ShapeDtypeStruct((feat, LANES), f32),
        ],
        scratch_shapes=[
            pltpu.VMEM((ATTRS, 192, LANES), f32),
            pltpu.VMEM((ATTRS, ATTRS, 8, LANES), f32),
            pltpu.VMEM((ATTRS, ATTRS, 8, LANES), f32),
            pltpu.VMEM((ATTRS, 64, LANES), f32),
            pltpu.VMEM((ATTRS, 64, LANES), f32),
            pltpu.VMEM((ATTRS, 192, LANES), f32),
            pltpu.VMEM((slots, width), f32),
        ],
        compiler_params=pltpu.CompilerParams(vmem_limit_bytes=56 * 2**20),
    )(
        pick.reshape(steps, 1, LANES), arrived, og,
        wqp, wqp.T, wop, wop.T, wu, wu.T, wd, wd.T, g3.reshape(feat, 1), g4.reshape(feat, 1),
    )
    return outs


def rows_order(dwqp, dwop):
    feat = dwop.shape[0]
    dwq = dwqp.reshape(feat, 3, 8, HEADS).transpose(0, 1, 3, 2).reshape(feat, 3 * feat)
    return dwq, dwop.reshape(8, HEADS, feat).transpose(1, 0, 2).reshape(feat, feat)


UNIT = 32


def placed(flat):
    if flat < 3072:
        return flat % 3 * 1024 + flat // 3
    if flat < 4096 or flat >= 8192:
        return flat
    return 4096 + flat % 4 * 1024 + (flat - 4096) // 4


def sorted_runs(per):
    orders, runs = [], []
    for first in range(0, 12288, per):
        places = [placed(first + i) for i in range(per)]
        order = sorted(range(per), key=lambda i: places[i])
        orders.append(order)
        for at, i in enumerate(order):
            if at and places[i] == runs[-1][1] + runs[-1][2] and places[i] % 1024:
                runs[-1][2] += 1
            else:
                runs.append([first + at, places[i], 1])
    return np.array(orders, np.int32), sorted((tuple(run) for run in runs), key=lambda run: run[1])


class Copies:
    def __init__(self, sems):
        self.sems, self.used = sems, 0

    def start(self, src, dst):
        copy = pltpu.make_async_copy(src, dst, self.sems.at[self.used])
        copy.start()
        self.used += 1
        return copy

    def rows(self, src, dst, parts=4):
        count = src.shape[0] // parts
        cuts = [pl.ds(i * count, count) for i in range(parts)]
        return [self.start(src.at[cut], dst.at[cut]) for cut in cuts]


def wait(copies):
    for copy in copies:
        copy.wait()


def load_mats(copies, runs, flat_ref, held, first, width):
    groups = [[] for _ in range(held.shape[0] // width)]
    for src, dst, rows in runs:
        i = dst // width - first
        if 0 <= i < len(groups):
            groups[i].append(copies.start(flat_ref.at[pl.ds(src, rows)], held.at[pl.ds(dst - first * width, rows)]))
    return groups


def low_norm(v, gain):
    center = v - jnp.mean(v, axis=1, keepdims=True)
    root = lax.rsqrt(jnp.mean(center * center, axis=1, keepdims=True) + norm_eps)
    return (center * root * gain).astype(jnp.bfloat16)


def pull_norm(v, gain, upstream):
    center = v - jnp.mean(v, axis=1, keepdims=True)
    root = lax.rsqrt(jnp.mean(center * center, axis=1, keepdims=True) + norm_eps)
    hat = center * root
    dhat = upstream * gain
    inner = jnp.mean(dhat * hat, axis=1, keepdims=True)
    grad = root * (dhat - jnp.mean(dhat, axis=1, keepdims=True) - hat * inner)
    return grad, jnp.sum(upstream * hat, axis=0, keepdims=True)


def forward_kernel(counts, turn, plane_ref, dest_ref, g1_ref, g2_ref, tall_ref, wide_ref, h0_ref, *refs):
    stages = []
    for count in counts:
        stages.append(refs[:count])
        refs = refs[count:]
    forward_body(turn, plane_ref, dest_ref, g1_ref, g2_ref, tall_ref, wide_ref, h0_ref, stages, *refs)


def forward_body(turn, plane_ref, dest_ref, g1_ref, g2_ref, tall_ref, wide_ref, h0_ref, stages,
                   big_out, joined_out, a1_out, o1_out, a2_out, u1_out, slope_out, h1_out, leave_out,
                   mats, bias, h0, joined, a1, o1, a2, u1, slope, h1, leave, load_sems, plane_sems, store_sems):
    f32, bf = jnp.float32, jnp.bfloat16
    slots, width = h0.shape
    head = width // HEADS
    tile = 512
    loads, stores = Copies(load_sems), Copies(store_sems)
    first = loads.rows(h0_ref, h0)
    part = mats.shape[0] // len(stages)

    def load_stage(s, plane):
        number = sum(piece.shape[0] for pieces in stages[:s] for piece in pieces) // UNIT
        for piece in stages[s]:
            for u in range(piece.shape[0] // UNIT):
                place = pl.multiple_of(dest_ref[number] * UNIT, UNIT)
                number += 1
                pltpu.make_async_copy(
                    piece.at[pl.ds(u * UNIT, UNIT)], mats.at[pl.ds(place, UNIT)], plane_sems.at[plane]
                ).start()

    for plane in range(len(stages)):
        for s in range(len(stages)):
            pl.when(plane_ref[0] ^ s == plane)(functools.partial(load_stage, s, plane))

    def arrived(plane):
        rows = mats.at[pl.ds(plane * part, part)]
        pltpu.make_async_copy(rows, rows, plane_sems.at[plane]).wait()

    saves = []
    bias[...] = jnp.where(tall_ref[...] == wide_ref[...], 0.0, -jnp.inf)
    wait(first)
    a1[...] = low_norm(h0[...].astype(f32), g1_ref[...])
    saves += stores.rows(a1, a1_out)
    for plane in range(len(stages) if len(stages) < 4 else 1):
        arrived(plane)
    for i in range(3):
        for t in range(width // tile):
            cols = slice(i * width + t * tile, i * width + (t + 1) * tile)
            joined[:, cols] = mm(a1[...], mats[i * width : (i + 1) * width, t * tile : (t + 1) * tile], ((1,), (0,))).astype(bf)
    saves += stores.rows(joined, joined_out)
    saves += stores.rows(mats.at[pl.ds(0, 3 * width)], big_out.at[pl.ds(0, 3 * width)], 3)

    def attend(h, carry):
        part = lambda i: joined[:, pl.ds(pl.multiple_of(i * width + h * head, head), head)]
        scores = mm(part(0), part(1), ((1,), (1,))) * head ** (-0.5) + bias[...]
        weights = jnp.exp(scores - jnp.max(scores, axis=1, keepdims=True))
        chance = weights * (1.0 / jnp.sum(weights, axis=1, keepdims=True))
        o1[:, pl.ds(pl.multiple_of(h * head, head), head)] = mm(chance.astype(bf), part(2), ((1,), (0,))).astype(bf)
        return carry

    lax.fori_loop(0, HEADS, attend, 0, unroll=2)
    saves += stores.rows(o1, o1_out)
    if len(stages) == 4:
        arrived(1)
    for t in range(width // tile):
        cols = slice(t * tile, (t + 1) * tile)
        h1[:, cols] = h0[:, cols].astype(f32) + mm(o1[...], mats[3 * width : 4 * width, cols], ((1,), (0,)))
    saves += stores.rows(h1, h1_out)
    a2[...] = low_norm(h1[...], g2_ref[...])
    saves += stores.rows(a2, a2_out)
    if len(stages) == 4:
        arrived(2)
    for i in range(4):
        for t in range(width // tile):
            cols = slice(t * tile, (t + 1) * tile)
            active, rise = gelu_pair(mm(a2[...], mats[(4 + i) * width : (5 + i) * width, cols], ((1,), (0,))))
            cols = slice(i * width + t * tile, i * width + (t + 1) * tile)
            u1[:, cols] = active.astype(bf)
            slope[:, cols] = rise.astype(bf)
            saves.append(stores.start(u1.at[:, cols], u1_out.at[:, cols]))
            saves.append(stores.start(slope.at[:, cols], slope_out.at[:, cols]))
    if len(stages) == 4:
        arrived(3)
    saves += stores.rows(mats.at[pl.ds(3 * width, 9 * width)], big_out.at[pl.ds(3 * width, 9 * width)], 9)
    to, source = (lax.broadcasted_iota(jnp.int32, (slots, slots), axis) for axis in (0, 1))
    hot = (source == to % turn * (slots // turn) + to // turn).astype(f32).astype(bf)
    for t in range(width // tile):
        cols = slice(t * tile, (t + 1) * tile)
        h2 = (h1[:, cols] + mm(u1[...], mats[8 * width :, cols], ((1,), (0,)))).astype(bf)
        leave[:, cols] = mm(hot, h2, ((1,), (0,))).astype(bf)
        saves.append(stores.start(leave.at[:, cols], leave_out.at[:, cols]))
    wait(saves)


def own_kernel(kernel, operands, small, outs, scratch, limit, flops):
    def spec(v):
        space = pltpu.SMEM if v.ndim == 1 else pltpu.VMEM
        return pl.BlockSpec(memory_space=space)

    anywhere = pl.BlockSpec(memory_space=pl.ANY)
    tiny = pl.BlockSpec(memory_space=pltpu.VMEM)
    return pl.pallas_call(
        kernel,
        in_specs=[spec(v) if n in small else anywhere for n, v in enumerate(operands)],
        out_specs=[tiny if out.shape[0] == 1 else anywhere for out in outs],
        out_shape=outs,
        scratch_shapes=scratch,
        compiler_params=pltpu.CompilerParams(vmem_limit_bytes=limit * 2**20),
        cost_estimate=pl.CostEstimate(flops=flops, bytes_accessed=40 * 2**20, transcendentals=10**6),
    )(*operands)


def forward_layer(turn, h0, g1, g2, labels, plane, stages, dest):
    f32, bf = jnp.float32, jnp.bfloat16
    slots, width = h0.shape
    shape, vmem = jax.ShapeDtypeStruct, pltpu.VMEM
    sizes = [(3, bf), (1, bf), (1, bf), (1, bf), (4, bf), (4, bf), (1, f32), (1, bf)]
    mats = (12 * width, width)
    return own_kernel(
        functools.partial(forward_kernel, tuple(len(pieces) for pieces in stages), turn),
        (plane, dest, g1.reshape(1, -1), g2.reshape(1, -1), labels.reshape(-1, 1), labels.reshape(1, -1), h0, *sum(stages, ())),
        (0, 1, 2, 3, 4, 5),
        [shape(mats, bf)] + [shape((slots, n * width), kind) for n, kind in sizes],
        [vmem(mats, bf), vmem((slots, slots), f32), vmem((slots, width), bf)]
        + [vmem((slots, n * width), kind) for n, kind in sizes]
        + [pltpu.SemaphoreType.DMA((4,)), pltpu.SemaphoreType.DMA((len(stages),)), pltpu.SemaphoreType.DMA((50,))],
        60,
        10**10,
    )


def widen_back_kernel(runs, turn, core_ref, g2_ref, raw_ref, slope_ref, h1_ref, flat_ref,
                      dpre_own, dpre_peer, dh_out, low_own, low_peer, gz_own, gz_peer, dg_ref,
                      ups, downs, raw, gz, slope, h1, dpre, dh, low, gz_sides, da, load_sems, store_sems):
    f32, bf = jnp.float32, jnp.bfloat16
    width = gz.shape[1]
    half = width // 2
    core = core_ref[0]
    loads, stores = Copies(load_sems), Copies(store_sems)
    raw_copies = loads.rows(raw_ref, raw)
    down_copies, slope_copies, up_copies = [], [], []
    for i in range(4):
        part, cols = pl.ds(i * width, width), pl.ds(i * width, width)
        down_copies += load_mats(loads, runs, flat_ref, downs.at[part], 8 + i, width)
        slope_copies.append(loads.start(slope_ref.at[:, cols], slope.at[:, cols]))
        up_copies += load_mats(loads, runs, flat_ref, ups.at[part], 4 + i, width)
    h1_copies = loads.rows(h1_ref, h1)
    wait(raw_copies)
    slots = gz.shape[0]
    slot, source = (lax.broadcasted_iota(jnp.int32, (slots, slots), axis) for axis in (0, 1))
    devices = slots // turn
    hot = (source == slot % devices * turn + slot // devices).astype(f32).astype(bf)
    gz[...] = mm(hot, raw[...], ((1,), (0,))).astype(bf)
    saves = []
    for s in range(2):
        gz_sides[s ^ core] = gz[:, s * half : (s + 1) * half]
    saves += [stores.start(gz_sides.at[0], gz_own), stores.start(gz_sides.at[1], gz_peer)]
    for i in range(4):
        wait(down_copies[i] + [slope_copies[i]] + up_copies[i])
        for s in range(2):
            hidden = slice(i * width + s * half, i * width + (s + 1) * half)
            du = mm(gz[...], downs[hidden], ((1,), (1,)))
            piece = (slope[:, hidden].astype(f32) * du).astype(bf)
            dpre[s ^ core, :, i * half : (i + 1) * half] = piece
            term = mm(piece, ups[i * width : (i + 1) * width, s * half : (s + 1) * half], ((1,), (1,)))
            da[...] = term if i == s == 0 else da[...] + term
        lanes = pl.ds(i * half, half)
        saves += [stores.start(dpre.at[0, :, lanes], dpre_own.at[:, lanes]), stores.start(dpre.at[1, :, lanes], dpre_peer.at[:, lanes])]
    wait(h1_copies)
    grad, dg_ref[...] = pull_norm(h1[...], g2_ref[...], da[...])
    dh[...] = gz[...].astype(f32) + grad
    saves += stores.rows(dh, dh_out)
    for s in range(2):
        low[s ^ core] = dh[:, s * half : (s + 1) * half].astype(bf)
    saves += [stores.start(low.at[0], low_own), stores.start(low.at[1], low_peer)]
    wait(saves)


def widen_back(runs, turn, core, raw, slope, h1, g2, flat):
    f32, bf = jnp.float32, jnp.bfloat16
    slots, width = raw.shape
    half = width // 2
    shape, vmem = jax.ShapeDtypeStruct, pltpu.VMEM
    side = shape((slots, half), bf)
    ups = sum(4 <= dst // width < 12 for _, dst, _ in runs)
    return own_kernel(
        functools.partial(widen_back_kernel, runs, turn),
        (core, g2.reshape(1, -1), raw, slope, h1, flat),
        (0, 1),
        [shape((slots, 2 * width), bf)] * 2 + [shape((slots, width), f32)] + [side] * 4 + [shape((1, width), f32)],
        [
            vmem((4 * width, width), bf), vmem((4 * width, width), bf), vmem((slots, width), bf), vmem((slots, width), bf),
            vmem((slots, 4 * width), bf),
            vmem((slots, width), f32), vmem((2, slots, 2 * width), bf), vmem((slots, width), f32), vmem((2, slots, half), bf),
            vmem((2, slots, half), bf), vmem((slots, width), f32),
            pltpu.SemaphoreType.DMA((ups + 12,)), pltpu.SemaphoreType.DMA((16,)),
        ],
        60,
        64 * 10**8,
    )


def attend_back_kernel(runs, core_ref, g1_ref, tall_ref, wide_ref, dh_ref, h0_ref, joined_ref, flat_ref,
                       own_out, peer_out, grad_out, dg_ref,
                       mats, bias, dh, h0, joined, dblend, dj, sides, load_sems, store_sems):
    f32, bf = jnp.float32, jnp.bfloat16
    slots, width = dh.shape
    head = width // HEADS
    half = width // 2
    tile = 512
    scaling = head ** (-0.5)
    core = core_ref[0]
    loads, stores = Copies(load_sems), Copies(store_sems)
    dh_copies = loads.rows(dh_ref, dh)
    out_copies = load_mats(loads, runs, flat_ref, mats.at[pl.ds(3 * width, width)], 3, width)
    joined_copies = loads.rows(joined_ref, joined)
    mat_copies = load_mats(loads, runs, flat_ref, mats.at[pl.ds(0, 3 * width)], 0, width)
    h0_copies = loads.rows(h0_ref, h0)
    bias[...] = jnp.where(tall_ref[...] == wide_ref[...], 0.0, -jnp.inf)
    wait(dh_copies)
    gz = dh[...].astype(bf)
    wait(out_copies[0])
    for t in range(width // tile):
        rows = slice(3 * width + t * tile, 3 * width + (t + 1) * tile)
        dblend[:, t * tile : (t + 1) * tile] = mm(gz, mats[rows], ((1,), (1,))).astype(bf)
    wait(joined_copies)

    def attend(h, carry):
        lanes = lambda i: pl.ds(pl.multiple_of(i * width + h * head, head), head)
        q, k, v = (joined[:, lanes(i)] for i in range(3))
        do = dblend[:, pl.ds(pl.multiple_of(h * head, head), head)]
        scores = mm(q, k, ((1,), (1,))) * scaling + bias[...]
        weights = jnp.exp(scores - jnp.max(scores, axis=1, keepdims=True))
        chance = weights * (1.0 / jnp.sum(weights, axis=1, keepdims=True))
        dchance = mm(do, v, ((1,), (1,)))
        dot = jnp.sum(chance * dchance, axis=1, keepdims=True)
        ds = (chance * (dchance - dot)).astype(bf)
        parts = (
            mm(ds, k, ((1,), (0,))) * scaling,
            mm(ds, q, ((0,), (0,))) * scaling,
            mm(chance.astype(bf), do, ((0,), (0,))),
        )
        per_side = HEADS // 2
        for i in range(3):
            part = parts[i].astype(bf)
            dj[:, lanes(i)] = part
            sides[(h // per_side) ^ core, :, pl.ds(pl.multiple_of(i * half + h % per_side * head, head), head)] = part
        return carry

    lax.fori_loop(0, HEADS, attend, 0, unroll=2)
    saves = [stores.start(sides.at[1], peer_out), stores.start(sides.at[0], own_out)]
    da = None
    for i in range(3):
        wait(mat_copies[i])
        term = mm(dj[:, i * width : (i + 1) * width], mats[i * width : (i + 1) * width], ((1,), (1,)))
        da = term if da is None else da + term
    wait(h0_copies)
    grad, dg_ref[...] = pull_norm(h0[...].astype(f32), g1_ref[...], da)
    dh[...] = dh[...] + grad
    wait(saves + stores.rows(dh, grad_out))


def attend_back(runs, core, dh, h0, g1, joined, labels, flat):
    f32, bf = jnp.float32, jnp.bfloat16
    slots, width = dh.shape
    shape, vmem = jax.ShapeDtypeStruct, pltpu.VMEM
    mats = sum(dst // width < 4 for _, dst, _ in runs)
    return own_kernel(
        functools.partial(attend_back_kernel, runs),
        (core, g1.reshape(1, -1), labels.reshape(-1, 1), labels.reshape(1, -1), dh, h0, joined, flat),
        (0, 1, 2, 3),
        [shape((slots, 3 * width // 2), bf)] * 2 + [shape((slots, width), f32), shape((1, width), f32)],
        [
            vmem((4 * width, width), bf), vmem((slots, slots), f32), vmem((slots, width), f32), vmem((slots, width), bf),
            vmem((slots, 3 * width), bf), vmem((slots, width), bf), vmem((slots, 3 * width), bf),
            vmem((2, slots, 3 * width // 2), bf),
            pltpu.SemaphoreType.DMA((mats + 12,)), pltpu.SemaphoreType.DMA((6,)),
        ],
        60,
        64 * 10**8,
    )


def chip_outer_kernel(runs, jobs, *refs):
    bf = jnp.bfloat16
    count = 4 * len(jobs)
    operands, refs = refs[:count], refs[-(count + 5) :]
    outs, held, (result, load_sems, store_sems) = refs[:2], refs[2 : count + 2], refs[count + 2 :]
    loads, stores = Copies(load_sems), Copies(store_sems)
    arrivals = [loads.rows(ref, v, 2) for ref, v in zip(operands, held, strict=True)]
    width, half = 1024, result.shape[1]
    tile = 512
    saves, done = [], 0
    for n, (first, matrices, tall) in enumerate(jobs):
        left, left_peer, right, right_peer = held[4 * n : 4 * n + 4]
        for copies in arrivals[4 * n : 4 * n + 4]:
            wait(copies)
        for i in range(matrices):
            lanes = slice(0, half) if tall else slice(i * half, (i + 1) * half)
            for t in range(width // tile):
                cols = (i if tall else 0) * width + t * tile
                cols = slice(cols, cols + tile)
                term = mm(left[:, cols], right[:, lanes], ((0,), (0,))) + mm(left_peer[:, cols], right_peer[:, lanes], ((0,), (0,)))
                result[done * width + t * tile : done * width + (t + 1) * tile, :] = term.astype(bf)
            for to, place, rows in runs:
                if place // width == first + i:
                    for side, out in enumerate(outs):
                        part = result.at[pl.ds(done * width + place % width, rows), pl.ds(side * half // 2, half // 2)]
                        saves.append(stores.start(part, out.at[pl.ds(to, rows)]))
            done += 1
    wait(saves)


def chip_outer(runs, jobs, operands, half, onto=()):
    bf = jnp.bfloat16
    anywhere = pl.BlockSpec(memory_space=pl.ANY)
    matrices = [first + i for first, n, _ in jobs for i in range(n)]
    saves = 2 * sum(place // 1024 in matrices for _, place, _ in runs)
    return pl.pallas_call(
        functools.partial(chip_outer_kernel, runs, jobs),
        in_specs=[anywhere] * (len(operands) + len(onto)),
        out_specs=[anywhere] * 2,
        out_shape=[jax.ShapeDtypeStruct((12288, half // 2), bf)] * 2,
        input_output_aliases={len(operands) + i: i for i in range(len(onto))},
        scratch_shapes=[pltpu.VMEM(v.shape, bf) for v in operands]
        + [
            pltpu.VMEM((len(matrices) * 1024, half), bf),
            pltpu.SemaphoreType.DMA((2 * len(operands),)),
            pltpu.SemaphoreType.DMA((saves,)),
        ],
        compiler_params=pltpu.CompilerParams(vmem_limit_bytes=60 * 2**20),
        cost_estimate=pl.CostEstimate(
            flops=len(matrices) * 8 * 10**8, bytes_accessed=len(matrices) * 3 * 2**20, transcendentals=0
        ),
    )(*operands, *onto)


CORE = 1


def send(v, bit):
    return lax.ppermute(v, "dev", [(d, d ^ bit) for d in range(32)])


def after(*values):
    return lax.optimization_barrier(values)


def sum_blocks(blocks, chip):
    f32, bf = jnp.float32, jnp.bfloat16
    half = blocks.shape[1] // 2
    block = lambda m: lax.dynamic_index_in_dim(blocks, chip ^ (m >> 1), 0, keepdims=False)
    total = lambda *parts: sum(part.astype(f32) for part in parts)
    both = lambda one, two: jnp.concatenate([one.astype(bf), two.astype(bf)])

    across_far, up_far, across = block(30), block(14), block(24)
    a, b, c, d, e = after(
        send(across_far[:half], 4), send(across_far[half:], 2), send(across, 8), send(up_far[:half], 4), send(up_far[half:], 2)
    )
    side, other = block(26), block(28)
    across_x, across_y = both(total(side[:half], a), side[half:]), both(other[:half], total(other[half:], b))
    side, other = block(10), block(12)
    up_x, up_y = both(total(side[:half], d), side[half:]), both(other[:half], total(other[half:], e))
    over = total(block(16), c)

    a, b, c = after(send(across_x, 8), send(up_x, 2), send(up_y, 4))
    over_x, up = total(block(18), a), total(block(8), b, c).astype(bf)
    over_far, own_far = block(22), block(6)
    a, b, c, d, e = after(
        send(across_y, 8), send(over_far[:half], 4), send(over_far[half:], 2), send(own_far[:half], 4), send(own_far[half:], 2)
    )
    other = total(block(20), a)
    over_x, over_y = both(total(over_x[:half], b), over_x[half:]), both(other[:half], total(other[half:], c))
    side, other = block(2), block(4)
    own_x, own_y = both(total(side[:half], d), side[half:]), both(other[:half], total(other[half:], e))

    a, b, c = after(send(over_x, 2), send(over_y, 4), send(up, 8))
    own = total(block(0), c)
    over = total(over, a, b).astype(bf)
    return total(own, send(over, 16), send(own_x, 2), send(own_y, 4))


def owned_rows(own, device):
    core, chip = device % 2, device // 2
    half = own.shape[0] // 2
    orders, _ = sorted_runs(2 * half)
    order = lax.dynamic_index_in_dim(jnp.asarray(np.argsort(orders, axis=1).astype(np.int32)), chip, 0, keepdims=False)
    own = jnp.take(own, order, axis=0)
    mine = lax.dynamic_slice_in_dim(own, core * half, half, 0)
    peer = send(lax.dynamic_slice_in_dim(own, (1 - core) * half, half, 0), CORE)
    return jnp.where(core == 0, jnp.concatenate([mine, peer], axis=1), jnp.concatenate([peer, mine], axis=1))


def gather_all(shard, small, device):
    per = shard.shape[0]
    half, extra = per // 2, small.shape[0]
    orders, runs = sorted_runs(per)
    order = lax.dynamic_index_in_dim(jnp.asarray(orders), device, 0, keepdims=False)
    hot = (order[:, None] == jnp.arange(per, dtype=jnp.int32)[None, :]).astype(jnp.bfloat16)
    own = jnp.concatenate([fwd_mul(hot, shard).astype(jnp.bfloat16), small])
    table = np.zeros((32 * per // UNIT,), np.int32)
    for src, dst, rows in runs:
        table[src // UNIT : (src + rows) // UNIT] = range(dst // UNIT, (dst + rows) // UNIT)
    by_mask = jnp.take(jnp.asarray(table.reshape(32, -1)), device ^ jnp.arange(32, dtype=jnp.int32), axis=0)
    stack = lambda *parts: jnp.concatenate([part[:per] for part in parts])

    own, own_x, own_y, up = after(own, send(own, 2), send(own, 4), send(own, 8))
    a, b, up_x, up_y, over = after(
        send(own_x[:half], 4), send(own_y[half:], 2), send(up, 2), send(up, 4), send(own, 16)
    )
    own_far = jnp.concatenate([a, b])
    own_stack = stack(own, own_x, own_y, own_far)
    a, b, over_x, over_y, across, own_stack = after(
        send(up_x[:half], 4), send(up_y[half:], 2), send(over, 2), send(over, 4), send(over, 8), own_stack
    )
    up_far = jnp.concatenate([a, b])
    up_stack = stack(up, up_x, up_y, up_far)
    over_far, across_x, across_y, own_peer, up_peer = after(
        send(over_y, 2), send(over_x, 8), send(across, 4), send(own_stack, CORE), send(up_stack, CORE)
    )
    a, b, over_far = after(across_x[:half], across_y[half:], over_far)
    over_stack, across_stack = stack(over, over_x, over_y, over_far), stack(across, across_x, across_y)
    a, b, over_peer, across_peer = after(send(a, 4), send(b, 2), send(over_stack, CORE), send(across_stack, CORE))
    plane = (own, own_x, own_y, own_far, up, up_x, up_y, up_far, over, over_x, over_y, over_far, across, across_x, across_y)
    small = jnp.concatenate([v[per:] for v in plane] + [b[per - half :]])
    last = (a, b[: per - half])
    last_peer, small_peer = tuple(send(v, CORE) for v in last), send(small, CORE)
    stages = (
        (own_stack, own_peer), (up_stack, up_peer), (over_stack, over_peer), (across_stack, across_peer, *last, *last_peer)
    )
    masks = [z + m + c for z in (0, 8, 16) for c in (0, 1) for m in (0, 2, 4, 6)] + [24, 26, 28, 25, 27, 29, 30, 31]
    dest = jnp.concatenate([by_mask[m] for m in masks])
    small = jnp.stack([small.reshape(16, -1), small_peer.reshape(16, -1)], axis=1).reshape(32, -1)
    number = jnp.arange(32, dtype=jnp.int32)
    hot = (number[None, :] == (number ^ device)[:, None]).astype(jnp.bfloat16)
    return stages, dest, fwd_mul(hot, small).astype(jnp.bfloat16)


def fwd_mul(left, right):
    return mm(left, right, ((1,), (0,)))


def outer(left, right):
    return mm(left, right, ((0,), (0,)))


def running(values):
    number = jnp.arange(values.shape[0], dtype=jnp.int32)
    return jnp.sum(jnp.where(number[None, :] <= number[:, None], values[None, :], 0), axis=1)


def block_rates(position, feature, out_fan):
    cut_one = 3 * feature * feature
    cut_two = cut_one + feature * feature
    cut_three = cut_two + 4 * feature * feature
    fans = (feature, out_fan, feature, 4 * feature)
    rates = [0.5 * fan ** (-0.5) for fan in fans]
    return jnp.where(
        position < cut_one,
        rates[0],
        jnp.where(position < cut_two, rates[1], jnp.where(position < cut_three, rates[2], rates[3])),
    ).astype(jnp.float32)


def adam_update(weight, gradient, first, second, rates, decay):
    first_new = beta_one * first + (1.0 - beta_one) * gradient
    second_new = beta_two * second + (1.0 - beta_two) * gradient * gradient
    corrected = first_new / (1.0 - beta_one**STEP)
    scaled = second_new / (1.0 - beta_two**STEP)
    weight_new = weight - rates * (corrected / (jnp.sqrt(scaled) + adam_eps) + decay * weight)
    return (weight_new, first_new, second_new)


def local(
    cells_in, lengths, sets_weights, rows_weights, norm_gains, sets_first, rows_first, gains_first,
    sets_second, rows_second, gains_second, out_grad,
):
    f32, bf = jnp.float32, jnp.bfloat16
    devices = lax.axis_size("dev")
    device = lax.axis_index("dev")
    slots, width = cells_in.shape
    feat = width // ATTRS
    per_peer = slots // devices
    rows_even = out_grad.shape[0]
    rows_pad = -(-rows_even // LANES) * LANES
    grid = devices == 32 and width == 1024 and slots == 384

    n_rows, n_gains = rows_weights.shape[0], norm_gains.shape[0]
    small = jnp.concatenate([rows_weights, norm_gains]).astype(bf)
    small = jnp.pad(small, (0, -small.shape[0] % 1024)).reshape(-1, 1024)
    shard = sets_weights.astype(bf).reshape(-1, width)
    if grid:
        stages, dest, small = gather_all(shard, small, device)
    else:
        small = lax.all_gather(small, "dev", axis=0, tiled=False)
        flat = lax.all_gather(shard, "dev", axis=0, tiled=True)
        parts = lambda v, n: v.reshape(width, n, width).transpose(1, 0, 2).reshape(n * width, width)
        flat = jnp.concatenate(
            [parts(flat[: 3 * width], 3), flat[3 * width : 4 * width], parts(flat[4 * width : 8 * width], 4), flat[8 * width :]]
        )
        stages, dest = ((flat,),), jnp.arange(12 * width // UNIT, dtype=jnp.int32)
    plane = device // 8 if grid else jnp.int32(0)
    runs = [(i * width, i * width, width) for i in range(12)]
    small = small.reshape(devices, -1)
    full_rows = small[:, :n_rows].reshape(-1)
    full_gains = small[:, n_rows : n_rows + n_gains].reshape(-1).astype(f32)
    square = feat * feat
    wq2 = full_rows[: 3 * square].reshape(feat, 3 * feat)
    wo2 = full_rows[3 * square : 4 * square].reshape(feat, feat)
    wu2 = full_rows[4 * square : 8 * square].reshape(feat, 4 * feat)
    wd2 = full_rows[8 * square :].reshape(4 * feat, feat)
    g1, g2 = full_gains[:width], full_gains[width : 2 * width]
    g3, g4 = full_gains[2 * width : 2 * width + feat], full_gains[2 * width + feat :]

    table = lengths.reshape(devices, SETS_DEV)
    own = lax.dynamic_index_in_dim(table, device, 0, keepdims=False)
    positions = jnp.arange(slots, dtype=jnp.int32)
    labels = jnp.sum((positions[:, None] >= running(own)[None, :]).astype(jnp.int32), axis=1)
    counts = jnp.sum(table, axis=1) // devices
    ends = running(counts)
    spot = jnp.arange(rows_pad, dtype=jnp.int32)
    past = (ends[None, :] <= spot[:, None]).astype(jnp.int32)
    start = jnp.sum(past * counts[None, :], axis=1)
    pick = jnp.where(spot < rows_even, jnp.sum(past, axis=1) * per_peer + spot - start, -1)

    flat, joined, a1, o1, a2, u1, slope, h1, leaving = forward_layer(
        per_peer, cells_in, g1, g2, labels, plane.reshape(1), stages, dest
    )

    swap = lambda v: lax.all_to_all(
        v.reshape(devices, -1, LANES), "dev", split_axis=0, concat_axis=0, tiled=True
    ).reshape(slots, width)
    og = jnp.pad(out_grad, ((0, rows_pad - rows_even), (0, 0)))
    rows_out, back, dq2, do2, du2, dd2, dg3, dg4 = rows_layer(
        pick, swap(leaving), og, wq2, wo2, wu2, wd2, g3, g4
    )
    rows_out = rows_out[:rows_even]
    raw = swap(back)

    core = device % 2
    which = core.reshape(1)
    half = width // 2
    pair = lambda v: (v, send(v, CORE))
    if grid:
        raw, *pairs = after(raw, *pair(u1), *pair(a2), *pair(o1), *pair(a1))
        u1, a2, o1, a1 = (tuple(pairs[i : i + 2]) for i in (0, 2, 4, 6))
    *dpre, dh1, low_own, low_peer, gz_own, gz_peer, dg2 = widen_back(runs, per_peer, which, raw, slope, h1, g2, flat)
    *dj, cells_grad, dg1 = attend_back(runs, which, dh1, cells_in, g1, joined, labels, flat)
    if grid:
        chip_runs = sorted_runs(2 * shard.shape[0])[1]
        swapped = lambda own, peer: (own, send(peer, CORE))
        many = u1 + swapped(gz_own, gz_peer) + a2 + swapped(*dpre) + o1 + swapped(low_own, low_peer)
        few = a1 + swapped(*dj)
        blocks = chip_outer(chip_runs, ((8, 4, True), (4, 4, False), (3, 1, True)), many, half)
        blocks = chip_outer(chip_runs, ((0, 3, False),), few, half, tuple(blocks))
        blocks = [v.reshape(16, -1, half // 2) for v in blocks]
        blocks[0], dq2, do2, du2, dd2, dg3, dg4 = after(blocks[0], dq2, do2, du2, dd2, dg3, dg4)
        sums = [sum_blocks(part, device // 2) for part in blocks]
        sets_grad = owned_rows(jnp.concatenate(sums, axis=1), device).reshape(-1)
    else:

        def sides(own, peer, n):
            both = jnp.where(core == 0, jnp.stack([own, peer]), jnp.stack([peer, own]))
            return both.reshape(2, slots, n, half).transpose(1, 2, 0, 3).reshape(slots, -1)

        dq1, du1 = outer(a1, sides(*dj, 3)), outer(a2, sides(*dpre, 4))
        gz = sides(gz_own, gz_peer, 1)
        full = jnp.concatenate([dq1.reshape(-1, width), outer(o1, dh1.astype(bf)), du1.reshape(-1, width), outer(u1, gz)])
        sets_grad = lax.psum_scatter(full.astype(bf), "dev", scatter_dimension=0, tiled=True).astype(f32).reshape(-1)

    rows_flat = jnp.concatenate([v.reshape(-1) for v in (*rows_order(dq2, do2), du2, dd2)])
    dg3, dg4 = jnp.sum(dg3, axis=1), jnp.sum(dg4, axis=1)
    gains = jnp.concatenate([dg1[0], dg2[0], dg3, dg4]).reshape(devices, n_gains)
    extra = jnp.concatenate([rows_flat.reshape(devices, n_rows), gains], axis=1).reshape(devices, 1, -1)
    extra = jnp.sum(lax.all_to_all(extra, "dev", split_axis=0, concat_axis=0, tiled=True), axis=(0, 1))
    rows_grad, gains_grad = extra[:n_rows], extra[n_rows:]

    set_index = device * sets_grad.shape[0] + jnp.arange(sets_grad.shape[0], dtype=jnp.int32)
    row_index = device * n_rows + jnp.arange(n_rows, dtype=jnp.int32)
    set_rates = block_rates(set_index, width, max(1, 3 * width // slots))
    row_rates = block_rates(row_index, feat, max(1, feat // 8))
    sets_new, sets_first_new, sets_second_new = adam_update(
        sets_weights, sets_grad, sets_first, sets_second, set_rates, decay_rate
    )
    rows_new, rows_first_new, rows_second_new = adam_update(
        rows_weights, rows_grad, rows_first, rows_second, row_rates, decay_rate
    )
    gains_new, gains_first_new, gains_second_new = adam_update(
        norm_gains, gains_grad, gains_first, gains_second, gain_rate, 0.0
    )
    return (
        rows_out, cells_grad, sets_grad, rows_grad, gains_grad, sets_new, rows_new, gains_new,
        sets_first_new, rows_first_new, gains_first_new, sets_second_new, rows_second_new, gains_second_new,
        sets_new.astype(bf), rows_new.astype(bf), gains_new.astype(bf),
    )


def solution(mesh):
    flat = P("dev")
    tall = P("dev", None)
    return jax.shard_map(
        local,
        mesh=mesh,
        in_specs=(tall, P()) + (flat,) * 9 + (tall,),
        out_specs=(tall, tall) + (flat,) * 15,
        check_vma=False,
    )
```

```python
import functools

import jax
import jax.numpy as jnp
import numpy as np
from jax import lax
from jax.experimental import pallas as pl
from jax.experimental.pallas import tpu as pltpu
from jax.sharding import PartitionSpec as P

ATTRS = 16
HEADS = 8
SETS_DEV = 2
STEP = 5
LANES = 128

norm_eps = 1e-05
beta_one = 0.5
beta_two = 0.5
adam_eps = 1e-08
decay_rate = 0.1
gain_rate = 0.5


BLOCK = 2


def mm(left, right, dims):
    return lax.dot_general(left, right, (dims, ((), ())), preferred_element_type=jnp.float32)


def gelu_pair(v):
    size = jnp.abs(v) * 0.7071067811865476
    t = 1.0 / (1.0 + 0.3275911 * size)
    bell = jnp.exp(-0.5 * v * v)
    poly = t * (0.254829592 + t * (-0.284496736 + t * (1.421413741 + t * (-1.453152027 + t * 1.061405429))))
    tail = 0.5 * poly * bell
    phi = jnp.where(v < 0.0, tail, 1.0 - tail)
    return v * phi, phi + v * (bell * 0.3989422804014327)


def rows_kernel(
    pick_ref, arrived_ref, og_ref, wq_ref, wqt_ref, wo_ref, wot_ref, wu_ref, wut_ref, wd_ref, wdt_ref, g3_ref, g4_ref,
    out_ref, back_ref, dwq_ref, dwo_ref, dwu_ref, dwd_ref, dg3_ref, dg4_ref,
    joined, prob, dscore, outs, douts, dj, back_acc,
):
    f32, bf = jnp.float32, jnp.bfloat16
    step = pl.program_id(0)
    last = pl.num_programs(0) - 1
    slots = arrived_ref.shape[0]
    scaling = HEADS ** (-0.5)
    feat = 64

    @pl.when(step == 0)
    def _():
        for ref in (dwq_ref, dwo_ref, dwu_ref, dwd_ref, dg3_ref, dg4_ref, back_acc):
            ref[...] = jnp.zeros_like(ref)

    source = lax.broadcasted_iota(jnp.int32, (slots, LANES), 0)
    hot = (source == pick_ref[0]).astype(f32).astype(bf)
    x_t = mm(arrived_ref[...], hot, ((0,), (0,)))

    def to_lanes(tall):
        return jnp.concatenate([tall[a * feat : (a + 1) * feat] for a in range(ATTRS)], axis=1)

    def to_tall(wide):
        return jnp.concatenate([wide[:, a * LANES : (a + 1) * LANES] for a in range(ATTRS)], axis=0)

    def norm(v):
        center = v - jnp.mean(v, axis=0, keepdims=True)
        root = lax.rsqrt(jnp.mean(center * center, axis=0, keepdims=True) + norm_eps)
        return center * root, root

    def norm_back(hat, root, gain, upstream):
        dhat = upstream * gain
        return root * (
            dhat - jnp.mean(dhat, axis=0, keepdims=True) - hat * jnp.mean(dhat * hat, axis=0, keepdims=True)
        )

    def fold(v):
        total = v[:, :LANES]
        for a in range(1, ATTRS):
            total = total + v[:, a * LANES : (a + 1) * LANES]
        return total

    x = to_lanes(x_t)
    g3, g4 = g3_ref[...], g4_ref[...]
    hat3, root3 = norm(x)
    a3 = (hat3 * g3).astype(bf)
    j_t = mm(wqt_ref[...], a3, ((1,), (0,))).astype(bf).astype(f32)
    for a in range(ATTRS):
        joined[a] = j_t[:, a * LANES : (a + 1) * LANES]

    def attend(n, carry):
        group = [n * BLOCK + i for i in range(BLOCK)]
        q = [[joined[a, d * 8 : d * 8 + 8] * scaling for d in range(8)] for a in group]
        scores = [[] for _ in group]
        for b in range(ATTRS):
            k = [joined[b, 64 + d * 8 : 72 + d * 8] for d in range(8)]
            for i in range(BLOCK):
                scores[i].append(functools.reduce(jnp.add, [q[i][d] * k[d] for d in range(8)]))
        inverse = []
        for i in range(BLOCK):
            peak = functools.reduce(jnp.maximum, scores[i])
            scores[i] = [jnp.exp(s - peak) for s in scores[i]]
            inverse.append(1.0 / functools.reduce(jnp.add, scores[i]))
        o = [[None] * 8 for _ in group]
        for b in range(ATTRS):
            v = [joined[b, 128 + d * 8 : 136 + d * 8] for d in range(8)]
            for i, a in enumerate(group):
                p = scores[i][b] * inverse[i]
                prob[a, b] = p
                p = p.astype(bf).astype(f32)
                for d in range(8):
                    o[i][d] = p * v[d] if b == 0 else o[i][d] + p * v[d]
        for i, a in enumerate(group):
            for d in range(8):
                outs[a, d * 8 : d * 8 + 8] = o[i][d]
        return carry

    lax.fori_loop(0, ATTRS // BLOCK, attend, 0, unroll=2)
    o = jnp.concatenate([outs[a] for a in range(ATTRS)], axis=1).astype(bf)
    h3 = x + mm(wot_ref[...], o, ((1,), (0,)))
    hat4, root4 = norm(h3)
    a4 = (hat4 * g4).astype(bf)
    pre = mm(wut_ref[...], a4, ((1,), (0,)))
    active, slope = gelu_pair(pre)
    u = active.astype(bf)
    y = h3 + mm(wdt_ref[...], u, ((1,), (0,)))
    out_ref[...] = to_tall(y).T.astype(bf)

    grad = to_lanes(og_ref[...].astype(f32).T)
    gz = grad.astype(bf)
    dwd_ref[...] += mm(u, gz, ((1,), (1,)))
    dpre = (slope * mm(wd_ref[...], gz, ((1,), (0,)))).astype(bf)
    dwu_ref[...] += mm(a4, dpre, ((1,), (1,)))
    da4 = mm(wu_ref[...], dpre, ((1,), (0,)))
    dg4_ref[...] += fold(da4 * hat4)
    dh3 = grad + norm_back(hat4, root4, g4, da4)

    gz = dh3.astype(bf)
    dwo_ref[...] += mm(o, gz, ((1,), (1,)))
    do = mm(wo_ref[...], gz, ((1,), (0,))).astype(bf).astype(f32)
    for a in range(ATTRS):
        douts[a] = do[:, a * LANES : (a + 1) * LANES]

    def spread(n, carry):
        group = [n * BLOCK + i for i in range(BLOCK)]
        up = [[douts[a, d * 8 : d * 8 + 8] for d in range(8)] for a in group]
        dot, slopes = [None] * BLOCK, [[] for _ in group]
        for b in range(ATTRS):
            v = [joined[b, 128 + d * 8 : 136 + d * 8] for d in range(8)]
            for i, a in enumerate(group):
                s = functools.reduce(jnp.add, [up[i][d] * v[d] for d in range(8)])
                slopes[i].append(s)
                term = prob[a, b] * s
                dot[i] = term if b == 0 else dot[i] + term
        dq = [[None] * 8 for _ in group]
        for b in range(ATTRS):
            k = [joined[b, 64 + d * 8 : 72 + d * 8] for d in range(8)]
            for i, a in enumerate(group):
                ds = (prob[a, b] * (slopes[i][b] - dot[i])).astype(bf).astype(f32) * scaling
                dscore[a, b] = ds
                for d in range(8):
                    dq[i][d] = ds * k[d] if b == 0 else dq[i][d] + ds * k[d]
        for i, a in enumerate(group):
            for d in range(8):
                dj[a, d * 8 : d * 8 + 8] = dq[i][d]
        return carry

    lax.fori_loop(0, ATTRS // BLOCK, spread, 0, unroll=2)

    def collect(n, carry):
        group = [n * BLOCK + i for i in range(BLOCK)]
        dk, dv = [[None] * 8 for _ in group], [[None] * 8 for _ in group]
        for a in range(ATTRS):
            q = [joined[a, d * 8 : d * 8 + 8] for d in range(8)]
            up = [douts[a, d * 8 : d * 8 + 8] for d in range(8)]
            for i, b in enumerate(group):
                ds = dscore[a, b]
                p = prob[a, b].astype(bf).astype(f32)
                for d in range(8):
                    dk[i][d] = ds * q[d] if a == 0 else dk[i][d] + ds * q[d]
                    dv[i][d] = p * up[d] if a == 0 else dv[i][d] + p * up[d]
        for i, b in enumerate(group):
            for d in range(8):
                dj[b, 64 + d * 8 : 72 + d * 8] = dk[i][d]
                dj[b, 128 + d * 8 : 136 + d * 8] = dv[i][d]
        return carry

    lax.fori_loop(0, ATTRS // BLOCK, collect, 0, unroll=2)
    djl = jnp.concatenate([dj[a] for a in range(ATTRS)], axis=1).astype(bf)
    dwq_ref[...] += mm(a3, djl, ((1,), (1,)))
    da3 = mm(wq_ref[...], djl, ((1,), (0,)))
    dg3_ref[...] += fold(da3 * hat3)
    dhc = to_tall(dh3 + norm_back(hat3, root3, g3, da3)).astype(bf)
    back_acc[...] += mm(hot, dhc, ((1,), (1,)))

    @pl.when(step == last)
    def _():
        back_ref[...] = back_acc[...].astype(bf)


def rows_layer(pick, arrived, og, wq, wo, wu, wd, g3, g4):
    f32, bf = jnp.float32, jnp.bfloat16
    total, width = og.shape
    slots = arrived.shape[0]
    steps = total // LANES
    feat = 64
    wqp = wq.reshape(feat, 3, HEADS, 8).transpose(0, 1, 3, 2).reshape(feat, 3 * feat)
    wop = wo.reshape(HEADS, 8, feat).transpose(1, 0, 2).reshape(feat, feat)
    whole = lambda *shape: pl.BlockSpec(shape, lambda t: (0,) * len(shape))
    outs = pl.pallas_call(
        rows_kernel,
        grid=(steps,),
        in_specs=[
            pl.BlockSpec((1, 1, LANES), lambda t: (t, 0, 0)),
            whole(slots, width),
            pl.BlockSpec((LANES, width), lambda t: (t, 0)),
            whole(feat, 192), whole(192, feat), whole(feat, feat), whole(feat, feat),
            whole(feat, 256), whole(256, feat), whole(256, feat), whole(feat, 256),
            whole(feat, 1), whole(feat, 1),
        ],
        out_specs=[
            pl.BlockSpec((LANES, width), lambda t: (t, 0)),
            whole(slots, width),
            whole(feat, 192), whole(feat, feat), whole(feat, 256), whole(256, feat),
            whole(feat, LANES), whole(feat, LANES),
        ],
        out_shape=[
            jax.ShapeDtypeStruct((total, width), bf),
            jax.ShapeDtypeStruct((slots, width), bf),
            jax.ShapeDtypeStruct((feat, 192), f32),
            jax.ShapeDtypeStruct((feat, feat), f32),
            jax.ShapeDtypeStruct((feat, 256), f32),
            jax.ShapeDtypeStruct((256, feat), f32),
            jax.ShapeDtypeStruct((feat, LANES), f32),
            jax.ShapeDtypeStruct((feat, LANES), f32),
        ],
        scratch_shapes=[
            pltpu.VMEM((ATTRS, 192, LANES), f32),
            pltpu.VMEM((ATTRS, ATTRS, 8, LANES), f32),
            pltpu.VMEM((ATTRS, ATTRS, 8, LANES), f32),
            pltpu.VMEM((ATTRS, 64, LANES), f32),
            pltpu.VMEM((ATTRS, 64, LANES), f32),
            pltpu.VMEM((ATTRS, 192, LANES), f32),
            pltpu.VMEM((slots, width), f32),
        ],
        compiler_params=pltpu.CompilerParams(vmem_limit_bytes=56 * 2**20),
    )(
        pick.reshape(steps, 1, LANES), arrived, og,
        wqp, wqp.T, wop, wop.T, wu, wu.T, wd, wd.T, g3.reshape(feat, 1), g4.reshape(feat, 1),
    )
    return outs


def rows_order(dwqp, dwop):
    feat = dwop.shape[0]
    dwq = dwqp.reshape(feat, 3, 8, HEADS).transpose(0, 1, 3, 2).reshape(feat, 3 * feat)
    return dwq, dwop.reshape(8, HEADS, feat).transpose(1, 0, 2).reshape(feat, feat)


UNIT = 32


def placed(flat):
    if flat < 3072:
        return flat % 3 * 1024 + flat // 3
    if flat < 4096 or flat >= 8192:
        return flat
    return 4096 + flat % 4 * 1024 + (flat - 4096) // 4


def sorted_runs(per):
    orders, runs = [], []
    for first in range(0, 12288, per):
        places = [placed(first + i) for i in range(per)]
        order = sorted(range(per), key=lambda i: places[i])
        orders.append(order)
        for at, i in enumerate(order):
            if at and places[i] == runs[-1][1] + runs[-1][2] and places[i] % 1024:
                runs[-1][2] += 1
            else:
                runs.append([first + at, places[i], 1])
    return np.array(orders, np.int32), sorted((tuple(run) for run in runs), key=lambda run: run[1])


class Copies:
    def __init__(self, sems):
        self.sems, self.used = sems, 0

    def start(self, src, dst):
        copy = pltpu.make_async_copy(src, dst, self.sems.at[self.used])
        copy.start()
        self.used += 1
        return copy

    def rows(self, src, dst, parts=4):
        count = src.shape[0] // parts
        cuts = [pl.ds(i * count, count) for i in range(parts)]
        return [self.start(src.at[cut], dst.at[cut]) for cut in cuts]


def wait(copies):
    for copy in copies:
        copy.wait()


def load_mats(copies, runs, flat_ref, held, first, width):
    groups = [[] for _ in range(held.shape[0] // width)]
    for src, dst, rows in runs:
        i = dst // width - first
        if 0 <= i < len(groups):
            groups[i].append(copies.start(flat_ref.at[pl.ds(src, rows)], held.at[pl.ds(dst - first * width, rows)]))
    return groups


def low_norm(v, gain):
    center = v - jnp.mean(v, axis=1, keepdims=True)
    root = lax.rsqrt(jnp.mean(center * center, axis=1, keepdims=True) + norm_eps)
    return (center * root * gain).astype(jnp.bfloat16)


def pull_norm(v, gain, upstream):
    center = v - jnp.mean(v, axis=1, keepdims=True)
    root = lax.rsqrt(jnp.mean(center * center, axis=1, keepdims=True) + norm_eps)
    hat = center * root
    dhat = upstream * gain
    inner = jnp.mean(dhat * hat, axis=1, keepdims=True)
    grad = root * (dhat - jnp.mean(dhat, axis=1, keepdims=True) - hat * inner)
    return grad, jnp.sum(upstream * hat, axis=0, keepdims=True)


def forward_kernel(counts, turn, plane_ref, dest_ref, g1_ref, g2_ref, tall_ref, wide_ref, h0_ref, *refs):
    stages = []
    for count in counts:
        stages.append(refs[:count])
        refs = refs[count:]
    forward_body(turn, plane_ref, dest_ref, g1_ref, g2_ref, tall_ref, wide_ref, h0_ref, stages, *refs)


def forward_body(turn, plane_ref, dest_ref, g1_ref, g2_ref, tall_ref, wide_ref, h0_ref, stages,
                   big_out, joined_out, a1_out, o1_out, a2_out, u1_out, slope_out, h1_out, leave_out,
                   mats, bias, h0, joined, a1, o1, a2, u1, slope, h1, leave, load_sems, plane_sems, store_sems):
    f32, bf = jnp.float32, jnp.bfloat16
    slots, width = h0.shape
    head = width // HEADS
    tile = 512
    loads, stores = Copies(load_sems), Copies(store_sems)
    first = loads.rows(h0_ref, h0)
    part = mats.shape[0] // len(stages)

    def load_stage(s, plane):
        number = sum(piece.shape[0] for pieces in stages[:s] for piece in pieces) // UNIT
        for piece in stages[s]:
            for u in range(piece.shape[0] // UNIT):
                place = pl.multiple_of(dest_ref[number] * UNIT, UNIT)
                number += 1
                pltpu.make_async_copy(
                    piece.at[pl.ds(u * UNIT, UNIT)], mats.at[pl.ds(place, UNIT)], plane_sems.at[plane]
                ).start()

    for plane in range(len(stages)):
        for s in range(len(stages)):
            pl.when(plane_ref[0] ^ s == plane)(functools.partial(load_stage, s, plane))

    def arrived(plane):
        rows = mats.at[pl.ds(plane * part, part)]
        pltpu.make_async_copy(rows, rows, plane_sems.at[plane]).wait()

    saves = []
    bias[...] = jnp.where(tall_ref[...] == wide_ref[...], 0.0, -jnp.inf)
    wait(first)
    a1[...] = low_norm(h0[...].astype(f32), g1_ref[...])
    saves += stores.rows(a1, a1_out)
    for plane in range(len(stages) if len(stages) < 4 else 1):
        arrived(plane)
    for i in range(3):
        for t in range(width // tile):
            cols = slice(i * width + t * tile, i * width + (t + 1) * tile)
            joined[:, cols] = mm(a1[...], mats[i * width : (i + 1) * width, t * tile : (t + 1) * tile], ((1,), (0,))).astype(bf)
    saves += stores.rows(joined, joined_out)
    saves += stores.rows(mats.at[pl.ds(0, 3 * width)], big_out.at[pl.ds(0, 3 * width)], 3)

    def attend(h, carry):
        part = lambda i: joined[:, pl.ds(pl.multiple_of(i * width + h * head, head), head)]
        scores = mm(part(0), part(1), ((1,), (1,))) * head ** (-0.5) + bias[...]
        weights = jnp.exp(scores - jnp.max(scores, axis=1, keepdims=True))
        chance = weights * (1.0 / jnp.sum(weights, axis=1, keepdims=True))
        o1[:, pl.ds(pl.multiple_of(h * head, head), head)] = mm(chance.astype(bf), part(2), ((1,), (0,))).astype(bf)
        return carry

    lax.fori_loop(0, HEADS, attend, 0, unroll=2)
    saves += stores.rows(o1, o1_out)
    if len(stages) == 4:
        arrived(1)
    for t in range(width // tile):
        cols = slice(t * tile, (t + 1) * tile)
        h1[:, cols] = h0[:, cols].astype(f32) + mm(o1[...], mats[3 * width : 4 * width, cols], ((1,), (0,)))
    saves += stores.rows(h1, h1_out)
    a2[...] = low_norm(h1[...], g2_ref[...])
    saves += stores.rows(a2, a2_out)
    if len(stages) == 4:
        arrived(2)
    for i in range(4):
        for t in range(width // tile):
            cols = slice(t * tile, (t + 1) * tile)
            active, rise = gelu_pair(mm(a2[...], mats[(4 + i) * width : (5 + i) * width, cols], ((1,), (0,))))
            cols = slice(i * width + t * tile, i * width + (t + 1) * tile)
            u1[:, cols] = active.astype(bf)
            slope[:, cols] = rise.astype(bf)
            saves.append(stores.start(u1.at[:, cols], u1_out.at[:, cols]))
            saves.append(stores.start(slope.at[:, cols], slope_out.at[:, cols]))
    if len(stages) == 4:
        arrived(3)
    saves += stores.rows(mats.at[pl.ds(3 * width, 9 * width)], big_out.at[pl.ds(3 * width, 9 * width)], 9)
    to, source = (lax.broadcasted_iota(jnp.int32, (slots, slots), axis) for axis in (0, 1))
    hot = (source == to % turn * (slots // turn) + to // turn).astype(f32).astype(bf)
    for t in range(width // tile):
        cols = slice(t * tile, (t + 1) * tile)
        h2 = (h1[:, cols] + mm(u1[...], mats[8 * width :, cols], ((1,), (0,)))).astype(bf)
        leave[:, cols] = mm(hot, h2, ((1,), (0,))).astype(bf)
        saves.append(stores.start(leave.at[:, cols], leave_out.at[:, cols]))
    wait(saves)


def own_kernel(kernel, operands, small, outs, scratch, limit, flops):
    def spec(v):
        space = pltpu.SMEM if v.ndim == 1 else pltpu.VMEM
        return pl.BlockSpec(memory_space=space)

    anywhere = pl.BlockSpec(memory_space=pl.ANY)
    tiny = pl.BlockSpec(memory_space=pltpu.VMEM)
    return pl.pallas_call(
        kernel,
        in_specs=[spec(v) if n in small else anywhere for n, v in enumerate(operands)],
        out_specs=[tiny if out.shape[0] == 1 else anywhere for out in outs],
        out_shape=outs,
        scratch_shapes=scratch,
        compiler_params=pltpu.CompilerParams(vmem_limit_bytes=limit * 2**20),
        cost_estimate=pl.CostEstimate(flops=flops, bytes_accessed=40 * 2**20, transcendentals=10**6),
    )(*operands)


def forward_layer(turn, h0, g1, g2, labels, plane, stages, dest):
    f32, bf = jnp.float32, jnp.bfloat16
    slots, width = h0.shape
    shape, vmem = jax.ShapeDtypeStruct, pltpu.VMEM
    sizes = [(3, bf), (1, bf), (1, bf), (1, bf), (4, bf), (4, bf), (1, f32), (1, bf)]
    mats = (12 * width, width)
    return own_kernel(
        functools.partial(forward_kernel, tuple(len(pieces) for pieces in stages), turn),
        (plane, dest, g1.reshape(1, -1), g2.reshape(1, -1), labels.reshape(-1, 1), labels.reshape(1, -1), h0, *sum(stages, ())),
        (0, 1, 2, 3, 4, 5),
        [shape(mats, bf)] + [shape((slots, n * width), kind) for n, kind in sizes],
        [vmem(mats, bf), vmem((slots, slots), f32), vmem((slots, width), bf)]
        + [vmem((slots, n * width), kind) for n, kind in sizes]
        + [pltpu.SemaphoreType.DMA((4,)), pltpu.SemaphoreType.DMA((len(stages),)), pltpu.SemaphoreType.DMA((50,))],
        60,
        10**10,
    )


def widen_back_kernel(runs, turn, core_ref, g2_ref, raw_ref, slope_ref, h1_ref, flat_ref,
                      dpre_own, dpre_peer, dh_out, low_own, low_peer, gz_own, gz_peer, dg_ref,
                      ups, downs, raw, gz, slope, h1, dpre, dh, low, gz_sides, da, load_sems, store_sems):
    f32, bf = jnp.float32, jnp.bfloat16
    width = gz.shape[1]
    half = width // 2
    core = core_ref[0]
    loads, stores = Copies(load_sems), Copies(store_sems)
    raw_copies = loads.rows(raw_ref, raw)
    down_copies, slope_copies, up_copies = [], [], []
    for i in range(4):
        part, cols = pl.ds(i * width, width), pl.ds(i * width, width)
        down_copies += load_mats(loads, runs, flat_ref, downs.at[part], 8 + i, width)
        slope_copies.append(loads.start(slope_ref.at[:, cols], slope.at[:, cols]))
        up_copies += load_mats(loads, runs, flat_ref, ups.at[part], 4 + i, width)
    h1_copies = loads.rows(h1_ref, h1)
    wait(raw_copies)
    slots = gz.shape[0]
    slot, source = (lax.broadcasted_iota(jnp.int32, (slots, slots), axis) for axis in (0, 1))
    devices = slots // turn
    hot = (source == slot % devices * turn + slot // devices).astype(f32).astype(bf)
    gz[...] = mm(hot, raw[...], ((1,), (0,))).astype(bf)
    saves = []
    for s in range(2):
        gz_sides[s ^ core] = gz[:, s * half : (s + 1) * half]
    saves += [stores.start(gz_sides.at[0], gz_own), stores.start(gz_sides.at[1], gz_peer)]
    for i in range(4):
        wait(down_copies[i] + [slope_copies[i]] + up_copies[i])
        for s in range(2):
            hidden = slice(i * width + s * half, i * width + (s + 1) * half)
            du = mm(gz[...], downs[hidden], ((1,), (1,)))
            piece = (slope[:, hidden].astype(f32) * du).astype(bf)
            dpre[s ^ core, :, i * half : (i + 1) * half] = piece
            term = mm(piece, ups[i * width : (i + 1) * width, s * half : (s + 1) * half], ((1,), (1,)))
            da[...] = term if i == s == 0 else da[...] + term
        lanes = pl.ds(i * half, half)
        saves += [stores.start(dpre.at[0, :, lanes], dpre_own.at[:, lanes]), stores.start(dpre.at[1, :, lanes], dpre_peer.at[:, lanes])]
    wait(h1_copies)
    grad, dg_ref[...] = pull_norm(h1[...], g2_ref[...], da[...])
    dh[...] = gz[...].astype(f32) + grad
    saves += stores.rows(dh, dh_out)
    for s in range(2):
        low[s ^ core] = dh[:, s * half : (s + 1) * half].astype(bf)
    saves += [stores.start(low.at[0], low_own), stores.start(low.at[1], low_peer)]
    wait(saves)


def widen_back(runs, turn, core, raw, slope, h1, g2, flat):
    f32, bf = jnp.float32, jnp.bfloat16
    slots, width = raw.shape
    half = width // 2
    shape, vmem = jax.ShapeDtypeStruct, pltpu.VMEM
    side = shape((slots, half), bf)
    ups = sum(4 <= dst // width < 12 for _, dst, _ in runs)
    return own_kernel(
        functools.partial(widen_back_kernel, runs, turn),
        (core, g2.reshape(1, -1), raw, slope, h1, flat),
        (0, 1),
        [shape((slots, 2 * width), bf)] * 2 + [shape((slots, width), f32)] + [side] * 4 + [shape((1, width), f32)],
        [
            vmem((4 * width, width), bf), vmem((4 * width, width), bf), vmem((slots, width), bf), vmem((slots, width), bf),
            vmem((slots, 4 * width), bf),
            vmem((slots, width), f32), vmem((2, slots, 2 * width), bf), vmem((slots, width), f32), vmem((2, slots, half), bf),
            vmem((2, slots, half), bf), vmem((slots, width), f32),
            pltpu.SemaphoreType.DMA((ups + 12,)), pltpu.SemaphoreType.DMA((16,)),
        ],
        60,
        64 * 10**8,
    )


def attend_back_kernel(runs, core_ref, g1_ref, tall_ref, wide_ref, dh_ref, h0_ref, joined_ref, flat_ref,
                       own_out, peer_out, grad_out, dg_ref,
                       mats, bias, dh, h0, joined, dblend, dj, sides, load_sems, store_sems):
    f32, bf = jnp.float32, jnp.bfloat16
    slots, width = dh.shape
    head = width // HEADS
    half = width // 2
    tile = 512
    scaling = head ** (-0.5)
    core = core_ref[0]
    loads, stores = Copies(load_sems), Copies(store_sems)
    dh_copies = loads.rows(dh_ref, dh)
    out_copies = load_mats(loads, runs, flat_ref, mats.at[pl.ds(3 * width, width)], 3, width)
    joined_copies = loads.rows(joined_ref, joined)
    mat_copies = load_mats(loads, runs, flat_ref, mats.at[pl.ds(0, 3 * width)], 0, width)
    h0_copies = loads.rows(h0_ref, h0)
    bias[...] = jnp.where(tall_ref[...] == wide_ref[...], 0.0, -jnp.inf)
    wait(dh_copies)
    gz = dh[...].astype(bf)
    wait(out_copies[0])
    for t in range(width // tile):
        rows = slice(3 * width + t * tile, 3 * width + (t + 1) * tile)
        dblend[:, t * tile : (t + 1) * tile] = mm(gz, mats[rows], ((1,), (1,))).astype(bf)
    wait(joined_copies)

    def attend(h, carry):
        lanes = lambda i: pl.ds(pl.multiple_of(i * width + h * head, head), head)
        q, k, v = (joined[:, lanes(i)] for i in range(3))
        do = dblend[:, pl.ds(pl.multiple_of(h * head, head), head)]
        scores = mm(q, k, ((1,), (1,))) * scaling + bias[...]
        weights = jnp.exp(scores - jnp.max(scores, axis=1, keepdims=True))
        chance = weights * (1.0 / jnp.sum(weights, axis=1, keepdims=True))
        dchance = mm(do, v, ((1,), (1,)))
        dot = jnp.sum(chance * dchance, axis=1, keepdims=True)
        ds = (chance * (dchance - dot)).astype(bf)
        parts = (
            mm(ds, k, ((1,), (0,))) * scaling,
            mm(ds, q, ((0,), (0,))) * scaling,
            mm(chance.astype(bf), do, ((0,), (0,))),
        )
        per_side = HEADS // 2
        for i in range(3):
            part = parts[i].astype(bf)
            dj[:, lanes(i)] = part
            sides[(h // per_side) ^ core, :, pl.ds(pl.multiple_of(i * half + h % per_side * head, head), head)] = part
        return carry

    lax.fori_loop(0, HEADS, attend, 0, unroll=2)
    saves = [stores.start(sides.at[1], peer_out), stores.start(sides.at[0], own_out)]
    da = None
    for i in range(3):
        wait(mat_copies[i])
        term = mm(dj[:, i * width : (i + 1) * width], mats[i * width : (i + 1) * width], ((1,), (1,)))
        da = term if da is None else da + term
    wait(h0_copies)
    grad, dg_ref[...] = pull_norm(h0[...].astype(f32), g1_ref[...], da)
    dh[...] = dh[...] + grad
    wait(saves + stores.rows(dh, grad_out))


def attend_back(runs, core, dh, h0, g1, joined, labels, flat):
    f32, bf = jnp.float32, jnp.bfloat16
    slots, width = dh.shape
    shape, vmem = jax.ShapeDtypeStruct, pltpu.VMEM
    mats = sum(dst // width < 4 for _, dst, _ in runs)
    return own_kernel(
        functools.partial(attend_back_kernel, runs),
        (core, g1.reshape(1, -1), labels.reshape(-1, 1), labels.reshape(1, -1), dh, h0, joined, flat),
        (0, 1, 2, 3),
        [shape((slots, 3 * width // 2), bf)] * 2 + [shape((slots, width), f32), shape((1, width), f32)],
        [
            vmem((4 * width, width), bf), vmem((slots, slots), f32), vmem((slots, width), f32), vmem((slots, width), bf),
            vmem((slots, 3 * width), bf), vmem((slots, width), bf), vmem((slots, 3 * width), bf),
            vmem((2, slots, 3 * width // 2), bf),
            pltpu.SemaphoreType.DMA((mats + 12,)), pltpu.SemaphoreType.DMA((6,)),
        ],
        60,
        64 * 10**8,
    )


def chip_outer_kernel(runs, jobs, *refs):
    bf = jnp.bfloat16
    count = 4 * len(jobs)
    operands, refs = refs[:count], refs[-(count + 5) :]
    outs, held, (result, load_sems, store_sems) = refs[:2], refs[2 : count + 2], refs[count + 2 :]
    loads, stores = Copies(load_sems), Copies(store_sems)
    arrivals = [loads.rows(ref, v, 2) for ref, v in zip(operands, held, strict=True)]
    width, half = 1024, result.shape[1]
    tile = 512
    saves, done = [], 0
    for n, (first, matrices, tall) in enumerate(jobs):
        left, left_peer, right, right_peer = held[4 * n : 4 * n + 4]
        for copies in arrivals[4 * n : 4 * n + 4]:
            wait(copies)
        for i in range(matrices):
            lanes = slice(0, half) if tall else slice(i * half, (i + 1) * half)
            for t in range(width // tile):
                cols = (i if tall else 0) * width + t * tile
                cols = slice(cols, cols + tile)
                term = mm(left[:, cols], right[:, lanes], ((0,), (0,))) + mm(left_peer[:, cols], right_peer[:, lanes], ((0,), (0,)))
                result[done * width + t * tile : done * width + (t + 1) * tile, :] = term.astype(bf)
            for to, place, rows in runs:
                if place // width == first + i:
                    for side, out in enumerate(outs):
                        part = result.at[pl.ds(done * width + place % width, rows), pl.ds(side * half // 2, half // 2)]
                        saves.append(stores.start(part, out.at[pl.ds(to, rows)]))
            done += 1
    wait(saves)


def chip_outer(runs, jobs, operands, half, onto=()):
    bf = jnp.bfloat16
    anywhere = pl.BlockSpec(memory_space=pl.ANY)
    matrices = [first + i for first, n, _ in jobs for i in range(n)]
    saves = 2 * sum(place // 1024 in matrices for _, place, _ in runs)
    return pl.pallas_call(
        functools.partial(chip_outer_kernel, runs, jobs),
        in_specs=[anywhere] * (len(operands) + len(onto)),
        out_specs=[anywhere] * 2,
        out_shape=[jax.ShapeDtypeStruct((12288, half // 2), bf)] * 2,
        input_output_aliases={len(operands) + i: i for i in range(len(onto))},
        scratch_shapes=[pltpu.VMEM(v.shape, bf) for v in operands]
        + [
            pltpu.VMEM((len(matrices) * 1024, half), bf),
            pltpu.SemaphoreType.DMA((2 * len(operands),)),
            pltpu.SemaphoreType.DMA((saves,)),
        ],
        compiler_params=pltpu.CompilerParams(vmem_limit_bytes=60 * 2**20),
        cost_estimate=pl.CostEstimate(
            flops=len(matrices) * 8 * 10**8, bytes_accessed=len(matrices) * 3 * 2**20, transcendentals=0
        ),
    )(*operands, *onto)


CORE = 1


def send(v, bit):
    return lax.ppermute(v, "dev", [(d, d ^ bit) for d in range(32)])


def after(*values):
    return lax.optimization_barrier(values)


def sum_blocks(blocks, chip):
    f32, bf = jnp.float32, jnp.bfloat16
    half = blocks.shape[1] // 2
    block = lambda m: lax.dynamic_index_in_dim(blocks, chip ^ (m >> 1), 0, keepdims=False)
    total = lambda *parts: sum(part.astype(f32) for part in parts)
    both = lambda one, two: jnp.concatenate([one.astype(bf), two.astype(bf)])

    across_far, up_far, across = block(30), block(14), block(24)
    a, b, c, d, e = after(
        send(across_far[:half], 4), send(across_far[half:], 2), send(across, 8), send(up_far[:half], 4), send(up_far[half:], 2)
    )
    side, other = block(26), block(28)
    across_x, across_y = both(total(side[:half], a), side[half:]), both(other[:half], total(other[half:], b))
    side, other = block(10), block(12)
    up_x, up_y = both(total(side[:half], d), side[half:]), both(other[:half], total(other[half:], e))
    over = total(block(16), c)

    a, b, c = after(send(across_x, 8), send(up_x, 2), send(up_y, 4))
    over_x, up = total(block(18), a), total(block(8), b, c).astype(bf)
    over_far, own_far = block(22), block(6)
    a, b, c, d, e = after(
        send(across_y, 8), send(over_far[:half], 4), send(over_far[half:], 2), send(own_far[:half], 4), send(own_far[half:], 2)
    )
    other = total(block(20), a)
    over_x, over_y = both(total(over_x[:half], b), over_x[half:]), both(other[:half], total(other[half:], c))
    side, other = block(2), block(4)
    own_x, own_y = both(total(side[:half], d), side[half:]), both(other[:half], total(other[half:], e))

    a, b, c = after(send(over_x, 2), send(over_y, 4), send(up, 8))
    own = total(block(0), c)
    over = total(over, a, b).astype(bf)
    return total(own, send(over, 16), send(own_x, 2), send(own_y, 4))


def owned_rows(own, device):
    core, chip = device % 2, device // 2
    half = own.shape[0] // 2
    orders, _ = sorted_runs(2 * half)
    order = lax.dynamic_index_in_dim(jnp.asarray(np.argsort(orders, axis=1).astype(np.int32)), chip, 0, keepdims=False)
    own = jnp.take(own, order, axis=0)
    mine = lax.dynamic_slice_in_dim(own, core * half, half, 0)
    peer = send(lax.dynamic_slice_in_dim(own, (1 - core) * half, half, 0), CORE)
    return jnp.where(core == 0, jnp.concatenate([mine, peer], axis=1), jnp.concatenate([peer, mine], axis=1))


def gather_all(shard, small, device):
    per = shard.shape[0]
    half, extra = per // 2, small.shape[0]
    orders, runs = sorted_runs(per)
    order = lax.dynamic_index_in_dim(jnp.asarray(orders), device, 0, keepdims=False)
    hot = (order[:, None] == jnp.arange(per, dtype=jnp.int32)[None, :]).astype(jnp.bfloat16)
    own = jnp.concatenate([fwd_mul(hot, shard).astype(jnp.bfloat16), small])
    table = np.zeros((32 * per // UNIT,), np.int32)
    for src, dst, rows in runs:
        table[src // UNIT : (src + rows) // UNIT] = range(dst // UNIT, (dst + rows) // UNIT)
    by_mask = jnp.take(jnp.asarray(table.reshape(32, -1)), device ^ jnp.arange(32, dtype=jnp.int32), axis=0)
    stack = lambda *parts: jnp.concatenate([part[:per] for part in parts])

    own, own_x, own_y, up = after(own, send(own, 2), send(own, 4), send(own, 8))
    a, b, up_x, up_y, over = after(
        send(own_x[:half], 4), send(own_y[half:], 2), send(up, 2), send(up, 4), send(own, 16)
    )
    own_far = jnp.concatenate([a, b])
    own_stack = stack(own, own_x, own_y, own_far)
    a, b, over_x, over_y, across, own_stack = after(
        send(up_x[:half], 4), send(up_y[half:], 2), send(over, 2), send(over, 4), send(over, 8), own_stack
    )
    up_far = jnp.concatenate([a, b])
    up_stack = stack(up, up_x, up_y, up_far)
    over_stack = stack(over, over_x, over_y)
    over_far, across_x, across_y, own_peer, up_peer, over_peer = after(
        send(over_y, 2), send(over_x, 8), send(across, 4), send(own_stack, CORE), send(up_stack, CORE), send(over_stack, CORE)
    )
    a, b, across = after(across_x[:half], across_y[half:], across)
    over_last, across_stack = over_far[:per], stack(across, across_x, across_y)
    a, b, over_last_peer, across_peer = after(
        send(a, 4), send(b, 2), send(over_last, CORE), send(across_stack, CORE)
    )
    plane = (own, own_x, own_y, own_far, up, up_x, up_y, up_far, over, over_x, over_y, over_far, across, across_x, across_y)
    small = jnp.concatenate([v[per:] for v in plane] + [b[per - half :]])
    last = (a, b[: per - half])
    last_peer, small_peer = tuple(send(v, CORE) for v in last), send(small, CORE)
    stages = (
        (own_stack, own_peer), (up_stack, up_peer), (over_stack, over_peer, over_last, over_last_peer), (across_stack, across_peer, *last, *last_peer)
    )
    masks = [z + m + c for z in (0, 8) for c in (0, 1) for m in (0, 2, 4, 6)]
    masks += [z + m for z in (16, 24) for m in (0, 2, 4, 1, 3, 5, 6, 7)]
    dest = jnp.concatenate([by_mask[m] for m in masks])
    small = jnp.stack([small.reshape(16, -1), small_peer.reshape(16, -1)], axis=1).reshape(32, -1)
    number = jnp.arange(32, dtype=jnp.int32)
    hot = (number[None, :] == (number ^ device)[:, None]).astype(jnp.bfloat16)
    return stages, dest, fwd_mul(hot, small).astype(jnp.bfloat16)


def fwd_mul(left, right):
    return mm(left, right, ((1,), (0,)))


def outer(left, right):
    return mm(left, right, ((0,), (0,)))


def running(values):
    number = jnp.arange(values.shape[0], dtype=jnp.int32)
    return jnp.sum(jnp.where(number[None, :] <= number[:, None], values[None, :], 0), axis=1)


def block_rates(position, feature, out_fan):
    cut_one = 3 * feature * feature
    cut_two = cut_one + feature * feature
    cut_three = cut_two + 4 * feature * feature
    fans = (feature, out_fan, feature, 4 * feature)
    rates = [0.5 * fan ** (-0.5) for fan in fans]
    return jnp.where(
        position < cut_one,
        rates[0],
        jnp.where(position < cut_two, rates[1], jnp.where(position < cut_three, rates[2], rates[3])),
    ).astype(jnp.float32)


def adam_update(weight, gradient, first, second, rates, decay):
    first_new = beta_one * first + (1.0 - beta_one) * gradient
    second_new = beta_two * second + (1.0 - beta_two) * gradient * gradient
    corrected = first_new / (1.0 - beta_one**STEP)
    scaled = second_new / (1.0 - beta_two**STEP)
    weight_new = weight - rates * (corrected / (jnp.sqrt(scaled) + adam_eps) + decay * weight)
    return (weight_new, first_new, second_new)


def local(
    cells_in, lengths, sets_weights, rows_weights, norm_gains, sets_first, rows_first, gains_first,
    sets_second, rows_second, gains_second, out_grad,
):
    f32, bf = jnp.float32, jnp.bfloat16
    devices = lax.axis_size("dev")
    device = lax.axis_index("dev")
    slots, width = cells_in.shape
    feat = width // ATTRS
    per_peer = slots // devices
    rows_even = out_grad.shape[0]
    rows_pad = -(-rows_even // LANES) * LANES
    grid = devices == 32 and width == 1024 and slots == 384

    n_rows, n_gains = rows_weights.shape[0], norm_gains.shape[0]
    small = jnp.concatenate([rows_weights, norm_gains]).astype(bf)
    small = jnp.pad(small, (0, -small.shape[0] % 1024)).reshape(-1, 1024)
    shard = sets_weights.astype(bf).reshape(-1, width)
    if grid:
        stages, dest, small = gather_all(shard, small, device)
    else:
        small = lax.all_gather(small, "dev", axis=0, tiled=False)
        flat = lax.all_gather(shard, "dev", axis=0, tiled=True)
        parts = lambda v, n: v.reshape(width, n, width).transpose(1, 0, 2).reshape(n * width, width)
        flat = jnp.concatenate(
            [parts(flat[: 3 * width], 3), flat[3 * width : 4 * width], parts(flat[4 * width : 8 * width], 4), flat[8 * width :]]
        )
        stages, dest = ((flat,),), jnp.arange(12 * width // UNIT, dtype=jnp.int32)
    plane = device // 8 if grid else jnp.int32(0)
    runs = [(i * width, i * width, width) for i in range(12)]
    small = small.reshape(devices, -1)
    full_rows = small[:, :n_rows].reshape(-1)
    full_gains = small[:, n_rows : n_rows + n_gains].reshape(-1).astype(f32)
    square = feat * feat
    wq2 = full_rows[: 3 * square].reshape(feat, 3 * feat)
    wo2 = full_rows[3 * square : 4 * square].reshape(feat, feat)
    wu2 = full_rows[4 * square : 8 * square].reshape(feat, 4 * feat)
    wd2 = full_rows[8 * square :].reshape(4 * feat, feat)
    g1, g2 = full_gains[:width], full_gains[width : 2 * width]
    g3, g4 = full_gains[2 * width : 2 * width + feat], full_gains[2 * width + feat :]

    table = lengths.reshape(devices, SETS_DEV)
    own = lax.dynamic_index_in_dim(table, device, 0, keepdims=False)
    positions = jnp.arange(slots, dtype=jnp.int32)
    labels = jnp.sum((positions[:, None] >= running(own)[None, :]).astype(jnp.int32), axis=1)
    counts = jnp.sum(table, axis=1) // devices
    ends = running(counts)
    spot = jnp.arange(rows_pad, dtype=jnp.int32)
    past = (ends[None, :] <= spot[:, None]).astype(jnp.int32)
    start = jnp.sum(past * counts[None, :], axis=1)
    pick = jnp.where(spot < rows_even, jnp.sum(past, axis=1) * per_peer + spot - start, -1)

    flat, joined, a1, o1, a2, u1, slope, h1, leaving = forward_layer(
        per_peer, cells_in, g1, g2, labels, plane.reshape(1), stages, dest
    )

    swap = lambda v: lax.all_to_all(
        v.reshape(devices, -1, LANES), "dev", split_axis=0, concat_axis=0, tiled=True
    ).reshape(slots, width)
    og = jnp.pad(out_grad, ((0, rows_pad - rows_even), (0, 0)))
    rows_out, back, dq2, do2, du2, dd2, dg3, dg4 = rows_layer(
        pick, swap(leaving), og, wq2, wo2, wu2, wd2, g3, g4
    )
    rows_out = rows_out[:rows_even]
    raw = swap(back)

    core = device % 2
    which = core.reshape(1)
    half = width // 2
    pair = lambda v: (v, send(v, CORE))
    if grid:
        raw, *pairs = after(raw, *pair(u1), *pair(a2), *pair(o1), *pair(a1))
        u1, a2, o1, a1 = (tuple(pairs[i : i + 2]) for i in (0, 2, 4, 6))
    *dpre, dh1, low_own, low_peer, gz_own, gz_peer, dg2 = widen_back(runs, per_peer, which, raw, slope, h1, g2, flat)
    *dj, cells_grad, dg1 = attend_back(runs, which, dh1, cells_in, g1, joined, labels, flat)
    if grid:
        chip_runs = sorted_runs(2 * shard.shape[0])[1]
        swapped = lambda own, peer: (own, send(peer, CORE))
        many = u1 + swapped(gz_own, gz_peer) + a2 + swapped(*dpre) + o1 + swapped(low_own, low_peer)
        few = a1 + swapped(*dj)
        blocks = chip_outer(chip_runs, ((8, 4, True), (4, 4, False), (3, 1, True)), many, half)
        blocks = chip_outer(chip_runs, ((0, 3, False),), few, half, tuple(blocks))
        blocks = [v.reshape(16, -1, half // 2) for v in blocks]
        blocks[0], dq2, do2, du2, dd2, dg3, dg4 = after(blocks[0], dq2, do2, du2, dd2, dg3, dg4)
        sums = [sum_blocks(part, device // 2) for part in blocks]
        sets_grad = owned_rows(jnp.concatenate(sums, axis=1), device).reshape(-1)
    else:

        def sides(own, peer, n):
            both = jnp.where(core == 0, jnp.stack([own, peer]), jnp.stack([peer, own]))
            return both.reshape(2, slots, n, half).transpose(1, 2, 0, 3).reshape(slots, -1)

        dq1, du1 = outer(a1, sides(*dj, 3)), outer(a2, sides(*dpre, 4))
        gz = sides(gz_own, gz_peer, 1)
        full = jnp.concatenate([dq1.reshape(-1, width), outer(o1, dh1.astype(bf)), du1.reshape(-1, width), outer(u1, gz)])
        sets_grad = lax.psum_scatter(full.astype(bf), "dev", scatter_dimension=0, tiled=True).astype(f32).reshape(-1)

    rows_flat = jnp.concatenate([v.reshape(-1) for v in (*rows_order(dq2, do2), du2, dd2)])
    dg3, dg4 = jnp.sum(dg3, axis=1), jnp.sum(dg4, axis=1)
    gains = jnp.concatenate([dg1[0], dg2[0], dg3, dg4]).reshape(devices, n_gains)
    extra = jnp.concatenate([rows_flat.reshape(devices, n_rows), gains], axis=1).reshape(devices, 1, -1)
    extra = jnp.sum(lax.all_to_all(extra, "dev", split_axis=0, concat_axis=0, tiled=True), axis=(0, 1))
    rows_grad, gains_grad = extra[:n_rows], extra[n_rows:]

    set_index = device * sets_grad.shape[0] + jnp.arange(sets_grad.shape[0], dtype=jnp.int32)
    row_index = device * n_rows + jnp.arange(n_rows, dtype=jnp.int32)
    set_rates = block_rates(set_index, width, max(1, 3 * width // slots))
    row_rates = block_rates(row_index, feat, max(1, feat // 8))
    sets_new, sets_first_new, sets_second_new = adam_update(
        sets_weights, sets_grad, sets_first, sets_second, set_rates, decay_rate
    )
    rows_new, rows_first_new, rows_second_new = adam_update(
        rows_weights, rows_grad, rows_first, rows_second, row_rates, decay_rate
    )
    gains_new, gains_first_new, gains_second_new = adam_update(
        norm_gains, gains_grad, gains_first, gains_second, gain_rate, 0.0
    )
    return (
        rows_out, cells_grad, sets_grad, rows_grad, gains_grad, sets_new, rows_new, gains_new,
        sets_first_new, rows_first_new, gains_first_new, sets_second_new, rows_second_new, gains_second_new,
        sets_new.astype(bf), rows_new.astype(bf), gains_new.astype(bf),
    )


def solution(mesh):
    flat = P("dev")
    tall = P("dev", None)
    return jax.shard_map(
        local,
        mesh=mesh,
        in_specs=(tall, P()) + (flat,) * 9 + (tall,),
        out_specs=(tall, tall) + (flat,) * 15,
        check_vma=False,
    )
```
